32 devices in a mesh: sub: 16 (over z, y, x), tm: 2 (over core).
Axes of the slice: x: 2, y: 2, z: 4, core: 2. Of those that a mesh axis runs over, the one named last changes fastest.
Arguments:
- data: bfloat16 [1, 16384, 512], P(None, 'sub', 'tm'), may hold values from -6 to 6
- delays: int32 [16384], P('sub'), may hold values from 0 to 15, as said below
- offsets: int32 [2048, 1024], P('sub'), may hold values from 0 to 96, as said below
- widths: int32 [8], replicated, may hold values from 1 to 128, as said below
Outputs:
- boxcars: float32 [2048, 1, 8, 512], P('sub', None, None, 'tm')
The draws below stay inside these ranges and needn't reach their ends.
Inputs may be any that keep to these rules, and one draw needn't show every extreme that they name: `delays`: some channel has delay 16 - 1. `offsets`: some entry equals 96 and some entry equals 0. `widths`: some entry equals 128.
All inputs are finite; a program needn't handle non-finite values.
Results may differ from the reference program's by a relative error of at most 0.0048.
Values may be sent and summed in bfloat16 or wider, within the bound.
No kernel may reach another device: no remote copies, remote signals or barrier semaphores. Data moves between devices by JAX's collectives and lax.ppermute only.
A program may use at most 64 MiB of HBM per device.

```python
import math
import jax
import jax.numpy as jnp
from jax import lax

NCHAN = 16384
NSUB = 1024
NDM = 2048
NW = 8
WMAX = 128
DCH = 16
OMAX = 96
BEAMS = 1
T_TOTAL = 512


def draw_delays(key, part):
    first, second_operand = jax.random.split(key, 2)
    values = jax.random.randint(first, (NCHAN,), 0, DCH, dtype=jnp.int32)
    target = jax.random.randint(second_operand, (), 0, NCHAN, dtype=jnp.int32)
    return values.at[target].set(DCH - 1)


def draw_offsets(key, part):
    first, second_operand, third, fourth, fifth = jax.random.split(jax.random.fold_in(key, 17), 5)
    dm_codes = jax.random.randint(first, (NDM,), 0, OMAX + 1, dtype=jnp.int32)
    band_codes = jax.random.randint(second_operand, (NSUB,), 0, 1025, dtype=jnp.int32)
    jitter_top = max(2, OMAX // 16)
    jitter = jax.random.randint(third, (NDM, NSUB), 0, jitter_top + 1, dtype=jnp.int32)
    values = dm_codes[:, None] * band_codes[None, :] // 1024 + jitter
    values = jnp.minimum(values, OMAX)
    top_row = jax.random.randint(fourth, (), 0, NDM, dtype=jnp.int32)
    top_col = jax.random.randint(fifth, (), 0, NSUB, dtype=jnp.int32)
    low_row = (top_row + 1) % NDM
    values = values.at[low_row, top_col].set(0)
    values = values.at[top_row, top_col].set(OMAX)
    return values


def draw_widths(key, part):
    first, second_operand = jax.random.split(jax.random.fold_in(key, 29), 2)
    values = jax.random.randint(first, (NW,), 1, WMAX + 1, dtype=jnp.int32)
    target = jax.random.randint(second_operand, (), 0, NW, dtype=jnp.int32)
    return values.at[target].set(WMAX)


def steps_of(stream_key, extent, shards, low, largest):
    gain = 1.0
    for axis_at, parts in shards:
        heights = jax.random.uniform(jax.random.fold_in(jax.random.fold_in(stream_key, 6), axis_at), (parts,), jnp.float32, low / len(shards), largest / len(shards))
        gain = gain * jnp.repeat(jnp.exp(heights), extent[axis_at] // parts).reshape((-1,) + (1,) * (len(extent) - 1 - axis_at))
    return gain


def normal_values(stream_key, dims, deviation, bound, shards=(), held_as=jnp.bfloat16):
    gain = steps_of(stream_key, dims, shards, -0.22, 0.18) if shards else 1.0
    array = jax.random.normal(stream_key, dims, jnp.float32) * deviation * gain
    return jnp.minimum(jnp.maximum(array, -bound), bound).astype(held_as)


def setup_inputs(seed: int = 0) -> dict:
    arg_keys = jax.random.split(jax.random.key(seed), 5)
    return {
        "data": normal_values(arg_keys[0], (BEAMS, NCHAN, T_TOTAL), 1.0, 6.0, ((1, 16), (2, 2))),
        "delays": draw_delays(jax.random.fold_in(arg_keys[4], 71), 0),
        "offsets": draw_offsets(jax.random.fold_in(arg_keys[4], 71), 0),
        "widths": draw_widths(jax.random.fold_in(arg_keys[4], 71), 0),
    }


def reference(data, delays, offsets, widths):
    beams, chans, total = data.shape
    nsub = offsets.shape[1]
    per_sub = chans // nsub
    span = total + OMAX
    padded = jnp.pad(data.astype(jnp.float32), ((0, 0), (0, 0), (0, OMAX + DCH - 1)))
    shifted = jnp.zeros((beams, chans, span), jnp.float32)
    for delay in range(DCH):
        shifted = shifted + jnp.where((delays == delay)[None, :, None], padded[:, :, delay:delay + span], 0.0)
    series = shifted.reshape(beams, nsub, per_sub, span).sum(axis=2).astype(jnp.bfloat16)
    times = jnp.arange(total, dtype=jnp.int32)

    def accumulate(running, inputs):
        series_row, lags = inputs
        picked = series_row[:, times[None, :] + lags[:, None]]
        return (running + picked.astype(jnp.float32), None)
    initial_prefix_sums = jnp.zeros((beams, NDM, total), jnp.float32)
    sums, unused = lax.scan(accumulate, initial_prefix_sums, (jnp.transpose(series, (1, 0, 2)), jnp.transpose(offsets)))
    scale = 1.0 / math.sqrt(chans)
    dedispersed = (sums * scale).astype(jnp.bfloat16)
    cumulative_total = jnp.cumsum(dedispersed.astype(jnp.float32), axis=2)
    cumulative_total = jnp.concatenate([jnp.zeros((beams, NDM, 1), jnp.float32), cumulative_total], axis=2)
    cumulative_total = jnp.pad(cumulative_total, ((0, 0), (0, 0), (0, WMAX - 1)), mode='edge')
    lower = cumulative_total[:, :, :total]
    filtered = []
    for column in range(NW):
        width = widths[column].astype(jnp.int32)
        upper = lax.dynamic_slice_in_dim(cumulative_total, width, total, 2)
        filtered.append((upper - lower) / jnp.sqrt(width.astype(jnp.float32)))
    stacked = jnp.stack(filtered, axis=0)
    return jnp.transpose(stacked, (2, 1, 0, 3))
```

```python
import functools
import math

import jax
import jax.numpy as jnp
from jax import lax
from jax.experimental import pallas as pl
from jax.experimental.pallas import tpu as pltpu
from jax.sharding import PartitionSpec as P

WMAX = 128
DCH = 16
OMAX = 96
LANES = 128
STEP = 16
VMEM = pl.BlockSpec(memory_space=pltpu.VMEM)
SMEM = pl.BlockSpec(memory_space=pltpu.SMEM)


def passed_back(value, axis):
    count = lax.axis_size(axis)
    return lax.ppermute(value, axis, [(source, source - 1) for source in range(1, count)])


def series_kernel(per_sub, key_ref, data_ref, halo_ref, series_ref):
    chans = data_ref.shape[0]
    span = series_ref.shape[1]
    block = min(chans, 256)
    subs = block // per_sub
    rows = lax.broadcasted_iota(jnp.int32, (DCH * subs, block), 0)
    for at in range(chans // block):
        here = pl.ds(at * block, block)
        member = jnp.where(rows == key_ref[:, here], 1.0, 0.0).astype(jnp.bfloat16)
        values = jnp.concatenate([data_ref[here, :], halo_ref[here, :]], axis=1)
        picked = jnp.dot(member, values, preferred_element_type=jnp.float32)
        total = picked[:subs, :]
        for delay in range(1, DCH):
            total = total + pltpu.roll(picked[delay * subs : (delay + 1) * subs, :], span - delay, 1)
        series_ref[pl.ds(at * subs, subs), :] = total.astype(jnp.bfloat16)


def where_equal(table, value):
    wanted = jnp.full((1, table.shape[1]), value, jnp.int32).astype(jnp.float32).astype(jnp.bfloat16)
    return jnp.where(table == wanted, jnp.bfloat16(1), jnp.bfloat16(0))


def dedisperse_kernel(scale, length, series_ref, offsets_ref, out_ref, head_ref, turned, lags, totals):
    nsub, span = series_ref.shape
    trials = offsets_ref.shape[0]
    for at in range(nsub // LANES):
        here = pl.ds(at * LANES, LANES)
        for first in range(0, span, LANES):
            tile = series_ref[here, pl.ds(first, LANES)].astype(jnp.float32)
            turned[pl.ds(first, LANES), here] = tile.T
        lags[here, :] = offsets_ref[:, here].astype(jnp.float32).T.astype(jnp.bfloat16)
    groups = OMAX // STEP
    rows = length + STEP
    totals[...] = jnp.zeros_like(totals)

    def one_lag(lag, carry):
        shifted = turned[pl.ds(0, length + OMAX - STEP), :].astype(jnp.bfloat16)
        for pair in range(groups // 2):
            chosen = [where_equal(lags[...], lag + STEP * (2 * pair + odd)) for odd in range(2)]
            first = 2 * STEP * pair
            totals[pair] += jnp.dot(
                shifted[first : first + rows],
                jnp.concatenate(chosen, axis=1),
                preferred_element_type=jnp.float32,
            )
        turned[pl.ds(0, span - 8), :] = turned[pl.ds(1, span - 8), :]
        return carry

    lax.fori_loop(0, STEP, one_lag, 0)
    last = where_equal(lags[...], OMAX)
    result = jnp.dot(
        turned[pl.ds(OMAX - STEP, length), :].astype(jnp.bfloat16), last, preferred_element_type=jnp.float32
    )
    for pair in range(groups // 2):
        result = result + totals[pair, pl.ds(0, length), pl.ds(0, trials)]
        result = result + totals[pair, pl.ds(STEP, length), pl.ds(trials, trials)]
    done = (result * scale).T.astype(jnp.bfloat16)
    out_ref[...] = done
    head_ref[...] = done[:, :WMAX]


def boxcar_kernel(widths_ref, main_ref, later_ref, out_ref, mixed):
    trials, length = main_ref.shape
    filters = widths_ref.shape[0]
    values = jnp.concatenate([main_ref[...], later_ref[...]], axis=1)
    shape = (length + WMAX, length)
    lag = lax.broadcasted_iota(jnp.int32, shape, 0) - lax.broadcasted_iota(jnp.int32, shape, 1)
    for at in range(filters):
        width = widths_ref[at]
        band = jnp.where((lag >= 0) & (lag < width), 1.0, 0.0).astype(jnp.bfloat16)
        sums = jnp.dot(values, band, preferred_element_type=jnp.float32)
        root = jnp.sqrt(jnp.full((1, length), width, jnp.int32).astype(jnp.float32))
        scaled = sums / root
        for part in range(length // LANES):
            lanes = slice(part * LANES, (part + 1) * LANES)
            mixed[part, pl.ds(at, trials, stride=filters), :] = scaled[:, lanes]
    for part in range(length // LANES):
        out_ref[:, :, pl.ds(part * LANES, LANES)] = mixed[part].reshape(trials, filters, LANES)


def per_device(data, delays, offsets, widths):
    beams, chans, length = data.shape
    trials, nsub = offsets.shape
    filters = widths.shape[0]
    groups = lax.axis_size("sub")
    sub_dev = nsub // groups
    per_sub = chans // sub_dev
    scale = 1.0 / math.sqrt(chans * groups)
    span = length + LANES
    outs = []
    padded = max(trials, LANES)
    lag_table = jnp.pad(offsets, ((0, padded - trials), (0, 0))) if padded > trials else offsets
    block_subs = min(chans, 256) // per_sub
    channel = jnp.arange(chans, dtype=jnp.int32)
    key = (delays * block_subs + (channel // per_sub) % block_subs)[None, :]
    for beam in range(beams):
        own = data[beam]
        halo = passed_back(own, "tm")
        series = pl.pallas_call(
            functools.partial(series_kernel, per_sub),
            out_shape=jax.ShapeDtypeStruct((sub_dev, span), jnp.bfloat16),
            grid=(1,),
            in_specs=[
                pl.BlockSpec((1, chans), lambda i: (0, 0)),
                pl.BlockSpec((chans, length), lambda i: (0, 0)),
                pl.BlockSpec((chans, LANES), lambda i: (0, 0)),
            ],
            out_specs=pl.BlockSpec((sub_dev, span), lambda i: (0, 0)),
            compiler_params=pltpu.CompilerParams(vmem_limit_bytes=32 << 20),
        )(key, own, halo)
        whole = lax.all_gather(series, "sub", axis=0, tiled=True)
        main, head = pl.pallas_call(
            functools.partial(dedisperse_kernel, scale, length),
            out_shape=[
                jax.ShapeDtypeStruct((padded, length), jnp.bfloat16),
                jax.ShapeDtypeStruct((padded, WMAX), jnp.bfloat16),
            ],
            in_specs=[VMEM, VMEM],
            out_specs=[VMEM, VMEM],
            scratch_shapes=[
                pltpu.VMEM((span, nsub), jnp.float32),
                pltpu.VMEM((nsub, padded), jnp.bfloat16),
                pltpu.VMEM((OMAX // STEP // 2, length + STEP, 2 * padded), jnp.float32),
            ],
            compiler_params=pltpu.CompilerParams(vmem_limit_bytes=40 << 20),
        )(whole, lag_table)
        later = passed_back(head, "tm")
        filtered = pl.pallas_call(
            boxcar_kernel,
            out_shape=jax.ShapeDtypeStruct((padded, filters, length), jnp.float32),
            in_specs=[SMEM, VMEM, VMEM],
            out_specs=VMEM,
            scratch_shapes=[pltpu.VMEM((length // LANES, padded * filters, LANES), jnp.float32)],
            compiler_params=pltpu.CompilerParams(vmem_limit_bytes=32 << 20),
        )(widths, main, later)
        outs.append(filtered.reshape(padded, 1, filters, length)[:trials])
    return outs[0] if beams == 1 else jnp.concatenate(outs, axis=1)


def solution(mesh):
    placed = (P(None, "sub", "tm"), P("sub"), P("sub", None), P())
    return jax.shard_map(
        per_device,
        mesh=mesh,
        in_specs=placed,
        out_specs=P("sub", None, None, "tm"),
        check_vma=False,
    )
```

```python
import functools
import math

import jax
import jax.numpy as jnp
from jax import lax
from jax.experimental import pallas as pl
from jax.experimental.pallas import tpu as pltpu
from jax.sharding import PartitionSpec as P

WMAX = 128
DCH = 16
OMAX = 96
LANES = 128
STEP = 16
VMEM = pl.BlockSpec(memory_space=pltpu.VMEM)
SMEM = pl.BlockSpec(memory_space=pltpu.SMEM)


def passed_back(value, axis):
    count = lax.axis_size(axis)
    return lax.ppermute(value, axis, [(source, source - 1) for source in range(1, count)])


def series_kernel(per_sub, key_ref, data_ref, halo_ref, series_ref):
    chans = data_ref.shape[0]
    copies, _, span = series_ref.shape
    block = min(chans, 256)
    subs = block // per_sub
    rows = lax.broadcasted_iota(jnp.int32, (DCH * subs, block), 0)
    for at in range(chans // block):
        here = pl.ds(at * block, block)
        member = jnp.where(rows == key_ref[:, here], 1.0, 0.0).astype(jnp.bfloat16)
        values = jnp.concatenate([data_ref[here, :], halo_ref[here, :]], axis=1)
        picked = jnp.dot(member, values, preferred_element_type=jnp.float32)
        total = picked[:subs, :]
        for delay in range(1, DCH):
            total = total + pltpu.roll(picked[delay * subs : (delay + 1) * subs, :], span - delay, 1)
        rounded = total.astype(jnp.bfloat16)
        for copy in range(copies):
            series_ref[copy, pl.ds(at * subs, subs), :] = rounded


def where_equal(table, value):
    wanted = jnp.full((1, table.shape[1]), value, jnp.int32).astype(jnp.float32).astype(jnp.bfloat16)
    return jnp.where(table == wanted, jnp.bfloat16(1), jnp.bfloat16(0))


def dedisperse_kernel(scale, length, series_ref, offsets_ref, out_ref, head_ref, turned, lags, totals):
    nsub, span = series_ref.shape
    trials = offsets_ref.shape[0]
    for at in range(nsub // LANES):
        here = pl.ds(at * LANES, LANES)
        for first in range(0, span, LANES):
            tile = series_ref[here, pl.ds(first, LANES)].astype(jnp.float32)
            turned[pl.ds(first, LANES), here] = tile.T
        lags[here, :] = offsets_ref[:, here].astype(jnp.float32).T.astype(jnp.bfloat16)
    groups = OMAX // STEP
    rows = length + STEP
    totals[...] = jnp.zeros_like(totals)

    def one_lag(lag, carry):
        shifted = turned[pl.ds(0, length + OMAX - STEP), :].astype(jnp.bfloat16)
        for pair in range(groups // 2):
            chosen = [where_equal(lags[...], lag + STEP * (2 * pair + odd)) for odd in range(2)]
            first = 2 * STEP * pair
            totals[pair] += jnp.dot(
                shifted[first : first + rows],
                jnp.concatenate(chosen, axis=1),
                preferred_element_type=jnp.float32,
            )
        turned[pl.ds(0, span - 8), :] = turned[pl.ds(1, span - 8), :]
        return carry

    lax.fori_loop(0, STEP, one_lag, 0)
    last = where_equal(lags[...], OMAX)
    result = jnp.dot(
        turned[pl.ds(OMAX - STEP, length), :].astype(jnp.bfloat16), last, preferred_element_type=jnp.float32
    )
    for pair in range(groups // 2):
        result = result + totals[pair, pl.ds(0, length), pl.ds(0, trials)]
        result = result + totals[pair, pl.ds(STEP, length), pl.ds(trials, trials)]
    done = (result * scale).T.astype(jnp.bfloat16)
    out_ref[...] = done
    head_ref[...] = done[:, :WMAX]


def boxcar_kernel(widths_ref, main_ref, later_ref, out_ref, mixed):
    trials, length = main_ref.shape
    filters = widths_ref.shape[0]
    values = jnp.concatenate([main_ref[...], later_ref[...]], axis=1)
    shape = (length + WMAX, length)
    lag = lax.broadcasted_iota(jnp.int32, shape, 0) - lax.broadcasted_iota(jnp.int32, shape, 1)
    for at in range(filters):
        width = widths_ref[at]
        band = jnp.where((lag >= 0) & (lag < width), 1.0, 0.0).astype(jnp.bfloat16)
        sums = jnp.dot(values, band, preferred_element_type=jnp.float32)
        root = jnp.sqrt(jnp.full((1, length), width, jnp.int32).astype(jnp.float32))
        scaled = sums / root
        for part in range(length // LANES):
            lanes = slice(part * LANES, (part + 1) * LANES)
            mixed[part, pl.ds(at, trials, stride=filters), :] = scaled[:, lanes]
    for part in range(length // LANES):
        out_ref[:, :, pl.ds(part * LANES, LANES)] = mixed[part].reshape(trials, filters, LANES)


def per_device(data, delays, offsets, widths):
    beams, chans, length = data.shape
    trials, nsub = offsets.shape
    filters = widths.shape[0]
    groups = lax.axis_size("sub")
    sub_dev = nsub // groups
    per_sub = chans // sub_dev
    scale = 1.0 / math.sqrt(chans * groups)
    span = length + LANES
    outs = []
    padded = max(trials, LANES)
    lag_table = jnp.pad(offsets, ((0, padded - trials), (0, 0))) if padded > trials else offsets
    block_subs = min(chans, 256) // per_sub
    channel = jnp.arange(chans, dtype=jnp.int32)
    key = (delays * block_subs + (channel // per_sub) % block_subs)[None, :]
    for beam in range(beams):
        own = data[beam]
        halo = passed_back(own, "tm")
        series = pl.pallas_call(
            functools.partial(series_kernel, per_sub),
            out_shape=jax.ShapeDtypeStruct((groups, sub_dev, span), jnp.bfloat16),
            grid=(1,),
            in_specs=[
                pl.BlockSpec((1, chans), lambda i: (0, 0)),
                pl.BlockSpec((chans, length), lambda i: (0, 0)),
                pl.BlockSpec((chans, LANES), lambda i: (0, 0)),
            ],
            out_specs=pl.BlockSpec((groups, sub_dev, span), lambda i: (0, 0, 0)),
            compiler_params=pltpu.CompilerParams(vmem_limit_bytes=32 << 20),
        )(key, own, halo)
        whole = lax.all_to_all(series, "sub", 0, 0, tiled=True).reshape(nsub, span)
        main, head = pl.pallas_call(
            functools.partial(dedisperse_kernel, scale, length),
            out_shape=[
                jax.ShapeDtypeStruct((padded, length), jnp.bfloat16),
                jax.ShapeDtypeStruct((padded, WMAX), jnp.bfloat16),
            ],
            in_specs=[VMEM, VMEM],
            out_specs=[VMEM, VMEM],
            scratch_shapes=[
                pltpu.VMEM((span, nsub), jnp.float32),
                pltpu.VMEM((nsub, padded), jnp.bfloat16),
                pltpu.VMEM((OMAX // STEP // 2, length + STEP, 2 * padded), jnp.float32),
            ],
            compiler_params=pltpu.CompilerParams(vmem_limit_bytes=40 << 20),
        )(whole, lag_table)
        later = passed_back(head, "tm")
        filtered = pl.pallas_call(
            boxcar_kernel,
            out_shape=jax.ShapeDtypeStruct((padded, filters, length), jnp.float32),
            in_specs=[SMEM, VMEM, VMEM],
            out_specs=VMEM,
            scratch_shapes=[pltpu.VMEM((length // LANES, padded * filters, LANES), jnp.float32)],
            compiler_params=pltpu.CompilerParams(vmem_limit_bytes=32 << 20),
        )(widths, main, later)
        outs.append(filtered.reshape(padded, 1, filters, length)[:trials])
    return outs[0] if beams == 1 else jnp.concatenate(outs, axis=1)


def solution(mesh):
    placed = (P(None, "sub", "tm"), P("sub"), P("sub", None), P())
    return jax.shard_map(
        per_device,
        mesh=mesh,
        in_specs=placed,
        out_specs=P("sub", None, None, "tm"),
        check_vma=False,
    )
```

```python
import functools
import math

import jax
import jax.numpy as jnp
from jax import lax
from jax.experimental import pallas as pl
from jax.experimental.pallas import tpu as pltpu
from jax.sharding import PartitionSpec as P

WMAX = 128
DCH = 16
OMAX = 96
LANES = 128
STEP = 16
TOGETHER = 4
VMEM = pl.BlockSpec(memory_space=pltpu.VMEM)
SMEM = pl.BlockSpec(memory_space=pltpu.SMEM)
LIMIT = pltpu.CompilerParams(vmem_limit_bytes=32 << 20)


def passed_back(value, axis):
    count = lax.axis_size(axis)
    return lax.ppermute(value, axis, [(source, source - 1) for source in range(1, count)])


def exchanged(value, axis, flip):
    count = lax.axis_size(axis)
    return lax.ppermute(value, axis, [(source, source ^ flip) for source in range(count)])


def series_kernel(per_sub, key_ref, data_ref, halo_ref, series_ref):
    chans = data_ref.shape[0]
    span = series_ref.shape[1]
    block = min(chans, 256)
    subs = block // per_sub
    rows = lax.broadcasted_iota(jnp.int32, (DCH * subs, block), 0)
    for at in range(chans // block):
        here = pl.ds(at * block, block)
        member = jnp.where(rows == key_ref[:, here], 1.0, 0.0).astype(jnp.bfloat16)
        values = jnp.concatenate([data_ref[here, :], halo_ref[here, :]], axis=1)
        picked = jnp.dot(member, values, preferred_element_type=jnp.float32)
        total = picked[:subs, :]
        for delay in range(1, DCH):
            total = total + pltpu.roll(picked[delay * subs : (delay + 1) * subs, :], span - delay, 1)
        series_ref[pl.ds(at * subs, subs), :] = total.astype(jnp.bfloat16)


def turn_offsets_kernel(offsets_ref, lags_ref):
    for at in range(offsets_ref.shape[1] // LANES):
        here = pl.ds(at * LANES, LANES)
        lags_ref[here, :] = offsets_ref[:, here].astype(jnp.float32).T.astype(jnp.bfloat16)


def turn_series_kernel(outer, place_ref, *refs):
    blocks, turned_ref, ordered = refs[:outer], refs[outer], refs[outer + 1]
    subs, span = blocks[0].shape
    me = place_ref[0]
    for flip in range(outer):
        start = pl.multiple_of((me ^ flip) * subs, subs)
        ordered[pl.ds(start, subs), :] = blocks[flip][...].astype(jnp.float32)
    rows = turned_ref.shape[0]
    for at in range(outer * subs // LANES):
        here = pl.ds(at * LANES, LANES)
        for first in range(0, rows, LANES):
            count = min(LANES, rows - first)
            tile = ordered[here, pl.ds(first, LANES)].T
            turned_ref[pl.ds(first, count), here] = tile[:count].astype(jnp.bfloat16)


def where_equal(table, value):
    wanted = jnp.full((1, table.shape[1]), value, jnp.int32).astype(jnp.float32).astype(jnp.bfloat16)
    return jnp.where(table == wanted, jnp.bfloat16(1), jnp.bfloat16(0))


def partial_sums(outer, flip, place_ref, turned_ref, lags_ref, moving, lags, totals):
    span, nsub = turned_ref.shape
    length = span - OMAX
    subs = nsub // outer
    trials = lags_ref.shape[1]
    inner = lags_ref.shape[0] // nsub
    column = place_ref[1] ^ flip
    for row in range(outer):
        start = pl.multiple_of((row * inner + column) * subs, subs)
        lags[pl.ds(row * subs, subs), :] = lags_ref[pl.ds(start, subs), :]
    moving[pl.ds(0, span), :] = turned_ref[...].astype(jnp.float32)
    pairs = OMAX // STEP // 2
    rows = length + STEP
    reach = length + OMAX - STEP
    totals[...] = jnp.zeros_like(totals)

    def some_lags(step, carry):
        shifted = jnp.concatenate(
            [moving[pl.ds(at, reach), :].astype(jnp.bfloat16) for at in range(TOGETHER)], axis=1
        )
        for pair in range(pairs):
            chosen = jnp.concatenate(
                [
                    jnp.concatenate(
                        [
                            where_equal(lags[...], step * TOGETHER + at + STEP * (2 * pair + odd))
                            for odd in range(2)
                        ],
                        axis=1,
                    )
                    for at in range(TOGETHER)
                ],
                axis=0,
            )
            first = 2 * STEP * pair
            totals[pair] += jnp.dot(
                shifted[first : first + rows], chosen, preferred_element_type=jnp.float32
            )
        moving[pl.ds(0, span), :] = moving[pl.ds(TOGETHER, span), :]
        return carry

    lax.fori_loop(0, STEP // TOGETHER, some_lags, 0)
    result = jnp.dot(
        moving[pl.ds(OMAX - STEP, length), :].astype(jnp.bfloat16),
        where_equal(lags[...], OMAX),
        preferred_element_type=jnp.float32,
    )
    for pair in range(pairs):
        result = result + totals[pair, pl.ds(0, length), pl.ds(0, trials)]
        result = result + totals[pair, pl.ds(STEP, length), pl.ds(trials, trials)]
    return result


def first_sums_kernel(outer, place_ref, turned_ref, lags_ref, sums_ref, *scratch):
    sums_ref[...] = partial_sums(outer, 0, place_ref, turned_ref, lags_ref, *scratch)


def more_sums_kernel(outer, flip, place_ref, turned_ref, lags_ref, before_ref, sums_ref, *scratch):
    sums_ref[...] = before_ref[...] + partial_sums(outer, flip, place_ref, turned_ref, lags_ref, *scratch)


def last_sums_kernel(
    outer, flip, scale, place_ref, turned_ref, lags_ref, before_ref, out_ref, head_ref, *scratch
):
    sums = before_ref[...] + partial_sums(outer, flip, place_ref, turned_ref, lags_ref, *scratch)
    done = (sums * scale).T.astype(jnp.bfloat16)
    out_ref[...] = done
    head_ref[...] = done[:, :WMAX]


def boxcar_kernel(widths_ref, main_ref, later_ref, out_ref, mixed):
    trials, length = main_ref.shape
    filters = widths_ref.shape[0]
    values = jnp.concatenate([main_ref[...], later_ref[...]], axis=1)
    shape = (length + WMAX, length)
    lag = lax.broadcasted_iota(jnp.int32, shape, 0) - lax.broadcasted_iota(jnp.int32, shape, 1)
    for at in range(filters):
        width = widths_ref[at]
        band = jnp.where((lag >= 0) & (lag < width), 1.0, 0.0).astype(jnp.bfloat16)
        sums = jnp.dot(values, band, preferred_element_type=jnp.float32)
        root = jnp.sqrt(jnp.full((1, length), width, jnp.int32).astype(jnp.float32))
        scaled = sums / root
        for part in range(length // LANES):
            lanes = slice(part * LANES, (part + 1) * LANES)
            mixed[part, pl.ds(at, trials, stride=filters), :] = scaled[:, lanes]
    for part in range(length // LANES):
        out_ref[:, :, pl.ds(part * LANES, LANES)] = mixed[part].reshape(trials, filters, LANES)


def one_beam(own, key, lags, widths, place, groups, outer, per_sub, scale):
    chans, length = own.shape
    sub_dev = chans // per_sub
    inner = groups // outer
    padded = lags.shape[1]
    filters = widths.shape[0]
    halo = passed_back(own, "tm")
    series = pl.pallas_call(
        functools.partial(series_kernel, per_sub),
        out_shape=jax.ShapeDtypeStruct((sub_dev, length + LANES), jnp.bfloat16),
        grid=(1,),
        in_specs=[
            pl.BlockSpec((1, chans), lambda i: (0, 0)),
            pl.BlockSpec((chans, length), lambda i: (0, 0)),
            pl.BlockSpec((chans, LANES), lambda i: (0, 0)),
        ],
        out_specs=pl.BlockSpec((sub_dev, length + LANES), lambda i: (0, 0)),
        compiler_params=LIMIT,
    )(key, own, halo)
    line = [series] + [exchanged(series, "sub", flip * inner) for flip in range(1, outer)]
    span = length + OMAX
    nsub = outer * sub_dev
    turned = pl.pallas_call(
        functools.partial(turn_series_kernel, outer),
        out_shape=jax.ShapeDtypeStruct((span, nsub), jnp.bfloat16),
        in_specs=[SMEM] + [VMEM] * outer,
        out_specs=VMEM,
        scratch_shapes=[pltpu.VMEM((nsub, length + LANES), jnp.float32)],
        compiler_params=LIMIT,
    )(place, *line)
    blocks = [turned] + [exchanged(turned, "sub", flip) for flip in range(1, inner)]
    scratch = [
        pltpu.VMEM((span + 8, nsub), jnp.float32),
        pltpu.VMEM((nsub, padded), jnp.bfloat16),
        pltpu.VMEM((OMAX // STEP // 2, length + STEP, 2 * padded), jnp.float32),
    ]
    sums_shape = jax.ShapeDtypeStruct((length, padded), jnp.float32)
    flops = 2 * span * nsub * padded * (OMAX + 1)
    cost = pl.CostEstimate(flops=flops, bytes_accessed=1 << 20, transcendentals=0)
    common = dict(scratch_shapes=scratch, compiler_params=LIMIT, cost_estimate=cost)
    sums = pl.pallas_call(
        functools.partial(first_sums_kernel, outer),
        out_shape=sums_shape,
        in_specs=[SMEM, VMEM, VMEM],
        out_specs=VMEM,
        **common,
    )(place, turned, lags)
    for flip in range(1, inner - 1):
        sums = pl.pallas_call(
            functools.partial(more_sums_kernel, outer, flip),
            out_shape=sums_shape,
            in_specs=[SMEM, VMEM, VMEM, VMEM],
            out_specs=VMEM,
            **common,
        )(place, blocks[flip], lags, sums)
    main, head = pl.pallas_call(
        functools.partial(last_sums_kernel, outer, inner - 1, scale),
        out_shape=[
            jax.ShapeDtypeStruct((padded, length), jnp.bfloat16),
            jax.ShapeDtypeStruct((padded, WMAX), jnp.bfloat16),
        ],
        in_specs=[SMEM, VMEM, VMEM, VMEM],
        out_specs=[VMEM, VMEM],
        **common,
    )(place, blocks[inner - 1], lags, sums)
    later = passed_back(head, "tm")
    return pl.pallas_call(
        boxcar_kernel,
        out_shape=jax.ShapeDtypeStruct((padded, filters, length), jnp.float32),
        in_specs=[SMEM, VMEM, VMEM],
        out_specs=VMEM,
        scratch_shapes=[pltpu.VMEM((length // LANES, padded * filters, LANES), jnp.float32)],
        compiler_params=LIMIT,
    )(widths, main, later)


def per_device(data, delays, offsets, widths):
    beams, chans, length = data.shape
    trials, nsub = offsets.shape
    groups = lax.axis_size("sub")
    outer = 1 << (groups.bit_length() // 2)
    outer = outer if groups % (outer * outer) == 0 else outer // 2
    inner = groups // outer
    per_sub = chans // (nsub // groups)
    scale = 1.0 / math.sqrt(chans * groups)
    padded = max(trials, LANES)
    lag_table = jnp.pad(offsets, ((0, padded - trials), (0, 0))) if padded > trials else offsets
    block_subs = min(chans, 256) // per_sub
    channel = jnp.arange(chans, dtype=jnp.int32)
    key = (delays * block_subs + (channel // per_sub) % block_subs)[None, :]
    me = lax.axis_index("sub")
    place = jnp.stack([me // inner, me % inner]).astype(jnp.int32)
    lags = pl.pallas_call(
        turn_offsets_kernel,
        out_shape=jax.ShapeDtypeStruct((nsub, padded), jnp.bfloat16),
        in_specs=[VMEM],
        out_specs=VMEM,
        compiler_params=LIMIT,
    )(lag_table)
    outs = [
        one_beam(data[beam], key, lags, widths, place, groups, outer, per_sub, scale)[:trials, None]
        for beam in range(beams)
    ]
    return outs[0] if beams == 1 else jnp.concatenate(outs, axis=1)


def solution(mesh):
    placed = (P(None, "sub", "tm"), P("sub"), P("sub", None), P())
    return jax.shard_map(
        per_device,
        mesh=mesh,
        in_specs=placed,
        out_specs=P("sub", None, None, "tm"),
        check_vma=False,
    )
```

```python
import functools
import math

import jax
import jax.numpy as jnp
from jax import lax
from jax.experimental import pallas as pl
from jax.experimental.pallas import tpu as pltpu
from jax.sharding import PartitionSpec as P

WMAX = 128
DCH = 16
OMAX = 96
LANES = 128
STEP = 16
VMEM = pl.BlockSpec(memory_space=pltpu.VMEM)
SMEM = pl.BlockSpec(memory_space=pltpu.SMEM)


def passed_back(value, axis):
    count = lax.axis_size(axis)
    return lax.ppermute(value, axis, [(source, source - 1) for source in range(1, count)])


def exchanged(value, axis, flip):
    count = lax.axis_size(axis)
    return lax.ppermute(value, axis, [(source, source ^ flip) for source in range(count)])


def own_series_kernel(per_sub, key_ref, data_ref, sums_ref, member_ref):
    block, length = data_ref.shape
    subs = block // per_sub
    span = sums_ref.shape[1]
    rows = lax.broadcasted_iota(jnp.int32, (DCH * subs, block), 0)
    member = jnp.where(rows == key_ref[...], 1.0, 0.0).astype(jnp.bfloat16)
    member_ref[...] = member
    picked = jnp.dot(member, data_ref[...], preferred_element_type=jnp.float32)
    blank = jnp.zeros((subs, span - length), jnp.float32)
    total = jnp.concatenate([picked[:subs, :], blank], axis=1)
    for delay in range(1, DCH):
        wide = jnp.concatenate([picked[delay * subs : (delay + 1) * subs, :], blank], axis=1)
        total = total + pltpu.roll(wide, span - delay, 1)
    sums_ref[...] = total


def halo_series_kernel(per_sub, own_ref, member_ref, halo_ref, series_ref):
    span = own_ref.shape[1]
    block = member_ref.shape[1]
    subs = block // per_sub
    first = span - 2 * LANES
    blank = jnp.zeros((subs, LANES), jnp.float32)
    for at in range(halo_ref.shape[0] // block):
        member = member_ref[pl.ds(at * DCH * subs, DCH * subs), :]
        picked = jnp.dot(member, halo_ref[pl.ds(at * block, block), :], preferred_element_type=jnp.float32)
        here = pl.ds(at * subs, subs)
        total = own_ref[here, pl.ds(first, 2 * LANES)]
        for delay in range(DCH):
            wide = jnp.concatenate([blank, picked[delay * subs : (delay + 1) * subs, :]], axis=1)
            total = total + (pltpu.roll(wide, 2 * LANES - delay, 1) if delay else wide)
        series_ref[here, pl.ds(0, first)] = own_ref[here, pl.ds(0, first)].astype(jnp.bfloat16)
        series_ref[here, pl.ds(first, 2 * LANES)] = total.astype(jnp.bfloat16)


def turn_offsets_kernel(offsets_ref, lags_ref):
    for at in range(offsets_ref.shape[1] // LANES):
        here = pl.ds(at * LANES, LANES)
        lags_ref[here, :] = offsets_ref[:, here].astype(jnp.float32).T.astype(jnp.bfloat16)


def choices_kernel(outer, inner, flip, me_ref, lags_ref, chosen_ref):
    trials = lags_ref.shape[1]
    subs = lags_ref.shape[0] // (outer * inner)
    nsub = outer * subs
    row = me_ref[0] // inner
    column = (me_ref[0] % inner) ^ flip
    for slot in range(outer):
        start = pl.multiple_of(((row ^ slot) * inner + column) * subs, subs)
        table = lags_ref[pl.ds(start, subs), :]
        for lag in range(OMAX + 1):
            group = min(lag // STEP, OMAX // STEP - 1)
            place = (group // 2 * STEP + lag - group * STEP) * nsub + slot * subs
            chosen_ref[pl.ds(place, subs), pl.ds(group % 2 * trials, trials)] = jnp.where(
                table == jnp.bfloat16(lag), jnp.bfloat16(1), jnp.bfloat16(0)
            )
        place = OMAX // 2 * nsub + slot * subs
        chosen_ref[pl.ds(place, subs), pl.ds(0, trials)] = jnp.zeros((subs, trials), jnp.bfloat16)


def turn_series_kernel(outer, *refs):
    blocks, turned_ref = refs[:outer], refs[-1]
    subs = blocks[0].shape[0]
    rows = turned_ref.shape[0]
    joined = LANES // subs
    for at in range(outer // joined):
        for first in range(0, rows, LANES):
            count = min(LANES, rows - first)
            tile = jnp.concatenate(
                [
                    blocks[at * joined + slot][:, pl.ds(first, LANES)].astype(jnp.float32)
                    for slot in range(joined)
                ],
                axis=0,
            ).T
            turned_ref[pl.ds(first, count), pl.ds(at * LANES, LANES)] = tile[:count].astype(jnp.bfloat16)


def partial_sums(turned_ref, chosen_ref, moving, shifted):
    span, nsub = turned_ref.shape
    length = span - OMAX
    trials = chosen_ref.shape[1] // 2
    reach = shifted.shape[0]
    rows = length + STEP
    moving[...] = turned_ref[...].astype(jnp.float32)
    for lag in range(STEP + 1):
        lanes = pl.ds(lag * nsub, nsub)
        if lag % STEP:
            shifted[:, lanes] = moving[pl.ds(lag, reach), :].astype(jnp.bfloat16)
        else:
            shifted[:, lanes] = turned_ref[pl.ds(lag, reach), :]
    result = None
    pairs = OMAX // STEP // 2
    for pair in range(pairs):
        depth = (STEP + (pair == pairs - 1)) * nsub
        sums = jnp.dot(
            shifted[pl.ds(2 * STEP * pair, rows), pl.ds(0, depth)],
            chosen_ref[pl.ds(pair * STEP * nsub, depth), :],
            preferred_element_type=jnp.float32,
        )
        both = sums[:length, :trials] + sums[STEP : STEP + length, trials:]
        result = both if result is None else result + both
    return result


def first_sums_kernel(turned_ref, chosen_ref, sums_ref, *scratch):
    sums_ref[...] = partial_sums(turned_ref, chosen_ref, *scratch)


def more_sums_kernel(turned_ref, chosen_ref, before_ref, sums_ref, *scratch):
    sums_ref[...] = before_ref[...] + partial_sums(turned_ref, chosen_ref, *scratch)


def last_sums_kernel(scale, turned_ref, chosen_ref, before_ref, out_ref, head_ref, *scratch):
    sums = before_ref[...] + partial_sums(turned_ref, chosen_ref, *scratch)
    done = (sums * scale).T.astype(jnp.bfloat16)
    out_ref[...] = done
    head_ref[...] = done[:, :WMAX]


def bands_kernel(widths_ref, bands_ref):
    shape = (bands_ref.shape[0], LANES)
    lag = lax.broadcasted_iota(jnp.int32, shape, 0) - lax.broadcasted_iota(jnp.int32, shape, 1)
    for at in range(widths_ref.shape[0]):
        band = jnp.where((lag >= 0) & (lag < widths_ref[at]), 1.0, 0.0)
        bands_ref[:, pl.ds(at * LANES, LANES)] = band.astype(jnp.bfloat16)


def boxcars_of(values, widths_ref, bands_ref, mixed):
    trials = values.shape[0]
    filters = widths_ref.shape[0]
    for at in range(filters):
        sums = jnp.dot(values, bands_ref[:, pl.ds(at * LANES, LANES)], preferred_element_type=jnp.float32)
        root = jnp.sqrt(jnp.full((1, LANES), widths_ref[at], jnp.int32).astype(jnp.float32))
        mixed[pl.ds(at, trials, stride=filters), :] = sums / root


def early_boxcars_kernel(widths_ref, bands_ref, main_ref, out_ref, mixed, tiles, sems):
    trials, length = main_ref.shape
    filters = widths_ref.shape[0]
    copies = []
    for part in range(length // LANES - 1):
        boxcars_of(main_ref[:, pl.ds(part * LANES, 2 * LANES)], widths_ref, bands_ref, mixed)
        tiles[part] = mixed[...].reshape(trials, filters, LANES)
        target = out_ref.at[:, :, pl.ds(part * LANES, LANES)]
        copies.append(pltpu.make_async_copy(tiles.at[part], target, sems.at[part]))
        copies[-1].start()
    for copy in copies:
        copy.wait()


def late_boxcars_kernel(widths_ref, bands_ref, main_ref, later_ref, early_ref, out_ref, mixed, tiles, sem):
    del early_ref
    trials, length = main_ref.shape
    filters = widths_ref.shape[0]
    last = pl.ds(length - LANES, LANES)
    values = jnp.concatenate([main_ref[:, last], later_ref[...]], axis=1)
    boxcars_of(values, widths_ref, bands_ref, mixed)
    tiles[...] = mixed[...].reshape(trials, filters, LANES)
    copy = pltpu.make_async_copy(tiles, out_ref.at[:, :, last], sem)
    copy.start()
    copy.wait()


def call(kernel, out_shape, in_specs, args, scratch=(), flops=0, **options):
    several = isinstance(out_shape, list)
    options.setdefault("out_specs", [VMEM] * len(out_shape) if several else VMEM)
    return pl.pallas_call(
        kernel,
        out_shape=out_shape,
        in_specs=in_specs,
        scratch_shapes=list(scratch),
        compiler_params=pltpu.CompilerParams(vmem_limit_bytes=12 << 20),
        cost_estimate=pl.CostEstimate(flops=flops, bytes_accessed=1 << 20, transcendentals=0),
        **options,
    )(*args)


def one_beam(own, key, choices, bands, widths, groups, outer, per_sub, scale):
    chans, length = own.shape
    sub_dev = chans // per_sub
    inner = groups // outer
    padded = choices[0].shape[1] // 2
    filters = widths.shape[0]
    block = min(chans, 256)
    wide = length + LANES
    halo = passed_back(own, "tm")
    sums, member = call(
        functools.partial(own_series_kernel, per_sub),
        [
            jax.ShapeDtypeStruct((sub_dev, wide), jnp.float32),
            jax.ShapeDtypeStruct((DCH * sub_dev, block), jnp.bfloat16),
        ],
        [
            pl.BlockSpec((1, block), lambda i: (0, i)),
            pl.BlockSpec((block, length), lambda i: (i, 0)),
        ],
        (key, own),
        grid=(chans // block,),
        out_specs=[
            pl.BlockSpec((block // per_sub, wide), lambda i: (i, 0)),
            pl.BlockSpec((DCH * block // per_sub, block), lambda i: (i, 0)),
        ],
    )
    series = call(
        functools.partial(halo_series_kernel, per_sub),
        jax.ShapeDtypeStruct((sub_dev, wide), jnp.bfloat16),
        [
            pl.BlockSpec((sub_dev, wide), lambda i: (0, 0)),
            pl.BlockSpec((DCH * sub_dev, block), lambda i: (0, 0)),
            pl.BlockSpec((chans, LANES), lambda i: (0, 0)),
        ],
        (sums, member, halo),
        grid=(1,),
        out_specs=pl.BlockSpec((sub_dev, wide), lambda i: (0, 0)),
    )
    line = [series] + [exchanged(series, "sub", flip * inner) for flip in range(1, outer)]
    span = length + OMAX
    nsub = outer * sub_dev
    tables = (*choices, bands)
    turned = call(
        functools.partial(turn_series_kernel, outer),
        jax.ShapeDtypeStruct((span, nsub), jnp.bfloat16),
        [VMEM] * outer + [pl.BlockSpec(memory_space=pl.ANY)] * len(tables),
        (*line, *tables),
    )
    blocks = [turned] + [exchanged(turned, "sub", flip) for flip in range(1, inner)]
    scratch = [
        pltpu.VMEM((span, nsub), jnp.float32),
        pltpu.VMEM((span - STEP, (STEP + 1) * nsub), jnp.bfloat16),
    ]
    flops = 2 * (length + STEP) * nsub * padded * (OMAX + 2)
    sums_shape = jax.ShapeDtypeStruct((length, padded), jnp.float32)
    sums = call(first_sums_kernel, sums_shape, [VMEM] * 2, (turned, choices[0]), scratch, flops)
    for flip in range(1, inner - 1):
        sums = call(
            more_sums_kernel, sums_shape, [VMEM] * 3, (blocks[flip], choices[flip], sums), scratch, flops
        )
    main, head = call(
        functools.partial(last_sums_kernel, scale),
        [
            jax.ShapeDtypeStruct((padded, length), jnp.bfloat16),
            jax.ShapeDtypeStruct((padded, WMAX), jnp.bfloat16),
        ],
        [VMEM] * 3,
        (blocks[-1], choices[-1], sums),
        scratch,
        flops,
    )
    later = passed_back(head, "tm")
    out_shape = jax.ShapeDtypeStruct((padded, filters, length), jnp.float32)
    mixed = pltpu.VMEM((padded * filters, LANES), jnp.float32)
    parts = length // LANES - 1
    early = call(
        early_boxcars_kernel,
        out_shape,
        [SMEM, VMEM, VMEM],
        (widths, bands, main),
        [
            mixed,
            pltpu.VMEM((parts, padded, filters, LANES), jnp.float32),
            pltpu.SemaphoreType.DMA((parts,)),
        ],
        out_specs=pl.BlockSpec(memory_space=pl.ANY),
    )
    return call(
        late_boxcars_kernel,
        out_shape,
        [SMEM, VMEM, VMEM, VMEM, pl.BlockSpec(memory_space=pl.ANY)],
        (widths, bands, main, later, early),
        [mixed, pltpu.VMEM((padded, filters, LANES), jnp.float32), pltpu.SemaphoreType.DMA],
        out_specs=pl.BlockSpec(memory_space=pl.ANY),
        input_output_aliases={4: 0},
    )


def per_device(data, delays, offsets, widths):
    beams, chans, length = data.shape
    trials, nsub = offsets.shape
    groups = lax.axis_size("sub")
    outer = 1 << (groups.bit_length() // 2)
    outer = outer if groups % (outer * outer) == 0 else outer // 2
    inner = groups // outer
    per_sub = chans // (nsub // groups)
    scale = 1.0 / math.sqrt(chans * groups)
    padded = max(trials, LANES)
    lag_table = jnp.pad(offsets, ((0, padded - trials), (0, 0))) if padded > trials else offsets
    block_subs = min(chans, 256) // per_sub
    channel = jnp.arange(chans, dtype=jnp.int32)
    key = (delays * block_subs + (channel // per_sub) % block_subs)[None, :]
    me = lax.axis_index("sub").astype(jnp.int32).reshape(1)
    lags = call(
        turn_offsets_kernel, jax.ShapeDtypeStruct((nsub, padded), jnp.bfloat16), [VMEM], (lag_table,)
    )
    rows = (OMAX // 2 + 1) * (nsub // inner)
    choices = [
        call(
            functools.partial(choices_kernel, outer, inner, flip),
            jax.ShapeDtypeStruct((rows, 2 * padded), jnp.bfloat16),
            [SMEM, VMEM],
            (me, lags),
        )
        for flip in range(inner)
    ]
    bands = call(
        bands_kernel,
        jax.ShapeDtypeStruct((2 * LANES, widths.shape[0] * LANES), jnp.bfloat16),
        [SMEM],
        (widths,),
    )
    outs = [
        one_beam(data[beam], key, choices, bands, widths, groups, outer, per_sub, scale)[:trials, None]
        for beam in range(beams)
    ]
    return outs[0] if beams == 1 else jnp.concatenate(outs, axis=1)


def solution(mesh):
    placed = (P(None, "sub", "tm"), P("sub"), P("sub", None), P())
    return jax.shard_map(
        per_device,
        mesh=mesh,
        in_specs=placed,
        out_specs=P("sub", None, None, "tm"),
        check_vma=False,
    )
```

```python
import functools
import math

import jax
import jax.numpy as jnp
from jax import lax
from jax.experimental import pallas as pl
from jax.experimental.pallas import tpu as pltpu
from jax.sharding import PartitionSpec as P

WMAX = 128
DCH = 16
OMAX = 96
LANES = 128
STEP = 16
GROUPS = OMAX // STEP
REACH = OMAX + DCH
VMEM = pl.BlockSpec(memory_space=pltpu.VMEM)
SMEM = pl.BlockSpec(memory_space=pltpu.SMEM)
HBM = pl.BlockSpec(memory_space=pltpu.HBM)
ANY = pl.BlockSpec(memory_space=pl.ANY)


def passed_back(value, axis):
    count = lax.axis_size(axis)
    return lax.ppermute(value, axis, [(source, source - 1) for source in range(1, count)])


def exchanged(value, axis, flip):
    count = lax.axis_size(axis)
    return lax.ppermute(value, axis, [(source, source ^ flip) for source in range(count)])


def series_kernel(per_sub, packed, delays_ref, data_ref, series_ref, held, sems):
    chans, length = data_ref.shape
    block = min(chans, 256)
    subs = block // per_sub
    wide = length + LANES
    copies = []
    for at in range(chans // block):
        here = pl.ds(at * block, block)
        copies.append(pltpu.make_async_copy(data_ref.at[here, :], held.at[here, :], sems.at[at]))
        copies[-1].start()
    rows = lax.broadcasted_iota(jnp.int32, (DCH * subs, block), 0)
    owner = lax.broadcasted_iota(jnp.int32, (1, block), 1) // per_sub
    blank = jnp.zeros((subs, LANES), jnp.float32)
    parts = []
    for at in range(chans // block):
        here = pl.ds(at * block, block)
        member = jnp.where(rows == delays_ref[:, here] * subs + owner, 1.0, 0.0).astype(jnp.bfloat16)
        copies[at].wait()
        picked = jnp.dot(member, held[here, :], preferred_element_type=jnp.float32)
        total = None
        for delay in range(DCH):
            late = jnp.concatenate([picked[delay * subs : (delay + 1) * subs, :], blank], axis=1)
            late = pltpu.roll(late, DCH - delay, 1)
            total = late if total is None else total + late
        parts.append(total)
    total = jnp.concatenate(parts, axis=0)
    if packed:
        half = series_ref.shape[0]
        both = jnp.concatenate([total, pltpu.roll(total, wide - half, 1)], axis=0)
        for first in range(0, half, LANES):
            count = min(LANES, half - first)
            tile = both[:, first : first + LANES].T
            series_ref[pl.ds(first, count), :] = tile[:count].astype(jnp.bfloat16)
    else:
        series_ref[...] = total.astype(jnp.bfloat16)


def join_packed_kernel(outer, *refs):
    blocks, joined_ref = refs[:outer], refs[-1]
    half = blocks[0].shape[0]
    rest = joined_ref.shape[0] - half
    lane = lax.broadcasted_iota(jnp.int32, (half, LANES), 1)
    for at in range(outer // 2):
        left = blocks[2 * at][...].astype(jnp.float32)
        right = blocks[2 * at + 1][...].astype(jnp.float32)
        lanes = pl.ds(at * LANES, LANES)
        early = jnp.where(lane < LANES // 2, left, pltpu.roll(right, LANES // 2, 1))
        late = jnp.where(lane < LANES // 2, pltpu.roll(left, LANES // 2, 1), right)
        joined_ref[pl.ds(0, half), lanes] = early.astype(jnp.bfloat16)
        joined_ref[pl.ds(half, rest), lanes] = late[:rest].astype(jnp.bfloat16)


def join_kernel(outer, *refs):
    blocks, joined_ref = refs[:outer], refs[-1]
    subs = blocks[0].shape[0]
    rows = joined_ref.shape[0]
    several = LANES // subs
    for at in range(outer // several):
        for first in range(0, rows, LANES):
            count = min(LANES, rows - first)
            tile = jnp.concatenate(
                [
                    blocks[at * several + slot][:, pl.ds(first, LANES)].astype(jnp.float32)
                    for slot in range(several)
                ],
                axis=0,
            ).T
            joined_ref[pl.ds(first, count), pl.ds(at * LANES, LANES)] = tile[:count].astype(jnp.bfloat16)


def offsets_kernel(offsets_ref, group_ref, lag_ref, held, sems):
    copies = []
    for at in range(offsets_ref.shape[1] // LANES):
        here = pl.ds(at * LANES, LANES)
        copies.append(pltpu.make_async_copy(offsets_ref.at[:, here], held.at[at], sems.at[at]))
        copies[-1].start()
    for at, copy in enumerate(copies):
        here = pl.ds(at * LANES, LANES)
        copy.wait()
        offset = held[at].astype(jnp.float32).T
        group = jnp.zeros_like(offset)
        for edge in range(1, GROUPS):
            group = group + jnp.where(offset >= float(STEP * edge), 1.0, 0.0)
        group_ref[here, :] = group.astype(jnp.bfloat16)
        lag_ref[here, :] = (offset - float(STEP) * group).astype(jnp.bfloat16)


def one_where(table, value):
    one = jnp.bfloat16(1)
    return jnp.maximum(one - jnp.abs(table - jnp.bfloat16(value)), jnp.bfloat16(0))


def choices_kernel(outer, inner, flip, me_ref, group_ref, lag_ref, chosen_ref):
    trials = lag_ref.shape[1]
    subs = lag_ref.shape[0] // (outer * inner)
    nsub = outer * subs
    row = me_ref[0] // inner
    column = (me_ref[0] % inner) ^ flip
    for slot in range(outer):
        start = pl.multiple_of(((row ^ slot) * inner + column) * subs, subs)
        groups = group_ref[pl.ds(start, subs), :]
        lags = lag_ref[pl.ds(start, subs), :]
        in_group = [one_where(groups, group) for group in range(GROUPS)]
        for lag in range(STEP + 1):
            at_lag = one_where(lags, lag)
            for group in range(GROUPS - 2 if lag == STEP else 0, GROUPS):
                place = (group // 2 * STEP + lag) * nsub + slot * subs
                chosen_ref[pl.ds(place, subs), pl.ds(group % 2 * trials, trials)] = at_lag * in_group[group]


def sums_kernel(given, joined_ref, chosen_ref, *refs):
    before_ref, sums_ref, *early_ref = refs[:-2] if given else (None, *refs[:-2])
    moving, shifted = refs[-2:]
    span, nsub = joined_ref.shape
    trials = chosen_ref.shape[1] // 2
    rows = span + STEP
    blank = jnp.zeros((STEP, nsub), jnp.float32)
    moving[pl.ds(0, STEP), :] = blank
    moving[pl.ds(STEP, span), :] = joined_ref[...].astype(jnp.float32)
    moving[pl.ds(STEP + span, STEP), :] = blank
    for lag in range(STEP + 1):
        shifted[:, pl.ds(lag * nsub, nsub)] = moving[pl.ds(lag, rows), :].astype(jnp.bfloat16)
    if before_ref is None:
        sums_ref[...] = jnp.zeros_like(sums_ref)
    else:
        sums_ref[...] = before_ref[...]
    for pair in range(GROUPS // 2):
        depth = (STEP + (pair == GROUPS // 2 - 1)) * nsub
        both = jnp.dot(
            shifted[:, pl.ds(0, depth)],
            chosen_ref[pl.ds(pair * STEP * nsub, depth), :],
            preferred_element_type=jnp.float32,
        )
        for odd in range(2):
            first = STEP * (GROUPS - 1 - 2 * pair - odd)
            sums_ref[pl.ds(first, rows), :] += both[:, odd * trials : (odd + 1) * trials]
    for ref in early_ref:
        ref[...] = sums_ref[pl.ds(0, ref.shape[0]), :]


def bands_kernel(widths_ref, bands_ref):
    shape = (bands_ref.shape[0], LANES)
    lag = lax.broadcasted_iota(jnp.int32, shape, 0) - lax.broadcasted_iota(jnp.int32, shape, 1)
    for at in range(widths_ref.shape[0]):
        band = jnp.where((lag >= 0) & (lag < widths_ref[at]), 1.0, 0.0)
        bands_ref[:, pl.ds(at * LANES, LANES)] = band.astype(jnp.bfloat16)


def boxcars_kernel(scale, widths_ref, bands_ref, sums_ref, later_ref, out_ref, values, mixed, tiles, sems):
    trials = sums_ref.shape[1]
    length = sums_ref.shape[0] - REACH
    filters = widths_ref.shape[0]
    whole = length - REACH
    total = jnp.concatenate(
        [
            sums_ref[pl.ds(REACH, whole), :],
            sums_ref[pl.ds(length, REACH), :] + later_ref[pl.ds(0, REACH), :],
            later_ref[pl.ds(REACH, WMAX), :],
        ],
        axis=0,
    )
    for first in range(0, length + WMAX, LANES):
        tile = (total[first : first + LANES] * scale).T
        values[:, pl.ds(first, LANES)] = tile.astype(jnp.bfloat16)
    share = trials // sems.shape[1]
    copies = []
    for part in range(length // LANES):
        lanes = pl.ds(part * LANES, LANES)
        for at in range(filters):
            sums = jnp.dot(
                values[:, pl.ds(part * LANES, LANES + WMAX)],
                bands_ref[:, pl.ds(at * LANES, LANES)],
                preferred_element_type=jnp.float32,
            )
            root = jnp.sqrt(jnp.full((1, LANES), widths_ref[at], jnp.int32).astype(jnp.float32))
            mixed[part, pl.ds(at, trials, stride=filters), :] = sums / root
        tiles[part] = mixed[part].reshape(trials, filters, LANES)
        for piece in range(sems.shape[1]):
            some = pl.ds(piece * share, share)
            copies.append(
                pltpu.make_async_copy(
                    tiles.at[part, some], out_ref.at[some, :, lanes], sems.at[part, piece]
                )
            )
            copies[-1].start()
    for copy in copies:
        copy.wait()


def call(kernel, out_shape, in_specs, args, scratch=(), flops=0, **options):
    several = isinstance(out_shape, list)
    options.setdefault("out_specs", [VMEM] * len(out_shape) if several else VMEM)
    return pl.pallas_call(
        kernel,
        out_shape=out_shape,
        in_specs=in_specs,
        scratch_shapes=list(scratch),
        compiler_params=pltpu.CompilerParams(vmem_limit_bytes=12 << 20),
        cost_estimate=pl.CostEstimate(flops=flops, bytes_accessed=1 << 20, transcendentals=0),
        **options,
    )(*args)


def one_beam(own, delays, choices, bands, widths, groups, outer, per_sub, scale):
    chans, length = own.shape
    sub_dev = chans // per_sub
    inner = groups // outer
    padded = choices[0].shape[1] // 2
    filters = widths.shape[0]
    span = length + DCH
    packed = 2 * sub_dev == LANES
    series_shape = (-(-span // 32) * 16, LANES) if packed else (sub_dev, length + LANES)
    steps = max(1, chans // 256)
    series = call(
        functools.partial(series_kernel, per_sub, packed),
        jax.ShapeDtypeStruct(series_shape, jnp.bfloat16),
        [VMEM, HBM],
        (delays[None, :], pltpu.with_memory_space_constraint(own, pltpu.HBM)),
        [pltpu.VMEM((chans, length), jnp.bfloat16), pltpu.SemaphoreType.DMA((steps,))],
    )
    line = [series] + [exchanged(series, "sub", flip * inner) for flip in range(1, outer)]
    nsub = outer * sub_dev
    tables = (*choices, bands)
    joined = call(
        functools.partial(join_packed_kernel if packed else join_kernel, outer),
        jax.ShapeDtypeStruct((span, nsub), jnp.bfloat16),
        [VMEM] * outer + [ANY] * len(tables),
        (*line, *tables),
    )
    blocks = [joined] + [exchanged(joined, "sub", flip) for flip in range(1, inner)]
    scratch = [
        pltpu.VMEM((span + 2 * STEP, nsub), jnp.float32),
        pltpu.VMEM((span + STEP, (STEP + 1) * nsub), jnp.bfloat16),
    ]
    flops = 2 * (span + STEP) * nsub * padded * (OMAX + 2)
    sums_shape = jax.ShapeDtypeStruct((length + REACH, padded), jnp.float32)
    early_shape = jax.ShapeDtypeStruct((REACH + WMAX, padded), jnp.float32)
    sums = []
    for flip in range(inner):
        sums = call(
            functools.partial(sums_kernel, flip > 0),
            [sums_shape, early_shape] if flip == inner - 1 else [sums_shape],
            [VMEM] * (2 + len(sums)),
            (blocks[flip], choices[flip], *sums),
            scratch,
            flops,
        )
    sums, early = sums
    later = passed_back(early, "tm")
    parts = length // LANES
    pieces = 4
    return call(
        functools.partial(boxcars_kernel, scale),
        jax.ShapeDtypeStruct((padded, filters, length), jnp.float32),
        [SMEM, VMEM, VMEM, VMEM],
        (widths, bands, sums, later),
        [
            pltpu.VMEM((padded, length + WMAX), jnp.bfloat16),
            pltpu.VMEM((parts, padded * filters, LANES), jnp.float32),
            pltpu.VMEM((parts, padded, filters, LANES), jnp.float32),
            pltpu.SemaphoreType.DMA((parts, pieces)),
        ],
        out_specs=HBM,
    )


def per_device(data, delays, offsets, widths):
    beams, chans, length = data.shape
    trials, nsub = offsets.shape
    groups = lax.axis_size("sub")
    outer = 1 << (groups.bit_length() // 2)
    outer = outer if groups % (outer * outer) == 0 else outer // 2
    inner = groups // outer
    per_sub = chans // (nsub // groups)
    scale = 1.0 / math.sqrt(chans * groups)
    padded = max(trials, LANES)
    offset_table = jnp.pad(offsets, ((0, padded - trials), (0, 0))) if padded > trials else offsets
    me = lax.axis_index("sub").astype(jnp.int32).reshape(1)
    split_shape = jax.ShapeDtypeStruct((nsub, padded), jnp.bfloat16)
    columns = nsub // LANES
    split = call(
        offsets_kernel,
        [split_shape, split_shape],
        [HBM],
        (pltpu.with_memory_space_constraint(offset_table, pltpu.HBM),),
        [pltpu.VMEM((columns, padded, LANES), jnp.int32), pltpu.SemaphoreType.DMA((columns,))],
    )
    rows = (GROUPS // 2 * STEP + 1) * (nsub // inner)
    choices = [
        call(
            functools.partial(choices_kernel, outer, inner, flip),
            jax.ShapeDtypeStruct((rows, 2 * padded), jnp.bfloat16),
            [SMEM, VMEM, VMEM],
            (me, *split),
        )
        for flip in range(inner)
    ]
    bands = call(
        bands_kernel,
        jax.ShapeDtypeStruct((LANES + WMAX, widths.shape[0] * LANES), jnp.bfloat16),
        [SMEM],
        (widths,),
    )
    outs = [
        one_beam(data[beam], delays, choices, bands, widths, groups, outer, per_sub, scale)[:trials, None]
        for beam in range(beams)
    ]
    return outs[0] if beams == 1 else jnp.concatenate(outs, axis=1)


def solution(mesh):
    placed = (P(None, "sub", "tm"), P("sub"), P("sub", None), P())
    return jax.shard_map(
        per_device,
        mesh=mesh,
        in_specs=placed,
        out_specs=P("sub", None, None, "tm"),
        check_vma=False,
    )
```

```python
import functools
import math

import jax
import jax.numpy as jnp
from jax import lax
from jax.experimental import pallas as pl
from jax.experimental.pallas import tpu as pltpu
from jax.sharding import PartitionSpec as P

WMAX = 128
DCH = 16
OMAX = 96
LANES = 128
STEP = 16
GROUPS = OMAX // STEP
REACH = OMAX + DCH
VMEM = pl.BlockSpec(memory_space=pltpu.VMEM)
SMEM = pl.BlockSpec(memory_space=pltpu.SMEM)
HBM = pl.BlockSpec(memory_space=pltpu.HBM)
ANY = pl.BlockSpec(memory_space=pl.ANY)


def passed_back(value, axis):
    count = lax.axis_size(axis)
    return lax.ppermute(value, axis, [(source, source - 1) for source in range(1, count)])


def exchanged(value, axis, flip):
    count = lax.axis_size(axis)
    return lax.ppermute(value, axis, [(source, source ^ flip) for source in range(count)])


def series_kernel(
    per_sub, packed, delays_ref, data_ref, offsets_ref, series_ref, fetched_ref, delays, held, delays_sem, sems
):
    chans, length = data_ref.shape
    block = min(chans, 256)
    subs = block // per_sub
    wide = length + LANES
    first_copy = pltpu.make_async_copy(delays_ref, delays, delays_sem)
    first_copy.start()
    copies = []
    steps = sems.shape[0] // 2
    for source, target, base in ((data_ref, held, 0), (offsets_ref, fetched_ref, steps)):
        share = source.shape[0] // steps
        for at in range(steps):
            here = pl.ds(at * share, share)
            copies.append(
                pltpu.make_async_copy(source.at[here, :], target.at[here, :], sems.at[base + at])
            )
            copies[-1].start()
    rows = lax.broadcasted_iota(jnp.int32, (DCH * subs, block), 0)
    owner = lax.broadcasted_iota(jnp.int32, (1, block), 1) // per_sub
    blank = jnp.zeros((subs, LANES), jnp.float32)
    first_copy.wait()
    members = [
        jnp.where(rows == delays[:, at * block : (at + 1) * block] * subs + owner, 1.0, 0.0).astype(jnp.bfloat16)
        for at in range(chans // block)
    ]
    for copy in copies[:steps]:
        copy.wait()
    parts = []
    for at, member in enumerate(members):
        picked = jnp.dot(member, held[pl.ds(at * block, block), :], preferred_element_type=jnp.float32)
        total = None
        for delay in range(DCH):
            late = jnp.concatenate([picked[delay * subs : (delay + 1) * subs, :], blank], axis=1)
            late = pltpu.roll(late, DCH - delay, 1)
            total = late if total is None else total + late
        parts.append(total)
    total = jnp.concatenate(parts, axis=0)
    if packed:
        half = series_ref.shape[0]
        both = jnp.concatenate([total, pltpu.roll(total, wide - half, 1)], axis=0)
        for first in range(0, half, LANES):
            count = min(LANES, half - first)
            tile = both[:, first : first + LANES].T
            series_ref[pl.ds(first, count), :] = tile[:count].astype(jnp.bfloat16)
    else:
        series_ref[...] = total.astype(jnp.bfloat16)
    for copy in copies[steps:]:
        copy.wait()


def join_packed_kernel(outer, *refs):
    blocks, joined_ref = refs[:outer], refs[-1]
    half = blocks[0].shape[0]
    rest = joined_ref.shape[0] - half
    lane = lax.broadcasted_iota(jnp.int32, (half, LANES), 1)
    for at in range(outer // 2):
        left = blocks[2 * at][...].astype(jnp.float32)
        right = blocks[2 * at + 1][...].astype(jnp.float32)
        lanes = pl.ds(at * LANES, LANES)
        early = jnp.where(lane < LANES // 2, left, pltpu.roll(right, LANES // 2, 1))
        late = jnp.where(lane < LANES // 2, pltpu.roll(left, LANES // 2, 1), right)
        joined_ref[pl.ds(0, half), lanes] = early.astype(jnp.bfloat16)
        joined_ref[pl.ds(half, rest), lanes] = late[:rest].astype(jnp.bfloat16)


def join_kernel(outer, *refs):
    blocks, joined_ref = refs[:outer], refs[-1]
    subs = blocks[0].shape[0]
    rows = joined_ref.shape[0]
    several = LANES // subs
    for at in range(outer // several):
        for first in range(0, rows, LANES):
            count = min(LANES, rows - first)
            tile = jnp.concatenate(
                [
                    blocks[at * several + slot][:, pl.ds(first, LANES)].astype(jnp.float32)
                    for slot in range(several)
                ],
                axis=0,
            ).T
            joined_ref[pl.ds(first, count), pl.ds(at * LANES, LANES)] = tile[:count].astype(jnp.bfloat16)


def offsets_kernel(offsets_ref, group_ref, lag_ref):
    for at in range(offsets_ref.shape[1] // LANES):
        here = pl.ds(at * LANES, LANES)
        offset = offsets_ref[:, here].astype(jnp.float32).T
        group = jnp.minimum(jnp.floor(offset * (1.0 / STEP)), float(GROUPS - 1))
        group_ref[here, :] = group.astype(jnp.bfloat16)
        lag_ref[here, :] = (offset - float(STEP) * group).astype(jnp.bfloat16)


def one_where(table, value):
    one = jnp.bfloat16(1)
    return jnp.maximum(one - jnp.abs(table - jnp.bfloat16(value)), jnp.bfloat16(0))


def sums_kernel(given, outer, inner, flip, me_ref, joined_ref, group_ref, lag_ref, *refs):
    before_ref, sums_ref, *early_ref = refs[:-4] if given else (None, *refs[:-4])
    moving, shifted, in_group, at_lag = refs[-4:]
    span, nsub = joined_ref.shape
    trials = lag_ref.shape[1]
    rows = span + STEP
    subs = nsub // outer
    row = me_ref[0] // inner
    column = (me_ref[0] % inner) ^ flip
    for slot in range(outer):
        start = pl.multiple_of(((row ^ slot) * inner + column) * subs, subs)
        groups = group_ref[pl.ds(start, subs), :]
        lags = lag_ref[pl.ds(start, subs), :]
        for group in range(GROUPS):
            in_group[pl.ds(group * nsub + slot * subs, subs), :] = one_where(groups, group)
        for lag in range(STEP + 1):
            at_lag[pl.ds(lag * nsub + slot * subs, subs), :] = one_where(lags, lag)
    blank = jnp.zeros((STEP, nsub), jnp.float32)
    moving[pl.ds(0, STEP), :] = blank
    moving[pl.ds(STEP, span), :] = joined_ref[...].astype(jnp.float32)
    moving[pl.ds(STEP + span, STEP), :] = blank
    for lag in range(STEP + 1):
        shifted[:, pl.ds(lag * nsub, nsub)] = moving[pl.ds(lag, rows), :].astype(jnp.bfloat16)
    if before_ref is None:
        sums_ref[...] = jnp.zeros_like(sums_ref)
    else:
        sums_ref[...] = before_ref[...]
    for pair in range(GROUPS // 2):
        lags = STEP + (pair == GROUPS // 2 - 1)
        chosen = jnp.concatenate(
            [
                jnp.concatenate(
                    [
                        at_lag[pl.ds(lag * nsub, nsub), :] * in_group[pl.ds((2 * pair + odd) * nsub, nsub), :]
                        for odd in range(2)
                    ],
                    axis=1,
                )
                for lag in range(lags)
            ],
            axis=0,
        )
        both = jnp.dot(shifted[:, pl.ds(0, lags * nsub)], chosen, preferred_element_type=jnp.float32)
        for odd in range(2):
            first = STEP * (GROUPS - 1 - 2 * pair - odd)
            sums_ref[pl.ds(first, rows), :] += both[:, odd * trials : (odd + 1) * trials]
    for ref in early_ref:
        ref[...] = sums_ref[pl.ds(0, ref.shape[0]), :]


def bands_kernel(widths_ref, early_ref, bands_ref):
    del early_ref
    shape = (bands_ref.shape[0], LANES)
    lag = lax.broadcasted_iota(jnp.int32, shape, 0) - lax.broadcasted_iota(jnp.int32, shape, 1)
    for at in range(widths_ref.shape[0]):
        band = jnp.where((lag >= 0) & (lag < widths_ref[at]), 1.0, 0.0)
        bands_ref[:, pl.ds(at * LANES, LANES)] = band.astype(jnp.bfloat16)


def boxcars_kernel(scale, widths_ref, bands_ref, sums_ref, later_ref, out_ref, values, mixed, tiles, sems):
    trials = sums_ref.shape[1]
    length = sums_ref.shape[0] - REACH
    filters = widths_ref.shape[0]
    whole = length - REACH
    total = jnp.concatenate(
        [
            sums_ref[pl.ds(REACH, whole), :],
            sums_ref[pl.ds(length, REACH), :] + later_ref[pl.ds(0, REACH), :],
            later_ref[pl.ds(REACH, WMAX), :],
        ],
        axis=0,
    )
    for first in range(0, length + WMAX, LANES):
        tile = (total[first : first + LANES] * scale).T
        values[:, pl.ds(first, LANES)] = tile.astype(jnp.bfloat16)
    share = trials // sems.shape[1]
    copies = []
    for part in range(length // LANES):
        lanes = pl.ds(part * LANES, LANES)
        for at in range(filters):
            sums = jnp.dot(
                values[:, pl.ds(part * LANES, LANES + WMAX)],
                bands_ref[:, pl.ds(at * LANES, LANES)],
                preferred_element_type=jnp.float32,
            )
            root = jnp.sqrt(jnp.full((1, LANES), widths_ref[at], jnp.int32).astype(jnp.float32))
            mixed[part, pl.ds(at, trials, stride=filters), :] = sums / root
        tiles[part] = mixed[part].reshape(trials, filters, LANES)
        for piece in range(sems.shape[1]):
            some = pl.ds(piece * share, share)
            copies.append(
                pltpu.make_async_copy(
                    tiles.at[part, some], out_ref.at[some, :, lanes], sems.at[part, piece]
                )
            )
            copies[-1].start()
    for copy in copies:
        copy.wait()


def call(kernel, out_shape, in_specs, args, scratch=(), flops=0, **options):
    several = isinstance(out_shape, list)
    options.setdefault("out_specs", [VMEM] * len(out_shape) if several else VMEM)
    return pl.pallas_call(
        kernel,
        out_shape=out_shape,
        in_specs=in_specs,
        scratch_shapes=list(scratch),
        compiler_params=pltpu.CompilerParams(vmem_limit_bytes=12 << 20),
        cost_estimate=pl.CostEstimate(flops=flops, bytes_accessed=1 << 20, transcendentals=0),
        **options,
    )(*args)


def one_beam(own, delays, offsets, me, widths, groups, outer, per_sub, scale):
    chans, length = own.shape
    padded, all_subs = offsets.shape
    sub_dev = chans // per_sub
    inner = groups // outer
    filters = widths.shape[0]
    span = length + DCH
    packed = 2 * sub_dev == LANES
    series_shape = (-(-span // 32) * 16, LANES) if packed else (sub_dev, length + LANES)
    steps = 4
    series, fetched = call(
        functools.partial(series_kernel, per_sub, packed),
        [
            jax.ShapeDtypeStruct(series_shape, jnp.bfloat16),
            jax.ShapeDtypeStruct((padded, all_subs), jnp.int32),
        ],
        [HBM, HBM, HBM],
        tuple(pltpu.with_memory_space_constraint(x, pltpu.HBM) for x in (delays[None, :], own, offsets)),
        [
            pltpu.VMEM((1, chans), jnp.int32),
            pltpu.VMEM((chans, length), jnp.bfloat16),
            pltpu.SemaphoreType.DMA,
            pltpu.SemaphoreType.DMA((2 * steps,)),
        ],
    )
    line = [series] + [exchanged(series, "sub", flip * inner) for flip in range(1, outer)]
    split_shape = jax.ShapeDtypeStruct((all_subs, padded), jnp.bfloat16)
    split = call(offsets_kernel, [split_shape, split_shape], [VMEM], (fetched,))
    nsub = outer * sub_dev
    joined = call(
        functools.partial(join_packed_kernel if packed else join_kernel, outer),
        jax.ShapeDtypeStruct((span, nsub), jnp.bfloat16),
        [VMEM] * outer + [ANY] * len(split),
        (*line, *split),
    )
    blocks = [joined] + [exchanged(joined, "sub", flip) for flip in range(1, inner)]
    scratch = [
        pltpu.VMEM((span + 2 * STEP, nsub), jnp.float32),
        pltpu.VMEM((span + STEP, (STEP + 1) * nsub), jnp.bfloat16),
        pltpu.VMEM((GROUPS * nsub, padded), jnp.bfloat16),
        pltpu.VMEM(((STEP + 1) * nsub, padded), jnp.bfloat16),
    ]
    flops = 2 * (span + STEP) * nsub * padded * (OMAX + 2)
    sums_shape = jax.ShapeDtypeStruct((length + REACH, padded), jnp.float32)
    early_shape = jax.ShapeDtypeStruct((REACH + WMAX, padded), jnp.float32)
    sums = []
    for flip in range(inner):
        sums = call(
            functools.partial(sums_kernel, flip > 0, outer, inner, flip),
            [sums_shape, early_shape] if flip == inner - 1 else [sums_shape],
            [SMEM] + [VMEM] * (3 + len(sums)),
            (me, blocks[flip], *split, *sums),
            scratch,
            flops,
        )
    sums, early = sums
    later = passed_back(early, "tm")
    bands = call(
        bands_kernel,
        jax.ShapeDtypeStruct((LANES + WMAX, filters * LANES), jnp.bfloat16),
        [SMEM, ANY],
        (widths, early),
    )
    parts = length // LANES
    pieces = 4
    return call(
        functools.partial(boxcars_kernel, scale),
        jax.ShapeDtypeStruct((padded, filters, length), jnp.float32),
        [SMEM, VMEM, VMEM, VMEM],
        (widths, bands, sums, later),
        [
            pltpu.VMEM((padded, length + WMAX), jnp.bfloat16),
            pltpu.VMEM((parts, padded * filters, LANES), jnp.float32),
            pltpu.VMEM((parts, padded, filters, LANES), jnp.float32),
            pltpu.SemaphoreType.DMA((parts, pieces)),
        ],
        out_specs=HBM,
    )


def per_device(data, delays, offsets, widths):
    beams, chans, length = data.shape
    trials, nsub = offsets.shape
    groups = lax.axis_size("sub")
    outer = 1 << (groups.bit_length() // 2)
    outer = outer if groups % (outer * outer) == 0 else outer // 2
    per_sub = chans // (nsub // groups)
    scale = 1.0 / math.sqrt(chans * groups)
    padded = max(trials, LANES)
    table = jnp.pad(offsets, ((0, padded - trials), (0, 0))) if padded > trials else offsets
    me = lax.axis_index("sub").astype(jnp.int32).reshape(1)
    outs = [
        one_beam(data[beam], delays, table, me, widths, groups, outer, per_sub, scale)[:trials, None]
        for beam in range(beams)
    ]
    return outs[0] if beams == 1 else jnp.concatenate(outs, axis=1)


def solution(mesh):
    placed = (P(None, "sub", "tm"), P("sub"), P("sub", None), P())
    return jax.shard_map(
        per_device,
        mesh=mesh,
        in_specs=placed,
        out_specs=P("sub", None, None, "tm"),
        check_vma=False,
    )
```

```python
import functools
import math

import jax
import jax.numpy as jnp
from jax import lax
from jax.experimental import pallas as pl
from jax.experimental.pallas import tpu as pltpu
from jax.sharding import PartitionSpec as P

WMAX = 128
DCH = 16
OMAX = 96
LANES = 128
STEP = 16
GROUPS = OMAX // STEP
REACH = OMAX + DCH
VMEM = pl.BlockSpec(memory_space=pltpu.VMEM)
SMEM = pl.BlockSpec(memory_space=pltpu.SMEM)
HBM = pl.BlockSpec(memory_space=pltpu.HBM)
ANY = pl.BlockSpec(memory_space=pl.ANY)


def passed_back(value, axis):
    count = lax.axis_size(axis)
    return lax.ppermute(value, axis, [(source, source - 1) for source in range(1, count)])


def exchanged(value, axis, flip):
    count = lax.axis_size(axis)
    return lax.ppermute(value, axis, [(source, source ^ flip) for source in range(count)])


def series_kernel(
    per_sub, packed, delays_ref, data_ref, offsets_ref, series_ref, fetched_ref, delays, held, delays_sem, sems
):
    chans, length = data_ref.shape
    block = min(chans, 256)
    subs = block // per_sub
    wide = length + LANES
    first_copy = pltpu.make_async_copy(delays_ref, delays, delays_sem)
    first_copy.start()
    copies = []
    steps = sems.shape[0] // 2
    for source, target, base in ((data_ref, held, 0), (offsets_ref, fetched_ref, steps)):
        share = source.shape[0] // steps
        for at in range(steps):
            here = pl.ds(at * share, share)
            copies.append(
                pltpu.make_async_copy(source.at[here, :], target.at[here, :], sems.at[base + at])
            )
            copies[-1].start()
    rows = lax.broadcasted_iota(jnp.int32, (DCH * subs, block), 0)
    owner = lax.broadcasted_iota(jnp.int32, (1, block), 1) // per_sub
    blank = jnp.zeros((subs, LANES), jnp.float32)
    first_copy.wait()
    members = [
        jnp.where(rows == delays[:, at * block : (at + 1) * block] * subs + owner, 1.0, 0.0).astype(jnp.bfloat16)
        for at in range(chans // block)
    ]
    for copy in copies[:steps]:
        copy.wait()
    parts = []
    for at, member in enumerate(members):
        picked = jnp.dot(member, held[pl.ds(at * block, block), :], preferred_element_type=jnp.float32)
        total = None
        for delay in range(DCH):
            late = jnp.concatenate([picked[delay * subs : (delay + 1) * subs, :], blank], axis=1)
            late = pltpu.roll(late, DCH - delay, 1)
            total = late if total is None else total + late
        parts.append(total)
    total = jnp.concatenate(parts, axis=0)
    if packed:
        half = series_ref.shape[0]
        both = jnp.concatenate([total, pltpu.roll(total, wide - half, 1)], axis=0)
        for first in range(0, half, LANES):
            count = min(LANES, half - first)
            tile = both[:, first : first + LANES].T
            series_ref[pl.ds(first, count), :] = tile[:count].astype(jnp.bfloat16)
    else:
        series_ref[...] = total.astype(jnp.bfloat16)
    for copy in copies[steps:]:
        copy.wait()


def join_packed_kernel(outer, *refs):
    blocks, joined_ref = refs[:outer], refs[-1]
    half = blocks[0].shape[0]
    rest = joined_ref.shape[0] - half
    lane = lax.broadcasted_iota(jnp.int32, (half, LANES), 1)
    for at in range(outer // 2):
        left = blocks[2 * at][...].astype(jnp.float32)
        right = blocks[2 * at + 1][...].astype(jnp.float32)
        lanes = pl.ds(at * LANES, LANES)
        early = jnp.where(lane < LANES // 2, left, pltpu.roll(right, LANES // 2, 1))
        late = jnp.where(lane < LANES // 2, pltpu.roll(left, LANES // 2, 1), right)
        joined_ref[pl.ds(0, half), lanes] = early.astype(jnp.bfloat16)
        joined_ref[pl.ds(half, rest), lanes] = late[:rest].astype(jnp.bfloat16)


def join_kernel(outer, *refs):
    blocks, joined_ref = refs[:outer], refs[-1]
    subs = blocks[0].shape[0]
    rows = joined_ref.shape[0]
    several = LANES // subs
    for at in range(outer // several):
        for first in range(0, rows, LANES):
            count = min(LANES, rows - first)
            tile = jnp.concatenate(
                [
                    blocks[at * several + slot][:, pl.ds(first, LANES)].astype(jnp.float32)
                    for slot in range(several)
                ],
                axis=0,
            ).T
            joined_ref[pl.ds(first, count), pl.ds(at * LANES, LANES)] = tile[:count].astype(jnp.bfloat16)


def offsets_kernel(offsets_ref, group_ref, lag_ref):
    for at in range(offsets_ref.shape[1] // LANES):
        here = pl.ds(at * LANES, LANES)
        offset = offsets_ref[:, here].astype(jnp.float32).T
        group = jnp.minimum(jnp.floor(offset * (1.0 / STEP)), float(GROUPS - 1))
        group_ref[here, :] = group.astype(jnp.bfloat16)
        lag_ref[here, :] = (offset - float(STEP) * group).astype(jnp.bfloat16)


def one_where(table, value):
    one = jnp.bfloat16(1)
    return jnp.maximum(one - jnp.abs(table - jnp.bfloat16(value)), jnp.bfloat16(0))


def store_choices(slot, outer, inner, flip, me_ref, group_ref, lag_ref, chosen_ref):
    trials = lag_ref.shape[1]
    subs = lag_ref.shape[0] // (outer * inner)
    nsub = outer * subs
    row = me_ref[0] // inner
    column = (me_ref[0] % inner) ^ flip
    start = pl.multiple_of(((row ^ slot) * inner + column) * subs, subs)
    groups = group_ref[pl.ds(start, subs), :]
    lags = lag_ref[pl.ds(start, subs), :]
    in_group = [one_where(groups, group) for group in range(GROUPS)]
    for lag in range(STEP + 1):
        at_lag = one_where(lags, lag)
        for group in range(GROUPS - 2 if lag == STEP else 0, GROUPS):
            place = (group // 2 * STEP + lag) * nsub + slot * subs
            chosen_ref[pl.ds(place, subs), pl.ds(group % 2 * trials, trials)] = at_lag * in_group[group]


def choices_kernel(outer, inner, me_ref, group_ref, lag_ref, chosen_ref):
    for slot in range(outer):
        store_choices(slot, outer, inner, 0, me_ref, group_ref, lag_ref, chosen_ref)


def sums_kernel(given, then, outer, inner, me_ref, joined_ref, group_ref, lag_ref, chosen_ref, *refs):
    before_ref, sums_ref, other_ref = refs[:-2] if given else (None, *refs[:-2])
    moving, shifted = refs[-2:]
    span, nsub = joined_ref.shape
    trials = lag_ref.shape[1]
    rows = span + STEP
    blank = jnp.zeros((STEP, nsub), jnp.float32)
    moving[pl.ds(0, STEP), :] = blank
    moving[pl.ds(STEP, span), :] = joined_ref[...].astype(jnp.float32)
    moving[pl.ds(STEP + span, STEP), :] = blank
    for lag in range(STEP + 1):
        shifted[:, pl.ds(lag * nsub, nsub)] = moving[pl.ds(lag, rows), :].astype(jnp.bfloat16)
    if before_ref is None:
        sums_ref[...] = jnp.zeros_like(sums_ref)
    else:
        sums_ref[...] = before_ref[...]
    pairs = GROUPS // 2
    for pair in range(pairs):
        if then < inner:
            for slot in range(outer * pair // pairs, outer * (pair + 1) // pairs):
                store_choices(slot, outer, inner, then, me_ref, group_ref, lag_ref, other_ref)
        depth = (STEP + (pair == pairs - 1)) * nsub
        both = jnp.dot(
            shifted[:, pl.ds(0, depth)],
            chosen_ref[pl.ds(pair * STEP * nsub, depth), :],
            preferred_element_type=jnp.float32,
        )
        for odd in range(2):
            first = STEP * (GROUPS - 1 - 2 * pair - odd)
            sums_ref[pl.ds(first, rows), :] += both[:, odd * trials : (odd + 1) * trials]
    if then == inner:
        other_ref[...] = sums_ref[pl.ds(0, other_ref.shape[0]), :]


def bands_kernel(widths_ref, early_ref, bands_ref):
    del early_ref
    shape = (bands_ref.shape[0], LANES)
    lag = lax.broadcasted_iota(jnp.int32, shape, 0) - lax.broadcasted_iota(jnp.int32, shape, 1)
    for at in range(widths_ref.shape[0]):
        band = jnp.where((lag >= 0) & (lag < widths_ref[at]), 1.0, 0.0)
        bands_ref[:, pl.ds(at * LANES, LANES)] = band.astype(jnp.bfloat16)


def boxcars_kernel(scale, widths_ref, bands_ref, sums_ref, later_ref, out_ref, values, mixed, tiles, sems):
    trials = sums_ref.shape[1]
    length = sums_ref.shape[0] - REACH
    filters = widths_ref.shape[0]
    whole = length - REACH
    total = jnp.concatenate(
        [
            sums_ref[pl.ds(REACH, whole), :],
            sums_ref[pl.ds(length, REACH), :] + later_ref[pl.ds(0, REACH), :],
            later_ref[pl.ds(REACH, WMAX), :],
        ],
        axis=0,
    )
    for first in range(0, length + WMAX, LANES):
        tile = (total[first : first + LANES] * scale).T
        values[:, pl.ds(first, LANES)] = tile.astype(jnp.bfloat16)
    share = trials // sems.shape[1]
    widths = [jnp.full((1, LANES), widths_ref[at], jnp.int32).astype(jnp.float32) for at in range(filters)]
    shares = [1.0 / jnp.sqrt(width) for width in widths]
    copies = []
    for part in range(length // LANES):
        lanes = pl.ds(part * LANES, LANES)
        for at in range(filters):
            sums = jnp.dot(
                values[:, pl.ds(part * LANES, LANES + WMAX)],
                bands_ref[:, pl.ds(at * LANES, LANES)],
                preferred_element_type=jnp.float32,
            )
            mixed[part, pl.ds(at, trials, stride=filters), :] = sums * shares[at]
        tiles[part] = mixed[part].reshape(trials, filters, LANES)
        for piece in range(sems.shape[1]):
            some = pl.ds(piece * share, share)
            copies.append(
                pltpu.make_async_copy(
                    tiles.at[part, some], out_ref.at[some, :, lanes], sems.at[part, piece]
                )
            )
            copies[-1].start()
    for copy in copies:
        copy.wait()


def call(kernel, out_shape, in_specs, args, scratch=(), flops=0, **options):
    several = isinstance(out_shape, list)
    options.setdefault("out_specs", [VMEM] * len(out_shape) if several else VMEM)
    return pl.pallas_call(
        kernel,
        out_shape=out_shape,
        in_specs=in_specs,
        scratch_shapes=list(scratch),
        compiler_params=pltpu.CompilerParams(vmem_limit_bytes=12 << 20),
        cost_estimate=pl.CostEstimate(flops=flops, bytes_accessed=1 << 20, transcendentals=0),
        **options,
    )(*args)


def one_beam(own, delays, offsets, me, widths, groups, outer, per_sub, scale):
    chans, length = own.shape
    padded, all_subs = offsets.shape
    sub_dev = chans // per_sub
    inner = groups // outer
    filters = widths.shape[0]
    span = length + DCH
    packed = 2 * sub_dev == LANES
    series_shape = (-(-span // 32) * 16, LANES) if packed else (sub_dev, length + LANES)
    steps = 4
    series, fetched = call(
        functools.partial(series_kernel, per_sub, packed),
        [
            jax.ShapeDtypeStruct(series_shape, jnp.bfloat16),
            jax.ShapeDtypeStruct((padded, all_subs), jnp.int32),
        ],
        [HBM, HBM, HBM],
        tuple(pltpu.with_memory_space_constraint(x, pltpu.HBM) for x in (delays[None, :], own, offsets)),
        [
            pltpu.VMEM((1, chans), jnp.int32),
            pltpu.VMEM((chans, length), jnp.bfloat16),
            pltpu.SemaphoreType.DMA,
            pltpu.SemaphoreType.DMA((2 * steps,)),
        ],
    )
    line = [series] + [exchanged(series, "sub", flip * inner) for flip in range(1, outer)]
    split_shape = jax.ShapeDtypeStruct((all_subs, padded), jnp.bfloat16)
    split = call(offsets_kernel, [split_shape, split_shape], [VMEM], (fetched,))
    nsub = outer * sub_dev
    chosen_shape = jax.ShapeDtypeStruct(((GROUPS // 2 * STEP + 1) * nsub, 2 * padded), jnp.bfloat16)
    chosen = call(
        functools.partial(choices_kernel, outer, inner), chosen_shape, [SMEM, VMEM, VMEM], (me, *split)
    )
    joined = call(
        functools.partial(join_packed_kernel if packed else join_kernel, outer),
        jax.ShapeDtypeStruct((span, nsub), jnp.bfloat16),
        [VMEM] * outer + [ANY],
        (*line, chosen),
    )
    blocks = [joined] + [exchanged(joined, "sub", flip) for flip in range(1, inner)]
    scratch = [
        pltpu.VMEM((span + 2 * STEP, nsub), jnp.float32),
        pltpu.VMEM((span + STEP, (STEP + 1) * nsub), jnp.bfloat16),
    ]
    flops = 2 * (span + STEP) * nsub * padded * (OMAX + 2)
    sums_shape = jax.ShapeDtypeStruct((length + REACH, padded), jnp.float32)
    early_shape = jax.ShapeDtypeStruct((REACH + WMAX, padded), jnp.float32)
    before = ()
    for flip in range(inner):
        sums, chosen = call(
            functools.partial(sums_kernel, flip > 0, flip + 1, outer, inner),
            [sums_shape, early_shape if flip == inner - 1 else chosen_shape],
            [SMEM] + [VMEM] * (4 + len(before)),
            (me, blocks[flip], *split, chosen, *before),
            scratch,
            flops,
        )
        before = (sums,)
    early = chosen
    later = passed_back(early, "tm")
    bands = call(
        bands_kernel,
        jax.ShapeDtypeStruct((LANES + WMAX, filters * LANES), jnp.bfloat16),
        [SMEM, ANY],
        (widths, early),
    )
    parts = length // LANES
    pieces = 4
    return call(
        functools.partial(boxcars_kernel, scale),
        jax.ShapeDtypeStruct((padded, filters, length), jnp.float32),
        [SMEM, VMEM, VMEM, VMEM],
        (widths, bands, sums, later),
        [
            pltpu.VMEM((padded, length + WMAX), jnp.bfloat16),
            pltpu.VMEM((parts, padded * filters, LANES), jnp.float32),
            pltpu.VMEM((parts, padded, filters, LANES), jnp.float32),
            pltpu.SemaphoreType.DMA((parts, pieces)),
        ],
        out_specs=HBM,
    )


def per_device(data, delays, offsets, widths):
    beams, chans, length = data.shape
    trials, nsub = offsets.shape
    groups = lax.axis_size("sub")
    outer = 1 << (groups.bit_length() // 2)
    outer = outer if groups % (outer * outer) == 0 else outer // 2
    per_sub = chans // (nsub // groups)
    scale = 1.0 / math.sqrt(chans * groups)
    padded = max(trials, LANES)
    table = jnp.pad(offsets, ((0, padded - trials), (0, 0))) if padded > trials else offsets
    me = lax.axis_index("sub").astype(jnp.int32).reshape(1)
    outs = [
        one_beam(data[beam], delays, table, me, widths, groups, outer, per_sub, scale)[:trials, None]
        for beam in range(beams)
    ]
    return outs[0] if beams == 1 else jnp.concatenate(outs, axis=1)


def solution(mesh):
    placed = (P(None, "sub", "tm"), P("sub"), P("sub", None), P())
    return jax.shard_map(
        per_device,
        mesh=mesh,
        in_specs=placed,
        out_specs=P("sub", None, None, "tm"),
        check_vma=False,
    )
```

```python
import functools
import math

import jax
import jax.numpy as jnp
from jax import lax
from jax.experimental import pallas as pl
from jax.experimental.pallas import tpu as pltpu
from jax.sharding import PartitionSpec as P

WMAX = 128
DCH = 16
OMAX = 96
LANES = 128
STEP = 16
GROUPS = OMAX // STEP
REACH = OMAX + DCH
VMEM = pl.BlockSpec(memory_space=pltpu.VMEM)
SMEM = pl.BlockSpec(memory_space=pltpu.SMEM)
HBM = pl.BlockSpec(memory_space=pltpu.HBM)
ANY = pl.BlockSpec(memory_space=pl.ANY)


def passed_back(value, axis):
    count = lax.axis_size(axis)
    return lax.ppermute(value, axis, [(source, source - 1) for source in range(1, count)])


def exchanged(value, axis, flip):
    count = lax.axis_size(axis)
    return lax.ppermute(value, axis, [(source, source ^ flip) for source in range(count)])


def series_kernel(
    per_sub, packed, delays_ref, data_ref, offsets_ref, series_ref, fetched_ref, delays, held, delays_sem, sems
):
    chans, length = data_ref.shape
    block = min(chans, 256)
    subs = block // per_sub
    wide = length + LANES
    first_copy = pltpu.make_async_copy(delays_ref, delays, delays_sem)
    first_copy.start()
    copies = []
    steps = sems.shape[0] // 2
    for source, target, base in ((data_ref, held, 0), (offsets_ref, fetched_ref, steps)):
        share = source.shape[0] // steps
        for at in range(steps):
            here = pl.ds(at * share, share)
            copies.append(
                pltpu.make_async_copy(source.at[here, :], target.at[here, :], sems.at[base + at])
            )
            copies[-1].start()
    rows = lax.broadcasted_iota(jnp.int32, (DCH * subs, block), 0)
    owner = lax.broadcasted_iota(jnp.int32, (1, block), 1) // per_sub
    blank = jnp.zeros((subs, LANES), jnp.float32)
    first_copy.wait()
    members = [
        jnp.where(rows == delays[:, at * block : (at + 1) * block] * subs + owner, 1.0, 0.0).astype(jnp.bfloat16)
        for at in range(chans // block)
    ]
    for copy in copies[:steps]:
        copy.wait()
    parts = []
    for at, member in enumerate(members):
        picked = jnp.dot(member, held[pl.ds(at * block, block), :], preferred_element_type=jnp.float32)
        total = None
        for delay in range(DCH):
            late = jnp.concatenate([picked[delay * subs : (delay + 1) * subs, :], blank], axis=1)
            late = pltpu.roll(late, DCH - delay, 1)
            total = late if total is None else total + late
        parts.append(total)
    total = jnp.concatenate(parts, axis=0)
    if packed:
        half = series_ref.shape[0]
        both = jnp.concatenate([total, pltpu.roll(total, wide - half, 1)], axis=0)
        for first in range(0, half, LANES):
            count = min(LANES, half - first)
            tile = both[:, first : first + LANES].T
            series_ref[pl.ds(first, count), :] = tile[:count].astype(jnp.bfloat16)
    else:
        series_ref[...] = total.astype(jnp.bfloat16)
    for copy in copies[steps:]:
        copy.wait()


def join_packed_kernel(outer, *refs):
    blocks, joined_ref = refs[:outer], refs[-1]
    half = blocks[0].shape[0]
    rest = joined_ref.shape[0] - half
    lane = lax.broadcasted_iota(jnp.int32, (half, LANES), 1)
    for at in range(outer // 2):
        left = blocks[2 * at][...].astype(jnp.float32)
        right = blocks[2 * at + 1][...].astype(jnp.float32)
        lanes = pl.ds(at * LANES, LANES)
        early = jnp.where(lane < LANES // 2, left, pltpu.roll(right, LANES // 2, 1))
        late = jnp.where(lane < LANES // 2, pltpu.roll(left, LANES // 2, 1), right)
        joined_ref[pl.ds(0, half), lanes] = early.astype(jnp.bfloat16)
        joined_ref[pl.ds(half, rest), lanes] = late[:rest].astype(jnp.bfloat16)


def join_kernel(outer, *refs):
    blocks, joined_ref = refs[:outer], refs[-1]
    subs = blocks[0].shape[0]
    rows = joined_ref.shape[0]
    several = LANES // subs
    for at in range(outer // several):
        for first in range(0, rows, LANES):
            count = min(LANES, rows - first)
            tile = jnp.concatenate(
                [
                    blocks[at * several + slot][:, pl.ds(first, LANES)].astype(jnp.float32)
                    for slot in range(several)
                ],
                axis=0,
            ).T
            joined_ref[pl.ds(first, count), pl.ds(at * LANES, LANES)] = tile[:count].astype(jnp.bfloat16)


def offsets_kernel(offsets_ref, group_ref, lag_ref):
    for at in range(offsets_ref.shape[1] // LANES):
        here = pl.ds(at * LANES, LANES)
        offset = offsets_ref[:, here].astype(jnp.float32).T
        group = jnp.minimum(jnp.floor(offset * (1.0 / STEP)), float(GROUPS - 1))
        group_ref[here, :] = group.astype(jnp.bfloat16)
        lag_ref[here, :] = (offset - float(STEP) * group).astype(jnp.bfloat16)


def one_where(table, value):
    one = jnp.bfloat16(1)
    return jnp.maximum(one - jnp.abs(table - jnp.bfloat16(value)), jnp.bfloat16(0))


def store_choices(slot, outer, inner, flip, me_ref, group_ref, lag_ref, chosen_ref):
    subs = lag_ref.shape[0] // (outer * inner)
    nsub = outer * subs
    row = me_ref[0] // inner
    column = (me_ref[0] % inner) ^ flip
    start = pl.multiple_of(((row ^ slot) * inner + column) * subs, subs)
    groups = group_ref[pl.ds(start, subs), :]
    lags = lag_ref[pl.ds(start, subs), :]
    in_group = [one_where(groups, group) for group in range(GROUPS)]
    for lag in range(STEP + 1):
        at_lag = one_where(lags, lag)
        for group in range(GROUPS - 2 if lag == STEP else 0, GROUPS):
            place = (group // 2 * STEP + lag) * nsub + slot * subs
            chosen_ref[group % 2, pl.ds(place, subs), :] = at_lag * in_group[group]


def choices_kernel(outer, inner, me_ref, group_ref, lag_ref, chosen_ref):
    for slot in range(outer):
        store_choices(slot, outer, inner, 0, me_ref, group_ref, lag_ref, chosen_ref)


def sums_kernel(given, then, outer, inner, me_ref, joined_ref, group_ref, lag_ref, chosen_ref, *refs):
    before_ref, sums_ref, other_ref = refs[:-2] if given else (None, *refs[:-2])
    moving, shifted = refs[-2:]
    span, nsub = joined_ref.shape
    trials = lag_ref.shape[1]
    rows = span + STEP
    blank = jnp.zeros((STEP, nsub), jnp.float32)
    moving[pl.ds(0, STEP), :] = blank
    moving[pl.ds(STEP, span), :] = joined_ref[...].astype(jnp.float32)
    moving[pl.ds(STEP + span, STEP), :] = blank
    for lag in range(STEP + 1):
        shifted[:, pl.ds(lag * nsub, nsub)] = moving[pl.ds(lag, rows), :].astype(jnp.bfloat16)
    if before_ref is None:
        sums_ref[...] = jnp.zeros_like(sums_ref)
    else:
        sums_ref[...] = before_ref[...]
    pairs = GROUPS // 2
    for pair in range(pairs):
        if then < inner:
            for slot in range(outer * pair // pairs, outer * (pair + 1) // pairs):
                store_choices(slot, outer, inner, then, me_ref, group_ref, lag_ref, other_ref)
        depth = (STEP + (pair == pairs - 1)) * nsub
        weights = [chosen_ref[odd, pl.ds(pair * STEP * nsub, depth), :] for odd in range(2)]
        both = jnp.dot(
            shifted[:, pl.ds(0, depth)],
            jnp.concatenate(weights, axis=1),
            preferred_element_type=jnp.float32,
        )
        for odd in range(2):
            first = STEP * (GROUPS - 1 - 2 * pair - odd)
            sums_ref[pl.ds(first, rows), :] += both[:, odd * trials : (odd + 1) * trials]
    if then == inner:
        other_ref[...] = sums_ref[pl.ds(0, other_ref.shape[0]), :]


def bands_kernel(widths_ref, early_ref, bands_ref):
    del early_ref
    shape = (bands_ref.shape[0], LANES)
    lag = lax.broadcasted_iota(jnp.int32, shape, 0) - lax.broadcasted_iota(jnp.int32, shape, 1)
    for at in range(widths_ref.shape[0]):
        band = jnp.where((lag >= 0) & (lag < widths_ref[at]), 1.0, 0.0)
        bands_ref[:, pl.ds(at * LANES, LANES)] = band.astype(jnp.bfloat16)


def boxcars_kernel(scale, widths_ref, bands_ref, sums_ref, later_ref, out_ref, values, mixed, tiles, sems):
    trials = sums_ref.shape[1]
    length = sums_ref.shape[0] - REACH
    filters = widths_ref.shape[0]
    whole = length - REACH
    total = jnp.concatenate(
        [
            sums_ref[pl.ds(REACH, whole), :],
            sums_ref[pl.ds(length, REACH), :] + later_ref[pl.ds(0, REACH), :],
            later_ref[pl.ds(REACH, WMAX), :],
        ],
        axis=0,
    )
    for first in range(0, length + WMAX, LANES):
        tile = (total[first : first + LANES] * scale).T
        values[:, pl.ds(first, LANES)] = tile.astype(jnp.bfloat16)
    share = trials // sems.shape[1]
    widths = [jnp.full((1, LANES), widths_ref[at], jnp.int32).astype(jnp.float32) for at in range(filters)]
    shares = [1.0 / jnp.sqrt(width) for width in widths]
    copies = []
    for part in range(length // LANES):
        lanes = pl.ds(part * LANES, LANES)
        for at in range(filters):
            sums = jnp.dot(
                values[:, pl.ds(part * LANES, LANES + WMAX)],
                bands_ref[:, pl.ds(at * LANES, LANES)],
                preferred_element_type=jnp.float32,
            )
            mixed[part, pl.ds(at, trials, stride=filters), :] = sums * shares[at]
        tiles[part] = mixed[part].reshape(trials, filters, LANES)
        for piece in range(sems.shape[1]):
            some = pl.ds(piece * share, share)
            copies.append(
                pltpu.make_async_copy(
                    tiles.at[part, some], out_ref.at[some, :, lanes], sems.at[part, piece]
                )
            )
            copies[-1].start()
    for copy in copies:
        copy.wait()


def call(kernel, out_shape, in_specs, args, scratch=(), flops=0, **options):
    several = isinstance(out_shape, list)
    options.setdefault("out_specs", [VMEM] * len(out_shape) if several else VMEM)
    return pl.pallas_call(
        kernel,
        out_shape=out_shape,
        in_specs=in_specs,
        scratch_shapes=list(scratch),
        compiler_params=pltpu.CompilerParams(vmem_limit_bytes=12 << 20),
        cost_estimate=pl.CostEstimate(flops=flops, bytes_accessed=1 << 20, transcendentals=0),
        **options,
    )(*args)


def one_beam(own, delays, offsets, me, widths, groups, outer, per_sub, scale):
    chans, length = own.shape
    padded, all_subs = offsets.shape
    sub_dev = chans // per_sub
    inner = groups // outer
    filters = widths.shape[0]
    span = length + DCH
    packed = 2 * sub_dev == LANES
    series_shape = (-(-span // 32) * 16, LANES) if packed else (sub_dev, length + LANES)
    steps = 4
    series, fetched = call(
        functools.partial(series_kernel, per_sub, packed),
        [
            jax.ShapeDtypeStruct(series_shape, jnp.bfloat16),
            jax.ShapeDtypeStruct((padded, all_subs), jnp.int32),
        ],
        [HBM, HBM, HBM],
        tuple(pltpu.with_memory_space_constraint(x, pltpu.HBM) for x in (delays[None, :], own, offsets)),
        [
            pltpu.VMEM((1, chans), jnp.int32),
            pltpu.VMEM((chans, length), jnp.bfloat16),
            pltpu.SemaphoreType.DMA,
            pltpu.SemaphoreType.DMA((2 * steps,)),
        ],
    )
    line = [series] + [exchanged(series, "sub", flip * inner) for flip in range(1, outer)]
    split_shape = jax.ShapeDtypeStruct((all_subs, padded), jnp.bfloat16)
    split = call(offsets_kernel, [split_shape, split_shape], [VMEM], (fetched,))
    nsub = outer * sub_dev
    chosen_shape = jax.ShapeDtypeStruct((2, (GROUPS // 2 * STEP + 1) * nsub, padded), jnp.bfloat16)
    chosen = call(
        functools.partial(choices_kernel, outer, inner), chosen_shape, [SMEM, VMEM, VMEM], (me, *split)
    )
    joined = call(
        functools.partial(join_packed_kernel if packed else join_kernel, outer),
        jax.ShapeDtypeStruct((span, nsub), jnp.bfloat16),
        [VMEM] * outer + [ANY],
        (*line, chosen),
    )
    blocks = [joined] + [exchanged(joined, "sub", flip) for flip in range(1, inner)]
    scratch = [
        pltpu.VMEM((span + 2 * STEP, nsub), jnp.float32),
        pltpu.VMEM((span + STEP, (STEP + 1) * nsub), jnp.bfloat16),
    ]
    flops = 2 * (span + STEP) * nsub * padded * (OMAX + 2)
    sums_shape = jax.ShapeDtypeStruct((length + REACH, padded), jnp.float32)
    early_shape = jax.ShapeDtypeStruct((REACH + WMAX, padded), jnp.float32)
    before = ()
    for flip in range(inner):
        sums, chosen = call(
            functools.partial(sums_kernel, flip > 0, flip + 1, outer, inner),
            [sums_shape, early_shape if flip == inner - 1 else chosen_shape],
            [SMEM] + [VMEM] * (4 + len(before)),
            (me, blocks[flip], *split, chosen, *before),
            scratch,
            flops,
        )
        before = (sums,)
    early = chosen
    later = passed_back(early, "tm")
    bands = call(
        bands_kernel,
        jax.ShapeDtypeStruct((LANES + WMAX, filters * LANES), jnp.bfloat16),
        [SMEM, ANY],
        (widths, early),
    )
    parts = length // LANES
    pieces = 4
    return call(
        functools.partial(boxcars_kernel, scale),
        jax.ShapeDtypeStruct((padded, filters, length), jnp.float32),
        [SMEM, VMEM, VMEM, VMEM],
        (widths, bands, sums, later),
        [
            pltpu.VMEM((padded, length + WMAX), jnp.bfloat16),
            pltpu.VMEM((parts, padded * filters, LANES), jnp.float32),
            pltpu.VMEM((parts, padded, filters, LANES), jnp.float32),
            pltpu.SemaphoreType.DMA((parts, pieces)),
        ],
        out_specs=HBM,
    )


def per_device(data, delays, offsets, widths):
    beams, chans, length = data.shape
    trials, nsub = offsets.shape
    groups = lax.axis_size("sub")
    outer = 1 << (groups.bit_length() // 2)
    outer = outer if groups % (outer * outer) == 0 else outer // 2
    per_sub = chans // (nsub // groups)
    scale = 1.0 / math.sqrt(chans * groups)
    padded = max(trials, LANES)
    table = jnp.pad(offsets, ((0, padded - trials), (0, 0))) if padded > trials else offsets
    me = lax.axis_index("sub").astype(jnp.int32).reshape(1)
    outs = [
        one_beam(data[beam], delays, table, me, widths, groups, outer, per_sub, scale)[:trials, None]
        for beam in range(beams)
    ]
    return outs[0] if beams == 1 else jnp.concatenate(outs, axis=1)


def solution(mesh):
    placed = (P(None, "sub", "tm"), P("sub"), P("sub", None), P())
    return jax.shard_map(
        per_device,
        mesh=mesh,
        in_specs=placed,
        out_specs=P("sub", None, None, "tm"),
        check_vma=False,
    )
```

```python
import functools
import math

import jax
import jax.numpy as jnp
from jax import lax
from jax.experimental import pallas as pl
from jax.experimental.pallas import tpu as pltpu
from jax.sharding import PartitionSpec as P

WMAX = 128
DCH = 16
OMAX = 96
LANES = 128
STEP = 16
GROUPS = OMAX // STEP
REACH = OMAX + DCH
VMEM = pl.BlockSpec(memory_space=pltpu.VMEM)
SMEM = pl.BlockSpec(memory_space=pltpu.SMEM)
HBM = pl.BlockSpec(memory_space=pltpu.HBM)
ANY = pl.BlockSpec(memory_space=pl.ANY)


def passed_back(value, axis):
    count = lax.axis_size(axis)
    return lax.ppermute(value, axis, [(source, source - 1) for source in range(1, count)])


def exchanged(value, axis, flip):
    count = lax.axis_size(axis)
    return lax.ppermute(value, axis, [(source, source ^ flip) for source in range(count)])


def series_kernel(
    per_sub, packed, delays_ref, data_ref, offsets_ref, series_ref, fetched_ref, delays, held, delays_sem, sems
):
    chans, length = data_ref.shape
    block = min(chans, 256)
    subs = block // per_sub
    wide = length + LANES
    first_copy = pltpu.make_async_copy(delays_ref, delays, delays_sem)
    first_copy.start()
    copies = []
    steps = sems.shape[0] // 2
    for source, target, base in ((data_ref, held, 0), (offsets_ref, fetched_ref, steps)):
        share = source.shape[0] // steps
        for at in range(steps):
            here = pl.ds(at * share, share)
            copies.append(
                pltpu.make_async_copy(source.at[here, :], target.at[here, :], sems.at[base + at])
            )
            copies[-1].start()
    rows = lax.broadcasted_iota(jnp.int32, (DCH * subs, block), 0)
    owner = lax.broadcasted_iota(jnp.int32, (1, block), 1) // per_sub
    blank = jnp.zeros((subs, LANES), jnp.float32)
    first_copy.wait()
    members = [
        jnp.where(rows == delays[:, at * block : (at + 1) * block] * subs + owner, 1.0, 0.0).astype(jnp.bfloat16)
        for at in range(chans // block)
    ]
    for copy in copies[:steps]:
        copy.wait()
    parts = []
    for at, member in enumerate(members):
        picked = jnp.dot(member, held[pl.ds(at * block, block), :], preferred_element_type=jnp.float32)
        total = None
        for delay in range(DCH):
            late = jnp.concatenate([picked[delay * subs : (delay + 1) * subs, :], blank], axis=1)
            late = pltpu.roll(late, DCH - delay, 1)
            total = late if total is None else total + late
        parts.append(total)
    total = jnp.concatenate(parts, axis=0)
    if packed:
        half = series_ref.shape[0]
        both = jnp.concatenate([total, pltpu.roll(total, wide - half, 1)], axis=0)
        for first in range(0, half, LANES):
            count = min(LANES, half - first)
            tile = both[:, first : first + LANES].T
            series_ref[pl.ds(first, count), :] = tile[:count].astype(jnp.bfloat16)
    else:
        series_ref[...] = total.astype(jnp.bfloat16)
    for copy in copies[steps:]:
        copy.wait()


def join_packed_kernel(outer, *refs):
    blocks, joined_ref = refs[:outer], refs[-1]
    half = blocks[0].shape[0]
    rest = joined_ref.shape[0] - half
    lane = lax.broadcasted_iota(jnp.int32, (half, LANES), 1)
    for at in range(outer // 2):
        left = blocks[2 * at][...].astype(jnp.float32)
        right = blocks[2 * at + 1][...].astype(jnp.float32)
        lanes = pl.ds(at * LANES, LANES)
        early = jnp.where(lane < LANES // 2, left, pltpu.roll(right, LANES // 2, 1))
        late = jnp.where(lane < LANES // 2, pltpu.roll(left, LANES // 2, 1), right)
        joined_ref[pl.ds(0, half), lanes] = early.astype(jnp.bfloat16)
        joined_ref[pl.ds(half, rest), lanes] = late[:rest].astype(jnp.bfloat16)


def join_kernel(outer, *refs):
    blocks, joined_ref = refs[:outer], refs[-1]
    subs = blocks[0].shape[0]
    rows = joined_ref.shape[0]
    several = LANES // subs
    for at in range(outer // several):
        for first in range(0, rows, LANES):
            count = min(LANES, rows - first)
            tile = jnp.concatenate(
                [
                    blocks[at * several + slot][:, pl.ds(first, LANES)].astype(jnp.float32)
                    for slot in range(several)
                ],
                axis=0,
            ).T
            joined_ref[pl.ds(first, count), pl.ds(at * LANES, LANES)] = tile[:count].astype(jnp.bfloat16)


def offsets_kernel(offsets_ref, group_ref, lag_ref):
    for at in range(offsets_ref.shape[1] // LANES):
        here = pl.ds(at * LANES, LANES)
        offset = offsets_ref[:, here].astype(jnp.float32).T
        group = jnp.minimum(jnp.floor(offset * (1.0 / STEP)), float(GROUPS - 1))
        group_ref[here, :] = group
        lag_ref[here, :] = offset - float(STEP) * group


def choices_kernel(outer, inner, flip, me_ref, group_ref, lag_ref, *refs):
    chosen_ref = refs[-1]
    subs = lag_ref.shape[0] // (outer * inner)
    nsub = outer * subs
    row = me_ref[0] // inner
    column = (me_ref[0] % inner) ^ flip
    for slot in range(outer):
        start = pl.multiple_of(((row ^ slot) * inner + column) * subs, subs)
        for first in range(0, subs, 16):
            here = pl.ds(pl.multiple_of(start + first, 16), 16)
            groups = group_ref[here, :]
            lags = lag_ref[here, :]
            in_group = [jnp.where(groups == float(group), 1.0, 0.0) for group in range(GROUPS)]
            for lag in range(STEP + 1):
                at_lag = jnp.where(lags == float(lag), 1.0, 0.0)
                for group in range(GROUPS - 2 if lag == STEP else 0, GROUPS):
                    place = (group // 2 * STEP + lag) * nsub + slot * subs + first
                    chosen_ref[group % 2, pl.ds(place, 16), :] = (at_lag * in_group[group]).astype(
                        jnp.bfloat16
                    )


def sums_kernel(given, joined_ref, chosen_ref, *refs):
    before_ref, sums_ref, *early_ref = refs[:-2] if given else (None, *refs[:-2])
    moving, shifted = refs[-2:]
    span, nsub = joined_ref.shape
    trials = chosen_ref.shape[2]
    rows = span + STEP
    blank = jnp.zeros((STEP, nsub), jnp.float32)
    moving[pl.ds(0, STEP), :] = blank
    moving[pl.ds(STEP, span), :] = joined_ref[...].astype(jnp.float32)
    moving[pl.ds(STEP + span, STEP), :] = blank
    for lag in range(STEP + 1):
        shifted[:, pl.ds(lag * nsub, nsub)] = moving[pl.ds(lag, rows), :].astype(jnp.bfloat16)
    if before_ref is None:
        sums_ref[...] = jnp.zeros_like(sums_ref)
    else:
        sums_ref[...] = before_ref[...]
    pairs = GROUPS // 2
    for pair in range(pairs):
        depth = (STEP + (pair == pairs - 1)) * nsub
        weights = [chosen_ref[odd, pl.ds(pair * STEP * nsub, depth), :] for odd in range(2)]
        both = jnp.dot(
            shifted[:, pl.ds(0, depth)],
            jnp.concatenate(weights, axis=1),
            preferred_element_type=jnp.float32,
        )
        for odd in range(2):
            first = STEP * (GROUPS - 1 - 2 * pair - odd)
            sums_ref[pl.ds(first, rows), :] += both[:, odd * trials : (odd + 1) * trials]
    for ref in early_ref:
        ref[...] = sums_ref[pl.ds(0, ref.shape[0]), :]


def bands_kernel(widths_ref, early_ref, bands_ref):
    del early_ref
    shape = (bands_ref.shape[0], LANES)
    lag = lax.broadcasted_iota(jnp.int32, shape, 0) - lax.broadcasted_iota(jnp.int32, shape, 1)
    for at in range(widths_ref.shape[0]):
        band = jnp.where((lag >= 0) & (lag < widths_ref[at]), 1.0, 0.0)
        bands_ref[:, pl.ds(at * LANES, LANES)] = band.astype(jnp.bfloat16)


def boxcars_kernel(scale, widths_ref, bands_ref, sums_ref, later_ref, out_ref, values, mixed, tiles, sems):
    trials = sums_ref.shape[1]
    length = sums_ref.shape[0] - REACH
    filters = widths_ref.shape[0]
    whole = length - REACH
    total = jnp.concatenate(
        [
            sums_ref[pl.ds(REACH, whole), :],
            sums_ref[pl.ds(length, REACH), :] + later_ref[pl.ds(0, REACH), :],
            later_ref[pl.ds(REACH, WMAX), :],
        ],
        axis=0,
    )
    for first in range(0, length + WMAX, LANES):
        tile = (total[first : first + LANES] * scale).T
        values[:, pl.ds(first, LANES)] = tile.astype(jnp.bfloat16)
    share = trials // sems.shape[1]
    widths = [jnp.full((1, LANES), widths_ref[at], jnp.int32).astype(jnp.float32) for at in range(filters)]
    shares = [1.0 / jnp.sqrt(width) for width in widths]
    copies = []
    for part in range(length // LANES):
        lanes = pl.ds(part * LANES, LANES)
        for at in range(filters):
            sums = jnp.dot(
                values[:, pl.ds(part * LANES, LANES + WMAX)],
                bands_ref[:, pl.ds(at * LANES, LANES)],
                preferred_element_type=jnp.float32,
            )
            mixed[part, pl.ds(at, trials, stride=filters), :] = sums * shares[at]
        tiles[part] = mixed[part].reshape(trials, filters, LANES)
        for piece in range(sems.shape[1]):
            some = pl.ds(piece * share, share)
            copies.append(
                pltpu.make_async_copy(
                    tiles.at[part, some], out_ref.at[some, :, lanes], sems.at[part, piece]
                )
            )
            copies[-1].start()
    for copy in copies:
        copy.wait()


def call(kernel, out_shape, in_specs, args, scratch=(), flops=0, **options):
    several = isinstance(out_shape, list)
    options.setdefault("out_specs", [VMEM] * len(out_shape) if several else VMEM)
    return pl.pallas_call(
        kernel,
        out_shape=out_shape,
        in_specs=in_specs,
        scratch_shapes=list(scratch),
        compiler_params=pltpu.CompilerParams(vmem_limit_bytes=12 << 20),
        cost_estimate=pl.CostEstimate(flops=flops, bytes_accessed=1 << 20, transcendentals=0),
        **options,
    )(*args)


def one_beam(own, delays, offsets, me, widths, groups, outer, per_sub, scale):
    chans, length = own.shape
    padded, all_subs = offsets.shape
    sub_dev = chans // per_sub
    inner = groups // outer
    filters = widths.shape[0]
    span = length + DCH
    packed = 2 * sub_dev == LANES
    series_shape = (-(-span // 32) * 16, LANES) if packed else (sub_dev, length + LANES)
    steps = 4
    series, fetched = call(
        functools.partial(series_kernel, per_sub, packed),
        [
            jax.ShapeDtypeStruct(series_shape, jnp.bfloat16),
            jax.ShapeDtypeStruct((padded, all_subs), jnp.int32),
        ],
        [HBM, HBM, HBM],
        tuple(pltpu.with_memory_space_constraint(x, pltpu.HBM) for x in (delays[None, :], own, offsets)),
        [
            pltpu.VMEM((1, chans), jnp.int32),
            pltpu.VMEM((chans, length), jnp.bfloat16),
            pltpu.SemaphoreType.DMA,
            pltpu.SemaphoreType.DMA((2 * steps,)),
        ],
    )
    line = [series] + [exchanged(series, "sub", flip * inner) for flip in range(1, outer)]
    split_shape = jax.ShapeDtypeStruct((all_subs, padded), jnp.float32)
    split = call(offsets_kernel, [split_shape, split_shape], [VMEM], (fetched,))
    nsub = outer * sub_dev
    chosen_shape = jax.ShapeDtypeStruct((2, (GROUPS // 2 * STEP + 1) * nsub, padded), jnp.bfloat16)

    def choices_of(flip, *after):
        return call(
            functools.partial(choices_kernel, outer, inner, flip),
            chosen_shape,
            [SMEM, VMEM, VMEM] + [ANY] * len(after),
            (me, *split, *after),
        )

    soon = [choices_of(flip) for flip in range(inner - 1)]
    joined = call(
        functools.partial(join_packed_kernel if packed else join_kernel, outer),
        jax.ShapeDtypeStruct((span, nsub), jnp.bfloat16),
        [VMEM] * outer + [ANY] * len(soon),
        (*line, *soon),
    )
    choices = soon + [choices_of(inner - 1, joined)]
    blocks = [joined] + [exchanged(joined, "sub", flip) for flip in range(1, inner)]
    scratch = [
        pltpu.VMEM((span + 2 * STEP, nsub), jnp.float32),
        pltpu.VMEM((span + STEP, (STEP + 1) * nsub), jnp.bfloat16),
    ]
    flops = 2 * (span + STEP) * nsub * padded * (OMAX + 2)
    sums_shape = jax.ShapeDtypeStruct((length + REACH, padded), jnp.float32)
    early_shape = jax.ShapeDtypeStruct((REACH + WMAX, padded), jnp.float32)
    sums = []
    for flip in range(inner):
        sums = call(
            functools.partial(sums_kernel, flip > 0),
            [sums_shape, early_shape] if flip == inner - 1 else [sums_shape],
            [VMEM] * (2 + len(sums)),
            (blocks[flip], choices[flip], *sums),
            scratch,
            flops,
        )
    sums, early = sums
    later = passed_back(early, "tm")
    bands = call(
        bands_kernel,
        jax.ShapeDtypeStruct((LANES + WMAX, filters * LANES), jnp.bfloat16),
        [SMEM, ANY],
        (widths, early),
    )
    parts = length // LANES
    pieces = 4
    return call(
        functools.partial(boxcars_kernel, scale),
        jax.ShapeDtypeStruct((padded, filters, length), jnp.float32),
        [SMEM, VMEM, VMEM, VMEM],
        (widths, bands, sums, later),
        [
            pltpu.VMEM((padded, length + WMAX), jnp.bfloat16),
            pltpu.VMEM((parts, padded * filters, LANES), jnp.float32),
            pltpu.VMEM((parts, padded, filters, LANES), jnp.float32),
            pltpu.SemaphoreType.DMA((parts, pieces)),
        ],
        out_specs=HBM,
    )


def per_device(data, delays, offsets, widths):
    beams, chans, length = data.shape
    trials, nsub = offsets.shape
    groups = lax.axis_size("sub")
    outer = 1 << (groups.bit_length() // 2)
    outer = outer if groups % (outer * outer) == 0 else outer // 2
    per_sub = chans // (nsub // groups)
    scale = 1.0 / math.sqrt(chans * groups)
    padded = max(trials, LANES)
    table = jnp.pad(offsets, ((0, padded - trials), (0, 0))) if padded > trials else offsets
    me = lax.axis_index("sub").astype(jnp.int32).reshape(1)
    outs = [
        one_beam(data[beam], delays, table, me, widths, groups, outer, per_sub, scale)[:trials, None]
        for beam in range(beams)
    ]
    return outs[0] if beams == 1 else jnp.concatenate(outs, axis=1)


def solution(mesh):
    placed = (P(None, "sub", "tm"), P("sub"), P("sub", None), P())
    return jax.shard_map(
        per_device,
        mesh=mesh,
        in_specs=placed,
        out_specs=P("sub", None, None, "tm"),
        check_vma=False,
    )
```

```python
import functools
import math

import jax
import jax.numpy as jnp
from jax import lax
from jax.experimental import pallas as pl
from jax.experimental.pallas import tpu as pltpu
from jax.sharding import PartitionSpec as P

WMAX = 128
DCH = 16
OMAX = 96
LANES = 128
STEP = 16
GROUPS = OMAX // STEP
REACH = OMAX + DCH
VMEM = pl.BlockSpec(memory_space=pltpu.VMEM)
SMEM = pl.BlockSpec(memory_space=pltpu.SMEM)
HBM = pl.BlockSpec(memory_space=pltpu.HBM)
ANY = pl.BlockSpec(memory_space=pl.ANY)


def passed_back(value, axis):
    count = lax.axis_size(axis)
    return lax.ppermute(value, axis, [(source, source - 1) for source in range(1, count)])


def exchanged(value, axis, flip):
    count = lax.axis_size(axis)
    return lax.ppermute(value, axis, [(source, source ^ flip) for source in range(count)])


def series_kernel(
    per_sub, packed, delays_ref, data_ref, offsets_ref, series_ref, fetched_ref, delays, held, delays_sem, sems
):
    chans, length = data_ref.shape
    block = min(chans, 256)
    subs = block // per_sub
    wide = length + LANES
    first_copy = pltpu.make_async_copy(delays_ref, delays, delays_sem)
    first_copy.start()
    copies = []
    steps = sems.shape[0] // 2
    for source, target, base in ((data_ref, held, 0), (offsets_ref, fetched_ref, steps)):
        share = source.shape[0] // steps
        for at in range(steps):
            here = pl.ds(at * share, share)
            copies.append(
                pltpu.make_async_copy(source.at[here, :], target.at[here, :], sems.at[base + at])
            )
            copies[-1].start()
    rows = lax.broadcasted_iota(jnp.int32, (DCH * subs, block), 0)
    owner = lax.broadcasted_iota(jnp.int32, (1, block), 1) // per_sub
    blank = jnp.zeros((subs, LANES), jnp.float32)
    first_copy.wait()
    members = [
        jnp.where(rows == delays[:, at * block : (at + 1) * block] * subs + owner, 1.0, 0.0).astype(jnp.bfloat16)
        for at in range(chans // block)
    ]
    for copy in copies[:steps]:
        copy.wait()
    parts = []
    for at, member in enumerate(members):
        picked = jnp.dot(member, held[pl.ds(at * block, block), :], preferred_element_type=jnp.float32)
        total = None
        for delay in range(DCH):
            late = jnp.concatenate([picked[delay * subs : (delay + 1) * subs, :], blank], axis=1)
            late = pltpu.roll(late, DCH - delay, 1)
            total = late if total is None else total + late
        parts.append(total)
    total = jnp.concatenate(parts, axis=0)
    if packed:
        half = series_ref.shape[0]
        both = jnp.concatenate([total, pltpu.roll(total, wide - half, 1)], axis=0)
        for first in range(0, half, LANES):
            count = min(LANES, half - first)
            tile = both[:, first : first + LANES].T
            series_ref[pl.ds(first, count), :] = tile[:count].astype(jnp.bfloat16)
    else:
        series_ref[...] = total.astype(jnp.bfloat16)
    for copy in copies[steps:]:
        copy.wait()


def join_packed_kernel(outer, *refs):
    blocks, joined_ref = refs[:outer], refs[-1]
    half = blocks[0].shape[0]
    rest = joined_ref.shape[0] - half
    lane = lax.broadcasted_iota(jnp.int32, (half, LANES), 1)
    for at in range(outer // 2):
        left = blocks[2 * at][...].astype(jnp.float32)
        right = blocks[2 * at + 1][...].astype(jnp.float32)
        lanes = pl.ds(at * LANES, LANES)
        early = jnp.where(lane < LANES // 2, left, pltpu.roll(right, LANES // 2, 1))
        late = jnp.where(lane < LANES // 2, pltpu.roll(left, LANES // 2, 1), right)
        joined_ref[pl.ds(0, half), lanes] = early.astype(jnp.bfloat16)
        joined_ref[pl.ds(half, rest), lanes] = late[:rest].astype(jnp.bfloat16)


def join_kernel(outer, *refs):
    blocks, joined_ref = refs[:outer], refs[-1]
    subs = blocks[0].shape[0]
    rows = joined_ref.shape[0]
    several = LANES // subs
    for at in range(outer // several):
        for first in range(0, rows, LANES):
            count = min(LANES, rows - first)
            tile = jnp.concatenate(
                [
                    blocks[at * several + slot][:, pl.ds(first, LANES)].astype(jnp.float32)
                    for slot in range(several)
                ],
                axis=0,
            ).T
            joined_ref[pl.ds(first, count), pl.ds(at * LANES, LANES)] = tile[:count].astype(jnp.bfloat16)


def offsets_kernel(offsets_ref, table_ref):
    for at in range(offsets_ref.shape[1] // LANES):
        here = pl.ds(at * LANES, LANES)
        table_ref[here, :] = offsets_ref[:, here].astype(jnp.float32).T


def slot_start(slot, flip, outer, inner, subs, me):
    return pl.multiple_of((((me // inner) ^ slot) * inner + ((me % inner) ^ flip)) * subs, subs)


def choices_kernel(outer, inner, me_ref, table_ref, chosen_ref):
    subs = table_ref.shape[0] // (outer * inner)
    nsub = outer * subs
    for slot in range(outer):
        start = slot_start(slot, 0, outer, inner, subs, me_ref[0])
        for first in range(0, subs, 16):
            offset = table_ref[pl.ds(pl.multiple_of(start + first, 16), 16), :]
            groups = jnp.minimum(jnp.floor(offset * (1.0 / STEP)), float(GROUPS - 1))
            lags = offset - float(STEP) * groups
            in_group = [jnp.where(groups == float(group), 1.0, 0.0) for group in range(GROUPS)]
            for lag in range(STEP + 1):
                at_lag = jnp.where(lags == float(lag), 1.0, 0.0)
                for group in range(GROUPS - 2 if lag == STEP else 0, GROUPS):
                    place = (group // 2 * STEP + lag) * nsub + slot * subs + first
                    chosen_ref[group % 2, pl.ds(place, 16), :] = (at_lag * in_group[group]).astype(
                        jnp.bfloat16
                    )


def shift_series(joined_ref, moving, shifted):
    span, nsub = joined_ref.shape
    blank = jnp.zeros((STEP, nsub), jnp.float32)
    moving[pl.ds(0, STEP), :] = blank
    moving[pl.ds(STEP, span), :] = joined_ref[...].astype(jnp.float32)
    moving[pl.ds(STEP + span, STEP), :] = blank
    for lag in range(STEP + 1):
        shifted[:, pl.ds(lag * nsub, nsub)] = moving[pl.ds(lag, span + STEP), :].astype(jnp.bfloat16)


def add_pair(total, pair, both):
    rows, trials = both.shape[0], both.shape[1] // 2
    for odd in range(2):
        first = STEP * (GROUPS - 1 - 2 * pair - odd)
        total[pl.ds(first, rows), :] += both[:, odd * trials : (odd + 1) * trials]


def first_sums_kernel(joined_ref, chosen_ref, sums_ref, moving, shifted):
    nsub = joined_ref.shape[1]
    shift_series(joined_ref, moving, shifted)
    sums_ref[...] = jnp.zeros_like(sums_ref)
    for pair in range(GROUPS // 2):
        depth = (STEP + (pair == GROUPS // 2 - 1)) * nsub
        weights = [chosen_ref[odd, pl.ds(pair * STEP * nsub, depth), :] for odd in range(2)]
        add_pair(
            sums_ref,
            pair,
            jnp.dot(
                shifted[:, pl.ds(0, depth)],
                jnp.concatenate(weights, axis=1),
                preferred_element_type=jnp.float32,
            ),
        )


def more_sums_kernel(outer, inner, flip, me_ref, joined_ref, table_ref, before_ref, sums_ref, *refs):
    *early_ref, moving, shifted, total, table = refs[: -(GROUPS // 2)]
    weights = refs[-(GROUPS // 2) :]
    nsub = joined_ref.shape[1]
    subs = nsub // outer
    trials = table_ref.shape[1]
    for slot in range(outer):
        start = slot_start(slot, flip, outer, inner, subs, me_ref[0])
        table[pl.ds(slot * subs, subs), :] = table_ref[pl.ds(start, subs), :]
    total[...] = before_ref[...]
    shift_series(joined_ref, moving, shifted)

    def make(pair):
        for first in range(0, nsub, 16):
            offset = table[pl.ds(first, 16), :]
            for lag in range(weights[pair].shape[0] // nsub):
                for odd in range(2):
                    wanted = float(STEP * (2 * pair + odd) + lag) if lag < STEP or odd else -1.0
                    weights[pair][pl.ds(lag * nsub + first, 16), pl.ds(odd * trials, trials)] = jnp.where(
                        offset == wanted, 1.0, 0.0
                    ).astype(jnp.bfloat16)

    make(0)
    for pair in range(GROUPS // 2):
        if pair + 1 < GROUPS // 2:
            make(pair + 1)
        both = jnp.dot(
            shifted[:, pl.ds(0, weights[pair].shape[0])],
            weights[pair][...],
            preferred_element_type=jnp.float32,
        )
        add_pair(total, pair, both)
    sums_ref[...] = total[...]
    for ref in early_ref:
        ref[...] = total[pl.ds(0, ref.shape[0]), :]


def bands_kernel(widths_ref, early_ref, bands_ref):
    del early_ref
    shape = (bands_ref.shape[0], LANES)
    lag = lax.broadcasted_iota(jnp.int32, shape, 0) - lax.broadcasted_iota(jnp.int32, shape, 1)
    for at in range(widths_ref.shape[0]):
        band = jnp.where((lag >= 0) & (lag < widths_ref[at]), 1.0, 0.0)
        bands_ref[:, pl.ds(at * LANES, LANES)] = band.astype(jnp.bfloat16)


def boxcars_kernel(scale, widths_ref, bands_ref, sums_ref, later_ref, out_ref, values, mixed, tiles, sems):
    trials = sums_ref.shape[1]
    length = sums_ref.shape[0] - REACH
    filters = widths_ref.shape[0]
    whole = length - REACH
    total = jnp.concatenate(
        [
            sums_ref[pl.ds(REACH, whole), :],
            sums_ref[pl.ds(length, REACH), :] + later_ref[pl.ds(0, REACH), :],
            later_ref[pl.ds(REACH, WMAX), :],
        ],
        axis=0,
    )
    for first in range(0, length + WMAX, LANES):
        tile = (total[first : first + LANES] * scale).T
        values[:, pl.ds(first, LANES)] = tile.astype(jnp.bfloat16)
    share = trials // sems.shape[1]
    widths = [jnp.full((1, LANES), widths_ref[at], jnp.int32).astype(jnp.float32) for at in range(filters)]
    shares = [1.0 / jnp.sqrt(width) for width in widths]
    copies = []
    for part in range(length // LANES):
        lanes = pl.ds(part * LANES, LANES)
        for at in range(filters):
            sums = jnp.dot(
                values[:, pl.ds(part * LANES, LANES + WMAX)],
                bands_ref[:, pl.ds(at * LANES, LANES)],
                preferred_element_type=jnp.float32,
            )
            mixed[part, pl.ds(at, trials, stride=filters), :] = sums * shares[at]
        tiles[part] = mixed[part].reshape(trials, filters, LANES)
        for piece in range(sems.shape[1]):
            some = pl.ds(piece * share, share)
            copies.append(
                pltpu.make_async_copy(
                    tiles.at[part, some], out_ref.at[some, :, lanes], sems.at[part, piece]
                )
            )
            copies[-1].start()
    for copy in copies:
        copy.wait()


def call(kernel, out_shape, in_specs, args, scratch=(), flops=0, **options):
    several = isinstance(out_shape, list)
    options.setdefault("out_specs", [VMEM] * len(out_shape) if several else VMEM)
    return pl.pallas_call(
        kernel,
        out_shape=out_shape,
        in_specs=in_specs,
        scratch_shapes=list(scratch),
        compiler_params=pltpu.CompilerParams(vmem_limit_bytes=16 << 20),
        cost_estimate=pl.CostEstimate(flops=flops, bytes_accessed=1 << 20, transcendentals=0),
        **options,
    )(*args)


def one_beam(own, delays, offsets, me, widths, groups, outer, per_sub, scale):
    chans, length = own.shape
    padded, all_subs = offsets.shape
    sub_dev = chans // per_sub
    inner = groups // outer
    filters = widths.shape[0]
    span = length + DCH
    packed = 2 * sub_dev == LANES
    series_shape = (-(-span // 32) * 16, LANES) if packed else (sub_dev, length + LANES)
    steps = 4
    series, fetched = call(
        functools.partial(series_kernel, per_sub, packed),
        [
            jax.ShapeDtypeStruct(series_shape, jnp.bfloat16),
            jax.ShapeDtypeStruct((padded, all_subs), jnp.int32),
        ],
        [HBM, HBM, HBM],
        tuple(pltpu.with_memory_space_constraint(x, pltpu.HBM) for x in (delays[None, :], own, offsets)),
        [
            pltpu.VMEM((1, chans), jnp.int32),
            pltpu.VMEM((chans, length), jnp.bfloat16),
            pltpu.SemaphoreType.DMA,
            pltpu.SemaphoreType.DMA((2 * steps,)),
        ],
    )
    line = [series] + [exchanged(series, "sub", flip * inner) for flip in range(1, outer)]
    nsub = outer * sub_dev
    table = call(offsets_kernel, jax.ShapeDtypeStruct((all_subs, padded), jnp.float32), [VMEM], (fetched,))
    chosen = call(
        functools.partial(choices_kernel, outer, inner),
        jax.ShapeDtypeStruct((2, (GROUPS // 2 * STEP + 1) * nsub, padded), jnp.bfloat16),
        [SMEM, VMEM],
        (me, table),
    )
    joined = call(
        functools.partial(join_packed_kernel if packed else join_kernel, outer),
        jax.ShapeDtypeStruct((span, nsub), jnp.bfloat16),
        [VMEM] * outer + [ANY],
        (*line, chosen),
    )
    blocks = [joined] + [exchanged(joined, "sub", flip) for flip in range(1, inner)]
    scratch = [
        pltpu.VMEM((span + 2 * STEP, nsub), jnp.float32),
        pltpu.VMEM((span + STEP, (STEP + 1) * nsub), jnp.bfloat16),
    ]
    flops = 2 * (span + STEP) * nsub * padded * (OMAX + 2)
    sums_shape = jax.ShapeDtypeStruct((length + REACH, padded), jnp.float32)
    early_shape = jax.ShapeDtypeStruct((REACH + WMAX, padded), jnp.float32)
    sums = call(first_sums_kernel, sums_shape, [VMEM, VMEM], (joined, chosen), scratch, flops)
    for flip in range(1, inner):
        sums, *early = call(
            functools.partial(more_sums_kernel, outer, inner, flip),
            [sums_shape, early_shape] if flip == inner - 1 else [sums_shape],
            [SMEM, VMEM, VMEM, VMEM],
            (me, blocks[flip], table, sums),
            [
                *scratch,
                pltpu.VMEM((length + REACH, padded), jnp.float32),
                pltpu.VMEM((nsub, padded), jnp.float32),
                *(
                    pltpu.VMEM(((STEP + (pair == GROUPS // 2 - 1)) * nsub, 2 * padded), jnp.bfloat16)
                    for pair in range(GROUPS // 2)
                ),
            ],
            flops,
        )
    early = early[0]
    later = passed_back(early, "tm")
    bands = call(
        bands_kernel,
        jax.ShapeDtypeStruct((LANES + WMAX, filters * LANES), jnp.bfloat16),
        [SMEM, ANY],
        (widths, early),
    )
    parts = length // LANES
    pieces = 4
    return call(
        functools.partial(boxcars_kernel, scale),
        jax.ShapeDtypeStruct((padded, filters, length), jnp.float32),
        [SMEM, VMEM, VMEM, VMEM],
        (widths, bands, sums, later),
        [
            pltpu.VMEM((padded, length + WMAX), jnp.bfloat16),
            pltpu.VMEM((parts, padded * filters, LANES), jnp.float32),
            pltpu.VMEM((parts, padded, filters, LANES), jnp.float32),
            pltpu.SemaphoreType.DMA((parts, pieces)),
        ],
        out_specs=HBM,
    )


def per_device(data, delays, offsets, widths):
    beams, chans, length = data.shape
    trials, nsub = offsets.shape
    groups = lax.axis_size("sub")
    outer = 1 << (groups.bit_length() // 2)
    outer = outer if groups % (outer * outer) == 0 else outer // 2
    per_sub = chans // (nsub // groups)
    scale = 1.0 / math.sqrt(chans * groups)
    padded = max(trials, LANES)
    table = jnp.pad(offsets, ((0, padded - trials), (0, 0))) if padded > trials else offsets
    me = lax.axis_index("sub").astype(jnp.int32).reshape(1)
    outs = [
        one_beam(data[beam], delays, table, me, widths, groups, outer, per_sub, scale)[:trials, None]
        for beam in range(beams)
    ]
    return outs[0] if beams == 1 else jnp.concatenate(outs, axis=1)


def solution(mesh):
    placed = (P(None, "sub", "tm"), P("sub"), P("sub", None), P())
    return jax.shard_map(
        per_device,
        mesh=mesh,
        in_specs=placed,
        out_specs=P("sub", None, None, "tm"),
        check_vma=False,
    )
```

```python
import functools
import math

import jax
import jax.numpy as jnp
from jax import lax
from jax.experimental import pallas as pl
from jax.experimental.pallas import tpu as pltpu
from jax.sharding import PartitionSpec as P

WMAX = 128
DCH = 16
OMAX = 96
LANES = 128
STEP = 16
GROUPS = OMAX // STEP
REACH = OMAX + DCH
VMEM = pl.BlockSpec(memory_space=pltpu.VMEM)
SMEM = pl.BlockSpec(memory_space=pltpu.SMEM)
HBM = pl.BlockSpec(memory_space=pltpu.HBM)
ANY = pl.BlockSpec(memory_space=pl.ANY)


def passed_back(value, axis):
    count = lax.axis_size(axis)
    return lax.ppermute(value, axis, [(source, source - 1) for source in range(1, count)])


def exchanged(value, axis, flip):
    count = lax.axis_size(axis)
    return lax.ppermute(value, axis, [(source, source ^ flip) for source in range(count)])


def series_kernel(
    per_sub, packed, delays_ref, data_ref, offsets_ref, series_ref, fetched_ref, delays, held, delays_sem, sems
):
    chans, length = data_ref.shape
    block = min(chans, 256)
    subs = block // per_sub
    wide = length + LANES
    first_copy = pltpu.make_async_copy(delays_ref, delays, delays_sem)
    first_copy.start()
    copies = []
    steps = sems.shape[0] // 2
    for source, target, base in ((data_ref, held, 0), (offsets_ref, fetched_ref, steps)):
        share = source.shape[0] // steps
        for at in range(steps):
            here = pl.ds(at * share, share)
            copies.append(
                pltpu.make_async_copy(source.at[here, :], target.at[here, :], sems.at[base + at])
            )
            copies[-1].start()
    rows = lax.broadcasted_iota(jnp.int32, (DCH * subs, block), 0)
    owner = lax.broadcasted_iota(jnp.int32, (1, block), 1) // per_sub
    blank = jnp.zeros((subs, LANES), jnp.float32)
    first_copy.wait()
    members = [
        jnp.where(rows == delays[:, at * block : (at + 1) * block] * subs + owner, 1.0, 0.0).astype(jnp.bfloat16)
        for at in range(chans // block)
    ]
    for copy in copies[:steps]:
        copy.wait()
    parts = []
    for at, member in enumerate(members):
        picked = jnp.dot(member, held[pl.ds(at * block, block), :], preferred_element_type=jnp.float32)
        total = None
        for delay in range(DCH):
            late = jnp.concatenate([picked[delay * subs : (delay + 1) * subs, :], blank], axis=1)
            late = pltpu.roll(late, DCH - delay, 1)
            total = late if total is None else total + late
        parts.append(total)
    total = jnp.concatenate(parts, axis=0)
    if packed:
        half = series_ref.shape[0]
        both = jnp.concatenate([total, pltpu.roll(total, wide - half, 1)], axis=0)
        for first in range(0, half, LANES):
            count = min(LANES, half - first)
            tile = both[:, first : first + LANES].T
            series_ref[pl.ds(first, count), :] = tile[:count].astype(jnp.bfloat16)
    else:
        series_ref[...] = total.astype(jnp.bfloat16)
    for copy in copies[steps:]:
        copy.wait()


def join_packed_kernel(outer, *refs):
    blocks, joined_ref = refs[:outer], refs[-1]
    half = blocks[0].shape[0]
    rest = joined_ref.shape[0] - half
    lane = lax.broadcasted_iota(jnp.int32, (half, LANES), 1)
    for at in range(outer // 2):
        left = blocks[2 * at][...].astype(jnp.float32)
        right = blocks[2 * at + 1][...].astype(jnp.float32)
        lanes = pl.ds(at * LANES, LANES)
        early = jnp.where(lane < LANES // 2, left, pltpu.roll(right, LANES // 2, 1))
        late = jnp.where(lane < LANES // 2, pltpu.roll(left, LANES // 2, 1), right)
        joined_ref[pl.ds(0, half), lanes] = early.astype(jnp.bfloat16)
        joined_ref[pl.ds(half, rest), lanes] = late[:rest].astype(jnp.bfloat16)


def join_kernel(outer, *refs):
    blocks, joined_ref = refs[:outer], refs[-1]
    subs = blocks[0].shape[0]
    rows = joined_ref.shape[0]
    several = LANES // subs
    for at in range(outer // several):
        for first in range(0, rows, LANES):
            count = min(LANES, rows - first)
            tile = jnp.concatenate(
                [
                    blocks[at * several + slot][:, pl.ds(first, LANES)].astype(jnp.float32)
                    for slot in range(several)
                ],
                axis=0,
            ).T
            joined_ref[pl.ds(first, count), pl.ds(at * LANES, LANES)] = tile[:count].astype(jnp.bfloat16)


def offsets_kernel(offsets_ref, table_ref):
    for at in range(offsets_ref.shape[1] // LANES):
        here = pl.ds(at * LANES, LANES)
        table_ref[here, :] = offsets_ref[:, here].astype(jnp.float32).T


def slot_start(slot, flip, outer, inner, subs, me):
    return pl.multiple_of((((me // inner) ^ slot) * inner + ((me % inner) ^ flip)) * subs, subs)


def choices_kernel(outer, inner, me_ref, table_ref, chosen_ref):
    subs = table_ref.shape[0] // (outer * inner)
    nsub = outer * subs
    for slot in range(outer):
        start = slot_start(slot, 0, outer, inner, subs, me_ref[0])
        for first in range(0, subs, 16):
            offset = table_ref[pl.ds(pl.multiple_of(start + first, 16), 16), :]
            groups = jnp.minimum(jnp.floor(offset * (1.0 / STEP)), float(GROUPS - 1))
            lags = offset - float(STEP) * groups
            in_group = [jnp.where(groups == float(group), 1.0, 0.0) for group in range(GROUPS)]
            for lag in range(STEP + 1):
                at_lag = jnp.where(lags == float(lag), 1.0, 0.0)
                for group in range(GROUPS - 2 if lag == STEP else 0, GROUPS):
                    place = (group // 2 * STEP + lag) * nsub + slot * subs + first
                    chosen_ref[group % 2, pl.ds(place, 16), :] = (at_lag * in_group[group]).astype(
                        jnp.bfloat16
                    )


def shift_series(joined_ref, moving, shifted):
    span, nsub = joined_ref.shape
    blank = jnp.zeros((STEP, nsub), jnp.float32)
    moving[pl.ds(0, STEP), :] = blank
    moving[pl.ds(STEP, span), :] = joined_ref[...].astype(jnp.float32)
    moving[pl.ds(STEP + span, STEP), :] = blank
    for lag in range(STEP + 1):
        shifted[:, pl.ds(lag * nsub, nsub)] = moving[pl.ds(lag, span + STEP), :].astype(jnp.bfloat16)


def add_pair(total, pair, both):
    rows, trials = both.shape[0], both.shape[1] // 2
    for odd in range(2):
        first = STEP * (GROUPS - 1 - 2 * pair - odd)
        total[pl.ds(first, rows), :] += both[:, odd * trials : (odd + 1) * trials]


def first_sums_kernel(joined_ref, chosen_ref, sums_ref, moving, shifted):
    nsub = joined_ref.shape[1]
    shift_series(joined_ref, moving, shifted)
    sums_ref[...] = jnp.zeros_like(sums_ref)
    for pair in range(GROUPS // 2):
        depth = (STEP + (pair == GROUPS // 2 - 1)) * nsub
        weights = [chosen_ref[odd, pl.ds(pair * STEP * nsub, depth), :] for odd in range(2)]
        add_pair(
            sums_ref,
            pair,
            jnp.dot(
                shifted[:, pl.ds(0, depth)],
                jnp.concatenate(weights, axis=1),
                preferred_element_type=jnp.float32,
            ),
        )


def more_sums_kernel(outer, inner, flip, me_ref, joined_ref, table_ref, before_ref, sums_ref, *refs):
    pairs = GROUPS // 2
    *early_ref, moving, shifted, table = refs[:-pairs]
    totals = refs[-pairs:]
    nsub = joined_ref.shape[1]
    subs = nsub // outer
    for slot in range(outer):
        start = slot_start(slot, flip, outer, inner, subs, me_ref[0])
        table[pl.ds(slot * subs, subs), :] = table_ref[pl.ds(start, subs), :]
    shift_series(joined_ref, moving, shifted)
    for lag in range(STEP + 1):
        for pair in range(pairs - 1 if lag == STEP else 0, pairs):
            weights = [
                jnp.where(table[...] == float(STEP * (2 * pair + odd) + lag), 1.0, 0.0).astype(jnp.bfloat16)
                if lag < STEP or odd
                else jnp.zeros(table.shape, jnp.bfloat16)
                for odd in range(2)
            ]
            both = jnp.dot(
                shifted[:, pl.ds(lag * nsub, nsub)],
                jnp.concatenate(weights, axis=1),
                preferred_element_type=jnp.float32,
            )
            if lag:
                totals[pair][...] += both
            else:
                totals[pair][...] = both
    sums_ref[...] = before_ref[...]
    for pair in range(pairs):
        add_pair(sums_ref, pair, totals[pair][...])
    for ref in early_ref:
        ref[...] = sums_ref[pl.ds(0, ref.shape[0]), :]


def bands_kernel(widths_ref, early_ref, bands_ref):
    del early_ref
    shape = (bands_ref.shape[0], LANES)
    lag = lax.broadcasted_iota(jnp.int32, shape, 0) - lax.broadcasted_iota(jnp.int32, shape, 1)
    for at in range(widths_ref.shape[0]):
        band = jnp.where((lag >= 0) & (lag < widths_ref[at]), 1.0, 0.0)
        bands_ref[:, pl.ds(at * LANES, LANES)] = band.astype(jnp.bfloat16)


def boxcars_kernel(scale, widths_ref, bands_ref, sums_ref, later_ref, out_ref, values, mixed, tiles, sems):
    trials = sums_ref.shape[1]
    length = sums_ref.shape[0] - REACH
    filters = widths_ref.shape[0]
    whole = length - REACH
    total = jnp.concatenate(
        [
            sums_ref[pl.ds(REACH, whole), :],
            sums_ref[pl.ds(length, REACH), :] + later_ref[pl.ds(0, REACH), :],
            later_ref[pl.ds(REACH, WMAX), :],
        ],
        axis=0,
    )
    for first in range(0, length + WMAX, LANES):
        tile = (total[first : first + LANES] * scale).T
        values[:, pl.ds(first, LANES)] = tile.astype(jnp.bfloat16)
    share = trials // sems.shape[1]
    widths = [jnp.full((1, LANES), widths_ref[at], jnp.int32).astype(jnp.float32) for at in range(filters)]
    shares = [1.0 / jnp.sqrt(width) for width in widths]
    copies = []
    for part in range(length // LANES):
        lanes = pl.ds(part * LANES, LANES)
        for at in range(filters):
            sums = jnp.dot(
                values[:, pl.ds(part * LANES, LANES + WMAX)],
                bands_ref[:, pl.ds(at * LANES, LANES)],
                preferred_element_type=jnp.float32,
            )
            mixed[part, pl.ds(at, trials, stride=filters), :] = sums * shares[at]
        tiles[part] = mixed[part].reshape(trials, filters, LANES)
        for piece in range(sems.shape[1]):
            some = pl.ds(piece * share, share)
            copies.append(
                pltpu.make_async_copy(
                    tiles.at[part, some], out_ref.at[some, :, lanes], sems.at[part, piece]
                )
            )
            copies[-1].start()
    for copy in copies:
        copy.wait()


def call(kernel, out_shape, in_specs, args, scratch=(), flops=0, **options):
    several = isinstance(out_shape, list)
    options.setdefault("out_specs", [VMEM] * len(out_shape) if several else VMEM)
    return pl.pallas_call(
        kernel,
        out_shape=out_shape,
        in_specs=in_specs,
        scratch_shapes=list(scratch),
        compiler_params=pltpu.CompilerParams(vmem_limit_bytes=16 << 20),
        cost_estimate=pl.CostEstimate(flops=flops, bytes_accessed=1 << 20, transcendentals=0),
        **options,
    )(*args)


def one_beam(own, delays, offsets, me, widths, groups, outer, per_sub, scale):
    chans, length = own.shape
    padded, all_subs = offsets.shape
    sub_dev = chans // per_sub
    inner = groups // outer
    filters = widths.shape[0]
    span = length + DCH
    packed = 2 * sub_dev == LANES
    series_shape = (-(-span // 32) * 16, LANES) if packed else (sub_dev, length + LANES)
    steps = 4
    series, fetched = call(
        functools.partial(series_kernel, per_sub, packed),
        [
            jax.ShapeDtypeStruct(series_shape, jnp.bfloat16),
            jax.ShapeDtypeStruct((padded, all_subs), jnp.int32),
        ],
        [HBM, HBM, HBM],
        tuple(pltpu.with_memory_space_constraint(x, pltpu.HBM) for x in (delays[None, :], own, offsets)),
        [
            pltpu.VMEM((1, chans), jnp.int32),
            pltpu.VMEM((chans, length), jnp.bfloat16),
            pltpu.SemaphoreType.DMA,
            pltpu.SemaphoreType.DMA((2 * steps,)),
        ],
    )
    line = [series] + [exchanged(series, "sub", flip * inner) for flip in range(1, outer)]
    nsub = outer * sub_dev
    table = call(offsets_kernel, jax.ShapeDtypeStruct((all_subs, padded), jnp.float32), [VMEM], (fetched,))
    chosen = call(
        functools.partial(choices_kernel, outer, inner),
        jax.ShapeDtypeStruct((2, (GROUPS // 2 * STEP + 1) * nsub, padded), jnp.bfloat16),
        [SMEM, VMEM],
        (me, table),
    )
    joined = call(
        functools.partial(join_packed_kernel if packed else join_kernel, outer),
        jax.ShapeDtypeStruct((span, nsub), jnp.bfloat16),
        [VMEM] * outer + [ANY],
        (*line, chosen),
    )
    blocks = [joined] + [exchanged(joined, "sub", flip) for flip in range(1, inner)]
    scratch = [
        pltpu.VMEM((span + 2 * STEP, nsub), jnp.float32),
        pltpu.VMEM((span + STEP, (STEP + 1) * nsub), jnp.bfloat16),
    ]
    flops = 2 * (span + STEP) * nsub * padded * (OMAX + 2)
    sums_shape = jax.ShapeDtypeStruct((length + REACH, padded), jnp.float32)
    early_shape = jax.ShapeDtypeStruct((REACH + WMAX, padded), jnp.float32)
    sums = call(first_sums_kernel, sums_shape, [VMEM, VMEM], (joined, chosen), scratch, flops)
    for flip in range(1, inner):
        sums, *early = call(
            functools.partial(more_sums_kernel, outer, inner, flip),
            [sums_shape, early_shape] if flip == inner - 1 else [sums_shape],
            [SMEM, VMEM, VMEM, VMEM],
            (me, blocks[flip], table, sums),
            [
                *scratch,
                pltpu.VMEM((nsub, padded), jnp.float32),
                *[pltpu.VMEM((span + STEP, 2 * padded), jnp.float32)] * (GROUPS // 2),
            ],
            flops,
        )
    early = early[0]
    later = passed_back(early, "tm")
    bands = call(
        bands_kernel,
        jax.ShapeDtypeStruct((LANES + WMAX, filters * LANES), jnp.bfloat16),
        [SMEM, ANY],
        (widths, early),
    )
    parts = length // LANES
    pieces = 4
    return call(
        functools.partial(boxcars_kernel, scale),
        jax.ShapeDtypeStruct((padded, filters, length), jnp.float32),
        [SMEM, VMEM, VMEM, VMEM],
        (widths, bands, sums, later),
        [
            pltpu.VMEM((padded, length + WMAX), jnp.bfloat16),
            pltpu.VMEM((parts, padded * filters, LANES), jnp.float32),
            pltpu.VMEM((parts, padded, filters, LANES), jnp.float32),
            pltpu.SemaphoreType.DMA((parts, pieces)),
        ],
        out_specs=HBM,
    )


def per_device(data, delays, offsets, widths):
    beams, chans, length = data.shape
    trials, nsub = offsets.shape
    groups = lax.axis_size("sub")
    outer = 1 << (groups.bit_length() // 2)
    outer = outer if groups % (outer * outer) == 0 else outer // 2
    per_sub = chans // (nsub // groups)
    scale = 1.0 / math.sqrt(chans * groups)
    padded = max(trials, LANES)
    table = jnp.pad(offsets, ((0, padded - trials), (0, 0))) if padded > trials else offsets
    me = lax.axis_index("sub").astype(jnp.int32).reshape(1)
    outs = [
        one_beam(data[beam], delays, table, me, widths, groups, outer, per_sub, scale)[:trials, None]
        for beam in range(beams)
    ]
    return outs[0] if beams == 1 else jnp.concatenate(outs, axis=1)


def solution(mesh):
    placed = (P(None, "sub", "tm"), P("sub"), P("sub", None), P())
    return jax.shard_map(
        per_device,
        mesh=mesh,
        in_specs=placed,
        out_specs=P("sub", None, None, "tm"),
        check_vma=False,
    )
```

```python
import functools
import math

import jax
import jax.numpy as jnp
from jax import lax
from jax.experimental import pallas as pl
from jax.experimental.pallas import tpu as pltpu
from jax.sharding import PartitionSpec as P

WMAX = 128
DCH = 16
OMAX = 96
LANES = 128
STEP = 16
GROUPS = OMAX // STEP
REACH = OMAX + DCH
VMEM = pl.BlockSpec(memory_space=pltpu.VMEM)
SMEM = pl.BlockSpec(memory_space=pltpu.SMEM)
HBM = pl.BlockSpec(memory_space=pltpu.HBM)
ANY = pl.BlockSpec(memory_space=pl.ANY)


def passed_back(value, axis):
    count = lax.axis_size(axis)
    return lax.ppermute(value, axis, [(source, source - 1) for source in range(1, count)])


def exchanged(value, axis, flip):
    count = lax.axis_size(axis)
    return lax.ppermute(value, axis, [(source, source ^ flip) for source in range(count)])


def series_kernel(
    per_sub, packed, delays_ref, data_ref, offsets_ref, series_ref, fetched_ref, delays, held, delays_sem, sems
):
    chans, length = data_ref.shape
    block = min(chans, 256)
    subs = block // per_sub
    wide = length + LANES
    first_copy = pltpu.make_async_copy(delays_ref, delays, delays_sem)
    first_copy.start()
    copies = []
    steps = sems.shape[0] // 2
    for source, target, base in ((data_ref, held, 0), (offsets_ref, fetched_ref, steps)):
        share = source.shape[0] // steps
        for at in range(steps):
            here = pl.ds(at * share, share)
            copies.append(
                pltpu.make_async_copy(source.at[here, :], target.at[here, :], sems.at[base + at])
            )
            copies[-1].start()
    rows = lax.broadcasted_iota(jnp.int32, (DCH * subs, block), 0)
    owner = lax.broadcasted_iota(jnp.int32, (1, block), 1) // per_sub
    blank = jnp.zeros((subs, LANES), jnp.float32)
    first_copy.wait()
    members = [
        jnp.where(rows == delays[:, at * block : (at + 1) * block] * subs + owner, 1.0, 0.0).astype(jnp.bfloat16)
        for at in range(chans // block)
    ]
    parts = []
    for at, member in enumerate(members):
        if at * 2 % steps == 0:
            for copy in copies[at : at + steps // 2] if len(members) == steps else copies[:steps]:
                copy.wait()
        picked = jnp.dot(member, held[pl.ds(at * block, block), :], preferred_element_type=jnp.float32)
        total = None
        for delay in range(DCH):
            late = jnp.concatenate([picked[delay * subs : (delay + 1) * subs, :], blank], axis=1)
            late = pltpu.roll(late, DCH - delay, 1)
            total = late if total is None else total + late
        parts.append(total)
    total = jnp.concatenate(parts, axis=0)
    if packed:
        half = series_ref.shape[0]
        both = jnp.concatenate([total, pltpu.roll(total, wide - half, 1)], axis=0)
        for first in range(0, half, LANES):
            count = min(LANES, half - first)
            tile = both[:, first : first + LANES].T
            series_ref[pl.ds(first, count), :] = tile[:count].astype(jnp.bfloat16)
    else:
        series_ref[...] = total.astype(jnp.bfloat16)
    for copy in copies[steps:]:
        copy.wait()


def join_packed_kernel(outer, *refs):
    blocks, joined_ref = refs[:outer], refs[-1]
    half = blocks[0].shape[0]
    rest = joined_ref.shape[0] - half
    lane = lax.broadcasted_iota(jnp.int32, (half, LANES), 1)
    for at in range(outer // 2):
        left = blocks[2 * at][...].astype(jnp.float32)
        right = blocks[2 * at + 1][...].astype(jnp.float32)
        lanes = pl.ds(at * LANES, LANES)
        early = jnp.where(lane < LANES // 2, left, pltpu.roll(right, LANES // 2, 1))
        late = jnp.where(lane < LANES // 2, pltpu.roll(left, LANES // 2, 1), right)
        joined_ref[pl.ds(0, half), lanes] = early.astype(jnp.bfloat16)
        joined_ref[pl.ds(half, rest), lanes] = late[:rest].astype(jnp.bfloat16)


def join_kernel(outer, *refs):
    blocks, joined_ref = refs[:outer], refs[-1]
    subs = blocks[0].shape[0]
    rows = joined_ref.shape[0]
    several = LANES // subs
    for at in range(outer // several):
        for first in range(0, rows, LANES):
            count = min(LANES, rows - first)
            tile = jnp.concatenate(
                [
                    blocks[at * several + slot][:, pl.ds(first, LANES)].astype(jnp.float32)
                    for slot in range(several)
                ],
                axis=0,
            ).T
            joined_ref[pl.ds(first, count), pl.ds(at * LANES, LANES)] = tile[:count].astype(jnp.bfloat16)


def offsets_kernel(offsets_ref, table_ref):
    for at in range(offsets_ref.shape[1] // LANES):
        here = pl.ds(at * LANES, LANES)
        table_ref[here, :] = offsets_ref[:, here].astype(jnp.float32).T


def slot_start(slot, flip, outer, inner, subs, me):
    return pl.multiple_of((((me // inner) ^ slot) * inner + ((me % inner) ^ flip)) * subs, subs)


def add_pair(total, pair, both):
    rows, trials = both.shape[0], both.shape[1] // 2
    for odd in range(2):
        first = STEP * (GROUPS - 1 - 2 * pair - odd)
        total[pl.ds(first, rows), :] += both[:, odd * trials : (odd + 1) * trials]


def sums_kernel(given, outer, inner, flip, me_ref, joined_ref, table_ref, *refs):
    pairs = GROUPS // 2
    before_ref, sums_ref, *early_ref = refs[: -3 - pairs] if given else (None, *refs[: -3 - pairs])
    moving, shifted, table = refs[-3 - pairs : -pairs]
    totals = refs[-pairs:]
    span, nsub = joined_ref.shape
    subs = nsub // outer
    for slot in range(outer):
        start = slot_start(slot, flip, outer, inner, subs, me_ref[0])
        table[pl.ds(slot * subs, subs), :] = table_ref[pl.ds(start, subs), :]
    blank = jnp.zeros((STEP, nsub), jnp.float32)
    moving[pl.ds(0, STEP), :] = blank
    moving[pl.ds(STEP, span), :] = joined_ref[...].astype(jnp.float32)
    moving[pl.ds(STEP + span, STEP), :] = blank

    def shift(lag):
        shifted[:, pl.ds(lag * nsub, nsub)] = moving[pl.ds(lag, span + STEP), :].astype(jnp.bfloat16)

    shift(0)
    for lag in range(STEP + 1):
        if lag < STEP:
            shift(lag + 1)
        for pair in range(pairs - 1 if lag == STEP else 0, pairs):
            weights = [
                jnp.where(table[...] == float(STEP * (2 * pair + odd) + lag), 1.0, 0.0).astype(jnp.bfloat16)
                if lag < STEP or odd
                else jnp.zeros(table.shape, jnp.bfloat16)
                for odd in range(2)
            ]
            both = jnp.dot(
                shifted[:, pl.ds(lag * nsub, nsub)],
                jnp.concatenate(weights, axis=1),
                preferred_element_type=jnp.float32,
            )
            if lag:
                totals[pair][...] += both
            else:
                totals[pair][...] = both
    if before_ref is None:
        sums_ref[...] = jnp.zeros_like(sums_ref)
    else:
        sums_ref[...] = before_ref[...]
    for pair in range(pairs):
        add_pair(sums_ref, pair, totals[pair][...])
    for ref in early_ref:
        ref[...] = sums_ref[pl.ds(0, ref.shape[0]), :]


def bands_kernel(widths_ref, early_ref, bands_ref):
    del early_ref
    shape = (bands_ref.shape[0], LANES)
    lag = lax.broadcasted_iota(jnp.int32, shape, 0) - lax.broadcasted_iota(jnp.int32, shape, 1)
    for at in range(widths_ref.shape[0]):
        band = jnp.where((lag >= 0) & (lag < widths_ref[at]), 1.0, 0.0)
        bands_ref[:, pl.ds(at * LANES, LANES)] = band.astype(jnp.bfloat16)


def boxcars_kernel(scale, widths_ref, bands_ref, sums_ref, later_ref, out_ref, values, mixed, sems):
    trials = sums_ref.shape[1]
    length = sums_ref.shape[0] - REACH
    filters = widths_ref.shape[0]
    whole = length - REACH
    total = jnp.concatenate(
        [
            sums_ref[pl.ds(REACH, whole), :],
            sums_ref[pl.ds(length, REACH), :] + later_ref[pl.ds(0, REACH), :],
            later_ref[pl.ds(REACH, WMAX), :],
        ],
        axis=0,
    )
    for first in range(0, length + WMAX, LANES):
        tile = (total[first : first + LANES] * scale).T
        values[:, pl.ds(first, LANES)] = tile.astype(jnp.bfloat16)
    parts, pieces = sems.shape
    share = trials // pieces
    widths = [jnp.full((1, LANES), widths_ref[at], jnp.int32).astype(jnp.float32) for at in range(filters)]
    shares = [1.0 / jnp.sqrt(width) for width in widths]
    tiles = mixed.reshape(parts, trials, filters, LANES)
    copies = []
    for piece in range(pieces):
        some = pl.ds(piece * share, share)
        windows = [values[some, pl.ds(part * LANES, LANES + WMAX)] for part in range(parts)]
        sums = jnp.dot(jnp.concatenate(windows, axis=0), bands_ref[...], preferred_element_type=jnp.float32)
        for part in range(parts):
            for at in range(filters):
                mixed[part, pl.ds(piece * share * filters + at, share, stride=filters), :] = (
                    sums[part * share : (part + 1) * share, at * LANES : (at + 1) * LANES] * shares[at]
                )
            target = out_ref.at[some, :, pl.ds(part * LANES, LANES)]
            copies.append(pltpu.make_async_copy(tiles.at[part, some], target, sems.at[part, piece]))
            copies[-1].start()
    for copy in copies:
        copy.wait()


def call(kernel, out_shape, in_specs, args, scratch=(), flops=0, **options):
    several = isinstance(out_shape, list)
    options.setdefault("out_specs", [VMEM] * len(out_shape) if several else VMEM)
    return pl.pallas_call(
        kernel,
        out_shape=out_shape,
        in_specs=in_specs,
        scratch_shapes=list(scratch),
        compiler_params=pltpu.CompilerParams(vmem_limit_bytes=16 << 20),
        cost_estimate=pl.CostEstimate(flops=flops, bytes_accessed=1 << 20, transcendentals=0),
        **options,
    )(*args)


def one_beam(own, delays, offsets, me, widths, groups, outer, per_sub, scale):
    chans, length = own.shape
    padded, all_subs = offsets.shape
    sub_dev = chans // per_sub
    inner = groups // outer
    filters = widths.shape[0]
    span = length + DCH
    packed = 2 * sub_dev == LANES
    series_shape = (-(-span // 32) * 16, LANES) if packed else (sub_dev, length + LANES)
    steps = 4
    series, fetched = call(
        functools.partial(series_kernel, per_sub, packed),
        [
            jax.ShapeDtypeStruct(series_shape, jnp.bfloat16),
            jax.ShapeDtypeStruct((padded, all_subs), jnp.int32),
        ],
        [HBM, HBM, HBM],
        tuple(pltpu.with_memory_space_constraint(x, pltpu.HBM) for x in (delays[None, :], own, offsets)),
        [
            pltpu.VMEM((1, chans), jnp.int32),
            pltpu.VMEM((chans, length), jnp.bfloat16),
            pltpu.SemaphoreType.DMA,
            pltpu.SemaphoreType.DMA((2 * steps,)),
        ],
    )
    line = [series] + [exchanged(series, "sub", flip * inner) for flip in range(1, outer)]
    nsub = outer * sub_dev
    table = call(offsets_kernel, jax.ShapeDtypeStruct((all_subs, padded), jnp.float32), [VMEM], (fetched,))
    joined = call(
        functools.partial(join_packed_kernel if packed else join_kernel, outer),
        jax.ShapeDtypeStruct((span, nsub), jnp.bfloat16),
        [VMEM] * outer + [ANY],
        (*line, table),
    )
    blocks = [joined] + [exchanged(joined, "sub", flip) for flip in range(1, inner)]
    scratch = [
        pltpu.VMEM((span + 2 * STEP, nsub), jnp.float32),
        pltpu.VMEM((span + STEP, (STEP + 1) * nsub), jnp.bfloat16),
        pltpu.VMEM((nsub, padded), jnp.float32),
        *[pltpu.VMEM((span + STEP, 2 * padded), jnp.float32)] * (GROUPS // 2),
    ]
    flops = 2 * (span + STEP) * nsub * padded * (OMAX + 2)
    sums_shape = jax.ShapeDtypeStruct((length + REACH, padded), jnp.float32)
    early_shape = jax.ShapeDtypeStruct((REACH + WMAX, padded), jnp.float32)
    given = ()
    for flip in range(inner):
        sums, *early = call(
            functools.partial(sums_kernel, flip > 0, outer, inner, flip),
            [sums_shape, early_shape] if flip == inner - 1 else [sums_shape],
            [SMEM] + [VMEM] * (2 + len(given)),
            (me, blocks[flip], table, *given),
            scratch,
            flops,
        )
        given = (sums,)
    early = early[0]
    later = passed_back(early, "tm")
    bands = call(
        bands_kernel,
        jax.ShapeDtypeStruct((LANES + WMAX, filters * LANES), jnp.bfloat16),
        [SMEM, ANY],
        (widths, early),
    )
    parts = length // LANES
    pieces = 2
    return call(
        functools.partial(boxcars_kernel, scale),
        jax.ShapeDtypeStruct((padded, filters, length), jnp.float32),
        [SMEM, VMEM, VMEM, VMEM],
        (widths, bands, sums, later),
        [
            pltpu.VMEM((padded, length + WMAX), jnp.bfloat16),
            pltpu.VMEM((parts, padded * filters, LANES), jnp.float32),
            pltpu.SemaphoreType.DMA((parts, pieces)),
        ],
        out_specs=HBM,
    )


def per_device(data, delays, offsets, widths):
    beams, chans, length = data.shape
    trials, nsub = offsets.shape
    groups = lax.axis_size("sub")
    outer = 1 << (groups.bit_length() // 2)
    outer = outer if groups % (outer * outer) == 0 else outer // 2
    per_sub = chans // (nsub // groups)
    scale = 1.0 / math.sqrt(chans * groups)
    padded = max(trials, LANES)
    table = jnp.pad(offsets, ((0, padded - trials), (0, 0))) if padded > trials else offsets
    me = lax.axis_index("sub").astype(jnp.int32).reshape(1)
    outs = [
        one_beam(data[beam], delays, table, me, widths, groups, outer, per_sub, scale)[:trials, None]
        for beam in range(beams)
    ]
    return outs[0] if beams == 1 else jnp.concatenate(outs, axis=1)


def solution(mesh):
    placed = (P(None, "sub", "tm"), P("sub"), P("sub", None), P())
    return jax.shard_map(
        per_device,
        mesh=mesh,
        in_specs=placed,
        out_specs=P("sub", None, None, "tm"),
        check_vma=False,
    )
```

```python
import functools
import math

import jax
import jax.numpy as jnp
from jax import lax
from jax.experimental import pallas as pl
from jax.experimental.pallas import tpu as pltpu
from jax.sharding import PartitionSpec as P

WMAX = 128
DCH = 16
OMAX = 96
LANES = 128
STEP = 16
GROUPS = OMAX // STEP
TOGETHER = 2
REACH = OMAX + DCH
VMEM = pl.BlockSpec(memory_space=pltpu.VMEM)
SMEM = pl.BlockSpec(memory_space=pltpu.SMEM)
HBM = pl.BlockSpec(memory_space=pltpu.HBM)
ANY = pl.BlockSpec(memory_space=pl.ANY)


def passed_back(value, axis):
    count = lax.axis_size(axis)
    return lax.ppermute(value, axis, [(source, source - 1) for source in range(1, count)])


def exchanged(value, axis, flip):
    count = lax.axis_size(axis)
    return lax.ppermute(value, axis, [(source, source ^ flip) for source in range(count)])


def series_kernel(
    per_sub, packed, delays_ref, data_ref, offsets_ref, series_ref, fetched_ref, delays, held, delays_sem, sems
):
    chans, length = data_ref.shape
    block = min(chans, 256)
    subs = block // per_sub
    wide = length + LANES
    first_copy = pltpu.make_async_copy(delays_ref, delays, delays_sem)
    first_copy.start()
    copies = []
    steps = sems.shape[0] // 2
    for source, target, base in ((data_ref, held, 0), (offsets_ref, fetched_ref, steps)):
        share = source.shape[0] // steps
        for at in range(steps):
            here = pl.ds(at * share, share)
            copies.append(
                pltpu.make_async_copy(source.at[here, :], target.at[here, :], sems.at[base + at])
            )
            copies[-1].start()
    rows = lax.broadcasted_iota(jnp.int32, (DCH * subs, block), 0)
    owner = lax.broadcasted_iota(jnp.int32, (1, block), 1) // per_sub
    blank = jnp.zeros((subs, LANES), jnp.float32)
    first_copy.wait()
    members = [
        jnp.where(rows == delays[:, at * block : (at + 1) * block] * subs + owner, 1.0, 0.0).astype(jnp.bfloat16)
        for at in range(chans // block)
    ]
    for copy in copies[:steps]:
        copy.wait()
    parts = []
    for at, member in enumerate(members):
        picked = jnp.dot(member, held[pl.ds(at * block, block), :], preferred_element_type=jnp.float32)
        total = None
        for delay in range(DCH):
            late = jnp.concatenate([picked[delay * subs : (delay + 1) * subs, :], blank], axis=1)
            late = pltpu.roll(late, DCH - delay, 1)
            total = late if total is None else total + late
        parts.append(total)
    total = jnp.concatenate(parts, axis=0)
    if packed:
        half = series_ref.shape[0]
        both = jnp.concatenate([total, pltpu.roll(total, wide - half, 1)], axis=0)
        for first in range(0, half, LANES):
            count = min(LANES, half - first)
            tile = both[:, first : first + LANES].T
            series_ref[pl.ds(first, count), :] = tile[:count].astype(jnp.bfloat16)
    else:
        series_ref[...] = total.astype(jnp.bfloat16)
    for copy in copies[steps:]:
        copy.wait()


def join_packed_kernel(outer, *refs):
    blocks, joined_ref = refs[:outer], refs[-1]
    half = blocks[0].shape[0]
    rest = joined_ref.shape[0] - half
    lane = lax.broadcasted_iota(jnp.int32, (half, LANES), 1)
    for at in range(outer // 2):
        left = blocks[2 * at][...].astype(jnp.float32)
        right = blocks[2 * at + 1][...].astype(jnp.float32)
        lanes = pl.ds(at * LANES, LANES)
        early = jnp.where(lane < LANES // 2, left, pltpu.roll(right, LANES // 2, 1))
        late = jnp.where(lane < LANES // 2, pltpu.roll(left, LANES // 2, 1), right)
        joined_ref[pl.ds(0, half), lanes] = early.astype(jnp.bfloat16)
        joined_ref[pl.ds(half, rest), lanes] = late[:rest].astype(jnp.bfloat16)


def join_kernel(outer, *refs):
    blocks, joined_ref = refs[:outer], refs[-1]
    subs = blocks[0].shape[0]
    rows = joined_ref.shape[0]
    several = LANES // subs
    for at in range(outer // several):
        for first in range(0, rows, LANES):
            count = min(LANES, rows - first)
            tile = jnp.concatenate(
                [
                    blocks[at * several + slot][:, pl.ds(first, LANES)].astype(jnp.float32)
                    for slot in range(several)
                ],
                axis=0,
            ).T
            joined_ref[pl.ds(first, count), pl.ds(at * LANES, LANES)] = tile[:count].astype(jnp.bfloat16)


def offsets_kernel(offsets_ref, table_ref):
    for at in range(offsets_ref.shape[1] // LANES):
        here = pl.ds(at * LANES, LANES)
        table_ref[here, :] = offsets_ref[:, here].astype(jnp.float32).T


def slot_start(slot, flip, outer, inner, subs, me):
    return pl.multiple_of((((me // inner) ^ slot) * inner + ((me % inner) ^ flip)) * subs, subs)


def add_pair(total, pair, both):
    rows, trials = both.shape[0], both.shape[1] // 2
    for odd in range(2):
        first = STEP * (GROUPS - 1 - 2 * pair - odd)
        total[pl.ds(first, rows), :] += both[:, odd * trials : (odd + 1) * trials]


def sums_kernel(given, outer, inner, flip, me_ref, joined_ref, table_ref, *refs):
    pairs = GROUPS // 2
    before_ref, sums_ref, *early_ref = refs[: -3 - pairs] if given else (None, *refs[: -3 - pairs])
    moving, shifted, table = refs[-3 - pairs : -pairs]
    totals = refs[-pairs:]
    span, nsub = joined_ref.shape
    subs = nsub // outer
    for slot in range(outer):
        start = slot_start(slot, flip, outer, inner, subs, me_ref[0])
        table[pl.ds(slot * subs, subs), :] = table_ref[pl.ds(start, subs), :]
    blank = jnp.zeros((STEP, nsub), jnp.float32)
    moving[pl.ds(0, STEP), :] = blank
    moving[pl.ds(STEP, span), :] = joined_ref[...].astype(jnp.float32)
    moving[pl.ds(STEP + span, STEP), :] = blank

    def shift(lag):
        shifted[:, pl.ds(lag * nsub, nsub)] = moving[pl.ds(lag, span + STEP), :].astype(jnp.bfloat16)

    def tile(lag, pair):
        halves = [
            jnp.where(table[...] == float(STEP * (2 * pair + odd) + lag), 1.0, 0.0).astype(jnp.bfloat16)
            if lag < STEP or odd
            else jnp.zeros(table.shape, jnp.bfloat16)
            for odd in range(2)
        ]
        return jnp.concatenate(halves, axis=1)

    for lag in range(TOGETHER):
        shift(lag)
    for first in range(0, STEP + 1, TOGETHER):
        lags = range(first, min(first + TOGETHER, STEP + 1))
        for lag in range(first + TOGETHER, min(first + 2 * TOGETHER, STEP + 1)):
            shift(lag)
        for pair in range(pairs - 1 if first == STEP else 0, pairs):
            both = jnp.dot(
                shifted[:, pl.ds(first * nsub, len(lags) * nsub)],
                jnp.concatenate([tile(lag, pair) for lag in lags], axis=0),
                preferred_element_type=jnp.float32,
            )
            if first:
                totals[pair][...] += both
            else:
                totals[pair][...] = both
    if before_ref is None:
        sums_ref[...] = jnp.zeros_like(sums_ref)
    else:
        sums_ref[...] = before_ref[...]
    for pair in range(pairs):
        add_pair(sums_ref, pair, totals[pair][...])
    for ref in early_ref:
        ref[...] = sums_ref[pl.ds(0, ref.shape[0]), :]


def bands_kernel(widths_ref, early_ref, bands_ref):
    del early_ref
    shape = (bands_ref.shape[0], LANES)
    lag = lax.broadcasted_iota(jnp.int32, shape, 0) - lax.broadcasted_iota(jnp.int32, shape, 1)
    for at in range(widths_ref.shape[0]):
        band = jnp.where((lag >= 0) & (lag < widths_ref[at]), 1.0, 0.0)
        bands_ref[:, pl.ds(at * LANES, LANES)] = band.astype(jnp.bfloat16)


def boxcars_kernel(scale, widths_ref, bands_ref, sums_ref, later_ref, out_ref, values, mixed, sems):
    trials = sums_ref.shape[1]
    length = sums_ref.shape[0] - REACH
    filters = widths_ref.shape[0]
    whole = length - REACH
    total = jnp.concatenate(
        [
            sums_ref[pl.ds(REACH, whole), :],
            sums_ref[pl.ds(length, REACH), :] + later_ref[pl.ds(0, REACH), :],
            later_ref[pl.ds(REACH, WMAX), :],
        ],
        axis=0,
    )
    for first in range(0, length + WMAX, LANES):
        tile = (total[first : first + LANES] * scale).T
        values[:, pl.ds(first, LANES)] = tile.astype(jnp.bfloat16)
    parts, pieces = sems.shape
    share = trials // pieces
    widths = [jnp.full((1, LANES), widths_ref[at], jnp.int32).astype(jnp.float32) for at in range(filters)]
    shares = [1.0 / jnp.sqrt(width) for width in widths]
    tiles = mixed.reshape(parts, trials, filters, LANES)
    copies = []
    for piece in range(pieces):
        some = pl.ds(piece * share, share)
        windows = [values[some, pl.ds(part * LANES, LANES + WMAX)] for part in range(parts)]
        sums = jnp.dot(jnp.concatenate(windows, axis=0), bands_ref[...], preferred_element_type=jnp.float32)
        for part in range(parts):
            for at in range(filters):
                mixed[part, pl.ds(piece * share * filters + at, share, stride=filters), :] = (
                    sums[part * share : (part + 1) * share, at * LANES : (at + 1) * LANES] * shares[at]
                )
            target = out_ref.at[some, :, pl.ds(part * LANES, LANES)]
            copies.append(pltpu.make_async_copy(tiles.at[part, some], target, sems.at[part, piece]))
            copies[-1].start()
    for copy in copies:
        copy.wait()


def call(kernel, out_shape, in_specs, args, scratch=(), flops=0, **options):
    several = isinstance(out_shape, list)
    options.setdefault("out_specs", [VMEM] * len(out_shape) if several else VMEM)
    return pl.pallas_call(
        kernel,
        out_shape=out_shape,
        in_specs=in_specs,
        scratch_shapes=list(scratch),
        compiler_params=pltpu.CompilerParams(vmem_limit_bytes=16 << 20),
        cost_estimate=pl.CostEstimate(flops=flops, bytes_accessed=1 << 20, transcendentals=0),
        **options,
    )(*args)


def one_beam(own, delays, offsets, me, widths, groups, outer, per_sub, scale):
    chans, length = own.shape
    padded, all_subs = offsets.shape
    sub_dev = chans // per_sub
    inner = groups // outer
    filters = widths.shape[0]
    span = length + DCH
    packed = 2 * sub_dev == LANES
    series_shape = (-(-span // 32) * 16, LANES) if packed else (sub_dev, length + LANES)
    steps = 4
    series, fetched = call(
        functools.partial(series_kernel, per_sub, packed),
        [
            jax.ShapeDtypeStruct(series_shape, jnp.bfloat16),
            jax.ShapeDtypeStruct((padded, all_subs), jnp.int32),
        ],
        [HBM, HBM, HBM],
        tuple(pltpu.with_memory_space_constraint(x, pltpu.HBM) for x in (delays[None, :], own, offsets)),
        [
            pltpu.VMEM((1, chans), jnp.int32),
            pltpu.VMEM((chans, length), jnp.bfloat16),
            pltpu.SemaphoreType.DMA,
            pltpu.SemaphoreType.DMA((2 * steps,)),
        ],
    )
    line = [series] + [exchanged(series, "sub", flip * inner) for flip in range(1, outer)]
    nsub = outer * sub_dev
    table = call(offsets_kernel, jax.ShapeDtypeStruct((all_subs, padded), jnp.float32), [VMEM], (fetched,))
    joined = call(
        functools.partial(join_packed_kernel if packed else join_kernel, outer),
        jax.ShapeDtypeStruct((span, nsub), jnp.bfloat16),
        [VMEM] * outer + [ANY],
        (*line, table),
    )
    blocks = [joined] + [exchanged(joined, "sub", flip) for flip in range(1, inner)]
    scratch = [
        pltpu.VMEM((span + 2 * STEP, nsub), jnp.float32),
        pltpu.VMEM((span + STEP, (STEP + 1) * nsub), jnp.bfloat16),
        pltpu.VMEM((nsub, padded), jnp.float32),
        *[pltpu.VMEM((span + STEP, 2 * padded), jnp.float32)] * (GROUPS // 2),
    ]
    flops = 2 * (span + STEP) * nsub * padded * (OMAX + 2)
    sums_shape = jax.ShapeDtypeStruct((length + REACH, padded), jnp.float32)
    early_shape = jax.ShapeDtypeStruct((REACH + WMAX, padded), jnp.float32)
    given = ()
    for flip in (0, *range(inner - 1, 0, -1)):
        sums, *early = call(
            functools.partial(sums_kernel, flip > 0, outer, inner, flip),
            [sums_shape, early_shape] if flip == 1 else [sums_shape],
            [SMEM] + [VMEM] * (2 + len(given)),
            (me, blocks[flip], table, *given),
            scratch,
            flops,
        )
        given = (sums,)
    early = early[0]
    later = passed_back(early, "tm")
    bands = call(
        bands_kernel,
        jax.ShapeDtypeStruct((LANES + WMAX, filters * LANES), jnp.bfloat16),
        [SMEM, ANY],
        (widths, early),
    )
    parts = length // LANES
    pieces = 2
    return call(
        functools.partial(boxcars_kernel, scale),
        jax.ShapeDtypeStruct((padded, filters, length), jnp.float32),
        [SMEM, VMEM, VMEM, VMEM],
        (widths, bands, sums, later),
        [
            pltpu.VMEM((padded, length + WMAX), jnp.bfloat16),
            pltpu.VMEM((parts, padded * filters, LANES), jnp.float32),
            pltpu.SemaphoreType.DMA((parts, pieces)),
        ],
        out_specs=HBM,
    )


def per_device(data, delays, offsets, widths):
    beams, chans, length = data.shape
    trials, nsub = offsets.shape
    groups = lax.axis_size("sub")
    outer = 1 << (groups.bit_length() // 2)
    outer = outer if groups % (outer * outer) == 0 else outer // 2
    per_sub = chans // (nsub // groups)
    scale = 1.0 / math.sqrt(chans * groups)
    padded = max(trials, LANES)
    table = jnp.pad(offsets, ((0, padded - trials), (0, 0))) if padded > trials else offsets
    me = lax.axis_index("sub").astype(jnp.int32).reshape(1)
    outs = [
        one_beam(data[beam], delays, table, me, widths, groups, outer, per_sub, scale)[:trials, None]
        for beam in range(beams)
    ]
    return outs[0] if beams == 1 else jnp.concatenate(outs, axis=1)


def solution(mesh):
    placed = (P(None, "sub", "tm"), P("sub"), P("sub", None), P())
    return jax.shard_map(
        per_device,
        mesh=mesh,
        in_specs=placed,
        out_specs=P("sub", None, None, "tm"),
        check_vma=False,
    )
```

```python
import functools
import math

import jax
import jax.numpy as jnp
from jax import lax
from jax.experimental import pallas as pl
from jax.experimental.pallas import tpu as pltpu
from jax.sharding import PartitionSpec as P

WMAX = 128
DCH = 16
OMAX = 96
LANES = 128
STEP = 16
GROUPS = OMAX // STEP
TOGETHER = 1
REACH = OMAX + DCH
VMEM = pl.BlockSpec(memory_space=pltpu.VMEM)
SMEM = pl.BlockSpec(memory_space=pltpu.SMEM)
HBM = pl.BlockSpec(memory_space=pltpu.HBM)
ANY = pl.BlockSpec(memory_space=pl.ANY)


def passed_back(value, axis):
    count = lax.axis_size(axis)
    return lax.ppermute(value, axis, [(source, source - 1) for source in range(1, count)])


def exchanged(value, axis, flip):
    count = lax.axis_size(axis)
    return lax.ppermute(value, axis, [(source, source ^ flip) for source in range(count)])


def series_kernel(
    per_sub, packed, delays_ref, data_ref, offsets_ref, series_ref, fetched_ref, delays, held, delays_sem, sems
):
    chans, length = data_ref.shape
    block = min(chans, 256)
    subs = block // per_sub
    wide = length + LANES
    first_copy = pltpu.make_async_copy(delays_ref, delays, delays_sem)
    first_copy.start()
    copies = []
    steps = sems.shape[0] // 2
    for source, target, base in ((data_ref, held, 0), (offsets_ref, fetched_ref, steps)):
        share = source.shape[0] // steps
        for at in range(steps):
            here = pl.ds(at * share, share)
            copies.append(
                pltpu.make_async_copy(source.at[here, :], target.at[here, :], sems.at[base + at])
            )
            copies[-1].start()
    rows = lax.broadcasted_iota(jnp.int32, (DCH * subs, block), 0)
    owner = lax.broadcasted_iota(jnp.int32, (1, block), 1) // per_sub
    blank = jnp.zeros((subs, LANES), jnp.float32)
    first_copy.wait()
    members = [
        jnp.where(rows == delays[:, at * block : (at + 1) * block] * subs + owner, 1.0, 0.0).astype(jnp.bfloat16)
        for at in range(chans // block)
    ]
    for copy in copies[:steps]:
        copy.wait()
    parts = []
    for at, member in enumerate(members):
        picked = jnp.dot(member, held[pl.ds(at * block, block), :], preferred_element_type=jnp.float32)
        total = None
        for delay in range(DCH):
            late = jnp.concatenate([picked[delay * subs : (delay + 1) * subs, :], blank], axis=1)
            late = pltpu.roll(late, DCH - delay, 1)
            total = late if total is None else total + late
        parts.append(total)
    total = jnp.concatenate(parts, axis=0)
    if packed:
        half = series_ref.shape[0]
        both = jnp.concatenate([total, pltpu.roll(total, wide - half, 1)], axis=0)
        for first in range(0, half, LANES):
            count = min(LANES, half - first)
            tile = both[:, first : first + LANES].T
            series_ref[pl.ds(first, count), :] = tile[:count].astype(jnp.bfloat16)
    else:
        series_ref[...] = total.astype(jnp.bfloat16)
    for copy in copies[steps:]:
        copy.wait()


def join_packed_kernel(outer, *refs):
    blocks, joined_ref = refs[:outer], refs[-1]
    half = blocks[0].shape[0]
    rest = joined_ref.shape[0] - half
    lane = lax.broadcasted_iota(jnp.int32, (half, LANES), 1)
    for at in range(outer // 2):
        left = blocks[2 * at][...].astype(jnp.float32)
        right = blocks[2 * at + 1][...].astype(jnp.float32)
        lanes = pl.ds(at * LANES, LANES)
        early = jnp.where(lane < LANES // 2, left, pltpu.roll(right, LANES // 2, 1))
        late = jnp.where(lane < LANES // 2, pltpu.roll(left, LANES // 2, 1), right)
        joined_ref[pl.ds(0, half), lanes] = early.astype(jnp.bfloat16)
        joined_ref[pl.ds(half, rest), lanes] = late[:rest].astype(jnp.bfloat16)


def join_kernel(outer, *refs):
    blocks, joined_ref = refs[:outer], refs[-1]
    subs = blocks[0].shape[0]
    rows = joined_ref.shape[0]
    several = LANES // subs
    for at in range(outer // several):
        for first in range(0, rows, LANES):
            count = min(LANES, rows - first)
            tile = jnp.concatenate(
                [
                    blocks[at * several + slot][:, pl.ds(first, LANES)].astype(jnp.float32)
                    for slot in range(several)
                ],
                axis=0,
            ).T
            joined_ref[pl.ds(first, count), pl.ds(at * LANES, LANES)] = tile[:count].astype(jnp.bfloat16)


def offsets_kernel(offsets_ref, table_ref):
    for at in range(offsets_ref.shape[1] // LANES):
        here = pl.ds(at * LANES, LANES)
        table_ref[here, :] = offsets_ref[:, here].astype(jnp.float32).T


def slot_start(slot, flip, outer, inner, subs, me):
    return pl.multiple_of((((me // inner) ^ slot) * inner + ((me % inner) ^ flip)) * subs, subs)


def add_pair(total, pair, both):
    rows, trials = both.shape[0], both.shape[1] // 2
    for odd in range(2):
        first = STEP * (GROUPS - 1 - 2 * pair - odd)
        total[pl.ds(first, rows), :] += both[:, odd * trials : (odd + 1) * trials]


def sums_kernel(given, here, outer, inner, flip, me_ref, joined_ref, table_ref, *refs):
    pairs = GROUPS // 2
    before_ref, sums_ref, *early_ref = refs[: -3 - pairs] if given else (None, *refs[: -3 - pairs])
    moving, shifted, table = refs[-3 - pairs : -pairs]
    totals = refs[-pairs:]
    if before_ref is None:
        sums_ref[...] = jnp.zeros_like(sums_ref)
    else:
        sums_ref[...] = before_ref[...]

    def add_block():
        span, nsub = joined_ref.shape
        subs = nsub // outer
        for slot in range(outer):
            start = slot_start(slot, flip, outer, inner, subs, me_ref[0])
            table[pl.ds(slot * subs, subs), :] = table_ref[pl.ds(start, subs), :]
        blank = jnp.zeros((STEP, nsub), jnp.float32)
        moving[pl.ds(0, STEP), :] = blank
        moving[pl.ds(STEP, span), :] = joined_ref[...].astype(jnp.float32)
        moving[pl.ds(STEP + span, STEP), :] = blank

        def shift(lag):
            shifted[:, pl.ds(lag * nsub, nsub)] = moving[pl.ds(lag, span + STEP), :].astype(jnp.bfloat16)

        def tile(lag, pair):
            halves = [
                jnp.where(table[...] == float(STEP * (2 * pair + odd) + lag), 1.0, 0.0).astype(jnp.bfloat16)
                if lag < STEP or odd
                else jnp.zeros(table.shape, jnp.bfloat16)
                for odd in range(2)
            ]
            return jnp.concatenate(halves, axis=1)

        for lag in range(TOGETHER):
            shift(lag)
        for first in range(0, STEP + 1, TOGETHER):
            lags = range(first, min(first + TOGETHER, STEP + 1))
            for lag in range(first + TOGETHER, min(first + 2 * TOGETHER, STEP + 1)):
                shift(lag)
            for pair in range(pairs - 1 if first == STEP else 0, pairs):
                both = jnp.dot(
                    shifted[:, pl.ds(first * nsub, len(lags) * nsub)],
                    jnp.concatenate([tile(lag, pair) for lag in lags], axis=0),
                    preferred_element_type=jnp.float32,
                )
                if first:
                    totals[pair][...] += both
                else:
                    totals[pair][...] = both
        for pair in range(pairs):
            add_pair(sums_ref, pair, totals[pair][...])

    if here is None:
        add_block()
    else:
        pl.when(here(me_ref[1]))(add_block)
    for ref in early_ref:
        ref[...] = sums_ref[pl.ds(0, ref.shape[0]), :]


def bands_kernel(widths_ref, bands_ref):
    shape = (bands_ref.shape[0], LANES)
    lag = lax.broadcasted_iota(jnp.int32, shape, 0) - lax.broadcasted_iota(jnp.int32, shape, 1)
    for at in range(widths_ref.shape[0]):
        band = jnp.where((lag >= 0) & (lag < widths_ref[at]), 1.0, 0.0)
        bands_ref[:, pl.ds(at * LANES, LANES)] = band.astype(jnp.bfloat16)


def boxcars_kernel(scale, widths_ref, bands_ref, sums_ref, later_ref, out_ref, values, mixed, sems):
    trials = sums_ref.shape[1]
    length = sums_ref.shape[0] - REACH
    filters = widths_ref.shape[0]
    whole = length - REACH
    total = jnp.concatenate(
        [
            sums_ref[pl.ds(REACH, whole), :],
            sums_ref[pl.ds(length, REACH), :] + later_ref[pl.ds(0, REACH), :],
            later_ref[pl.ds(REACH, WMAX), :],
        ],
        axis=0,
    )
    for first in range(0, length + WMAX, LANES):
        tile = (total[first : first + LANES] * scale).T
        values[:, pl.ds(first, LANES)] = tile.astype(jnp.bfloat16)
    parts, pieces = sems.shape
    share = trials // pieces
    widths = [jnp.full((1, LANES), widths_ref[at], jnp.int32).astype(jnp.float32) for at in range(filters)]
    shares = [1.0 / jnp.sqrt(width) for width in widths]
    tiles = mixed.reshape(parts, trials, filters, LANES)
    copies = []
    for piece in range(pieces):
        some = pl.ds(piece * share, share)
        windows = [values[some, pl.ds(part * LANES, LANES + WMAX)] for part in range(parts)]
        sums = jnp.dot(jnp.concatenate(windows, axis=0), bands_ref[...], preferred_element_type=jnp.float32)
        for part in range(parts):
            for at in range(filters):
                mixed[part, pl.ds(piece * share * filters + at, share, stride=filters), :] = (
                    sums[part * share : (part + 1) * share, at * LANES : (at + 1) * LANES] * shares[at]
                )
            target = out_ref.at[some, :, pl.ds(part * LANES, LANES)]
            copies.append(pltpu.make_async_copy(tiles.at[part, some], target, sems.at[part, piece]))
            copies[-1].start()
    for copy in copies:
        copy.wait()


def call(kernel, out_shape, in_specs, args, scratch=(), flops=0, **options):
    several = isinstance(out_shape, list)
    options.setdefault("out_specs", [VMEM] * len(out_shape) if several else VMEM)
    return pl.pallas_call(
        kernel,
        out_shape=out_shape,
        in_specs=in_specs,
        scratch_shapes=list(scratch),
        compiler_params=pltpu.CompilerParams(vmem_limit_bytes=16 << 20),
        cost_estimate=pl.CostEstimate(flops=flops, bytes_accessed=1 << 20, transcendentals=0),
        **options,
    )(*args)


def one_beam(own, delays, offsets, me, widths, groups, outer, per_sub, scale):
    chans, length = own.shape
    padded, all_subs = offsets.shape
    sub_dev = chans // per_sub
    inner = groups // outer
    filters = widths.shape[0]
    span = length + DCH
    packed = 2 * sub_dev == LANES
    series_shape = (-(-span // 32) * 16, LANES) if packed else (sub_dev, length + LANES)
    steps = 4
    series, fetched = call(
        functools.partial(series_kernel, per_sub, packed),
        [
            jax.ShapeDtypeStruct(series_shape, jnp.bfloat16),
            jax.ShapeDtypeStruct((padded, all_subs), jnp.int32),
        ],
        [HBM, HBM, HBM],
        tuple(pltpu.with_memory_space_constraint(x, pltpu.HBM) for x in (delays[None, :], own, offsets)),
        [
            pltpu.VMEM((1, chans), jnp.int32),
            pltpu.VMEM((chans, length), jnp.bfloat16),
            pltpu.SemaphoreType.DMA,
            pltpu.SemaphoreType.DMA((2 * steps,)),
        ],
    )
    line = [series] + [exchanged(series, "sub", flip * inner) for flip in range(1, outer)]
    nsub = outer * sub_dev
    table = call(offsets_kernel, jax.ShapeDtypeStruct((all_subs, padded), jnp.float32), [VMEM], (fetched,))
    bands = call(
        bands_kernel,
        jax.ShapeDtypeStruct((LANES + WMAX, filters * LANES), jnp.bfloat16),
        [SMEM],
        (widths,),
    )
    joined = call(
        functools.partial(join_packed_kernel if packed else join_kernel, outer),
        jax.ShapeDtypeStruct((span, nsub), jnp.bfloat16),
        [VMEM] * outer + [ANY] * 2,
        (*line, table, bands),
    )
    blocks = [joined] + [exchanged(joined, "sub", flip) for flip in range(1, inner)]
    scratch = [
        pltpu.VMEM((span + 2 * STEP, nsub), jnp.float32),
        pltpu.VMEM((span + STEP, (STEP + 1) * nsub), jnp.bfloat16),
        pltpu.VMEM((nsub, padded), jnp.float32),
        *[pltpu.VMEM((span + STEP, 2 * padded), jnp.float32)] * (GROUPS // 2),
    ]
    flops = 2 * (span + STEP) * nsub * padded * (OMAX + 2)
    sums_shape = jax.ShapeDtypeStruct((length + REACH, padded), jnp.float32)
    early_shape = jax.ShapeDtypeStruct((REACH + WMAX, padded), jnp.float32)
    steps = [(flip, None) for flip in range(inner - 1)]
    steps += [(inner - 1, lambda tm: tm > 0), (inner - 1, lambda tm: tm == 0)]
    given = ()
    for at, (flip, here) in enumerate(steps):
        sums, *rest = call(
            functools.partial(sums_kernel, at > 0, here, outer, inner, flip),
            [sums_shape, early_shape] if at == inner - 1 else [sums_shape],
            [SMEM] + [VMEM] * (2 + len(given)),
            (me, blocks[flip], table, *given),
            scratch,
            flops,
        )
        given = (sums,)
        if rest:
            later = passed_back(rest[0], "tm")
    parts = length // LANES
    pieces = 2
    return call(
        functools.partial(boxcars_kernel, scale),
        jax.ShapeDtypeStruct((padded, filters, length), jnp.float32),
        [SMEM, VMEM, VMEM, VMEM],
        (widths, bands, sums, later),
        [
            pltpu.VMEM((padded, length + WMAX), jnp.bfloat16),
            pltpu.VMEM((parts, padded * filters, LANES), jnp.float32),
            pltpu.SemaphoreType.DMA((parts, pieces)),
        ],
        out_specs=HBM,
    )


def per_device(data, delays, offsets, widths):
    beams, chans, length = data.shape
    trials, nsub = offsets.shape
    groups = lax.axis_size("sub")
    outer = 1 << (groups.bit_length() // 2)
    outer = outer if groups % (outer * outer) == 0 else outer // 2
    per_sub = chans // (nsub // groups)
    scale = 1.0 / math.sqrt(chans * groups)
    padded = max(trials, LANES)
    table = jnp.pad(offsets, ((0, padded - trials), (0, 0))) if padded > trials else offsets
    me = jnp.stack([lax.axis_index("sub"), lax.axis_index("tm")]).astype(jnp.int32)
    outs = [
        one_beam(data[beam], delays, table, me, widths, groups, outer, per_sub, scale)[:trials, None]
        for beam in range(beams)
    ]
    return outs[0] if beams == 1 else jnp.concatenate(outs, axis=1)


def solution(mesh):
    placed = (P(None, "sub", "tm"), P("sub"), P("sub", None), P())
    return jax.shard_map(
        per_device,
        mesh=mesh,
        in_specs=placed,
        out_specs=P("sub", None, None, "tm"),
        check_vma=False,
    )
```

```python
import functools
import math

import jax
import jax.numpy as jnp
from jax import lax
from jax.experimental import pallas as pl
from jax.experimental.pallas import tpu as pltpu
from jax.sharding import PartitionSpec as P

WMAX = 128
DCH = 16
OMAX = 96
LANES = 128
STEP = 16
GROUPS = OMAX // STEP
TOGETHER = 1
REACH = OMAX + DCH
VMEM = pl.BlockSpec(memory_space=pltpu.VMEM)
SMEM = pl.BlockSpec(memory_space=pltpu.SMEM)
HBM = pl.BlockSpec(memory_space=pltpu.HBM)
ANY = pl.BlockSpec(memory_space=pl.ANY)


def passed_back(value, axis):
    count = lax.axis_size(axis)
    return lax.ppermute(value, axis, [(source, source - 1) for source in range(1, count)])


def exchanged(value, axis, flip):
    count = lax.axis_size(axis)
    return lax.ppermute(value, axis, [(source, source ^ flip) for source in range(count)])


def series_kernel(
    per_sub, packed, delays_ref, data_ref, offsets_ref, series_ref, fetched_ref, delays, held, delays_sem, sems
):
    chans, length = data_ref.shape
    block = min(chans, 256)
    subs = block // per_sub
    wide = length + LANES
    first_copy = pltpu.make_async_copy(delays_ref, delays, delays_sem)
    first_copy.start()
    copies = []
    steps = sems.shape[0] // 2
    for source, target, base in ((data_ref, held, 0), (offsets_ref, fetched_ref, steps)):
        share = source.shape[0] // steps
        for at in range(steps):
            here = pl.ds(at * share, share)
            copies.append(
                pltpu.make_async_copy(source.at[here, :], target.at[here, :], sems.at[base + at])
            )
            copies[-1].start()
    rows = lax.broadcasted_iota(jnp.int32, (DCH * subs, block), 0)
    owner = lax.broadcasted_iota(jnp.int32, (1, block), 1) // per_sub
    blank = jnp.zeros((subs, LANES), jnp.float32)
    first_copy.wait()
    members = [
        jnp.where(rows == delays[:, at * block : (at + 1) * block] * subs + owner, 1.0, 0.0).astype(jnp.bfloat16)
        for at in range(chans // block)
    ]
    for copy in copies[:steps]:
        copy.wait()
    parts = []
    for at, member in enumerate(members):
        picked = jnp.dot(member, held[pl.ds(at * block, block), :], preferred_element_type=jnp.float32)
        total = None
        for delay in range(DCH):
            late = jnp.concatenate([picked[delay * subs : (delay + 1) * subs, :], blank], axis=1)
            late = pltpu.roll(late, DCH - delay, 1)
            total = late if total is None else total + late
        parts.append(total)
    total = jnp.concatenate(parts, axis=0)
    if packed:
        half = series_ref.shape[0]
        both = jnp.concatenate([total, pltpu.roll(total, wide - half, 1)], axis=0)
        for first in range(0, half, LANES):
            count = min(LANES, half - first)
            tile = both[:, first : first + LANES].T
            series_ref[pl.ds(first, count), :] = tile[:count].astype(jnp.bfloat16)
    else:
        series_ref[...] = total.astype(jnp.bfloat16)
    for copy in copies[steps:]:
        copy.wait()


def join_packed_kernel(outer, *refs):
    blocks, joined_ref = refs[:outer], refs[-1]
    half = blocks[0].shape[0]
    rest = joined_ref.shape[0] - half
    lane = lax.broadcasted_iota(jnp.int32, (half, LANES), 1)
    for at in range(outer // 2):
        left = blocks[2 * at][...].astype(jnp.float32)
        right = blocks[2 * at + 1][...].astype(jnp.float32)
        lanes = pl.ds(at * LANES, LANES)
        early = jnp.where(lane < LANES // 2, left, pltpu.roll(right, LANES // 2, 1))
        late = jnp.where(lane < LANES // 2, pltpu.roll(left, LANES // 2, 1), right)
        joined_ref[pl.ds(0, half), lanes] = early.astype(jnp.bfloat16)
        joined_ref[pl.ds(half, rest), lanes] = late[:rest].astype(jnp.bfloat16)


def join_kernel(outer, *refs):
    blocks, joined_ref = refs[:outer], refs[-1]
    subs = blocks[0].shape[0]
    rows = joined_ref.shape[0]
    several = LANES // subs
    for at in range(outer // several):
        for first in range(0, rows, LANES):
            count = min(LANES, rows - first)
            tile = jnp.concatenate(
                [
                    blocks[at * several + slot][:, pl.ds(first, LANES)].astype(jnp.float32)
                    for slot in range(several)
                ],
                axis=0,
            ).T
            joined_ref[pl.ds(first, count), pl.ds(at * LANES, LANES)] = tile[:count].astype(jnp.bfloat16)


def offsets_kernel(offsets_ref, table_ref):
    for at in range(offsets_ref.shape[1] // LANES):
        here = pl.ds(at * LANES, LANES)
        table_ref[here, :] = offsets_ref[:, here].astype(jnp.float32).T


def slot_start(slot, flip, outer, inner, subs, me):
    return pl.multiple_of((((me // inner) ^ slot) * inner + ((me % inner) ^ flip)) * subs, subs)


def add_pair(total, pair, both):
    rows, trials = both.shape[0], both.shape[1] // 2
    for odd in range(2):
        first = STEP * (GROUPS - 1 - 2 * pair - odd)
        total[pl.ds(first, rows), :] += both[:, odd * trials : (odd + 1) * trials]


def sums_kernel(given, here, outer, inner, flip, me_ref, tm_ref, joined_ref, table_ref, *refs):
    pairs = GROUPS // 2
    before_ref, sums_ref, *early_ref = refs[: -3 - pairs] if given else (None, *refs[: -3 - pairs])
    moving, shifted, table = refs[-3 - pairs : -pairs]
    totals = refs[-pairs:]
    if before_ref is None:
        sums_ref[...] = jnp.zeros_like(sums_ref)
    else:
        sums_ref[...] = before_ref[...]

    def add_block():
        span, nsub = joined_ref.shape
        subs = nsub // outer
        for slot in range(outer):
            start = slot_start(slot, flip, outer, inner, subs, me_ref[0])
            table[pl.ds(slot * subs, subs), :] = table_ref[pl.ds(start, subs), :]
        blank = jnp.zeros((STEP, nsub), jnp.float32)
        moving[pl.ds(0, STEP), :] = blank
        moving[pl.ds(STEP, span), :] = joined_ref[...].astype(jnp.float32)
        moving[pl.ds(STEP + span, STEP), :] = blank

        def shift(lag):
            shifted[:, pl.ds(lag * nsub, nsub)] = moving[pl.ds(lag, span + STEP), :].astype(jnp.bfloat16)

        def tile(lag, pair):
            halves = [
                jnp.where(table[...] == float(STEP * (2 * pair + odd) + lag), 1.0, 0.0).astype(jnp.bfloat16)
                if lag < STEP or odd
                else jnp.zeros(table.shape, jnp.bfloat16)
                for odd in range(2)
            ]
            return jnp.concatenate(halves, axis=1)

        for lag in range(TOGETHER):
            shift(lag)
        for first in range(0, STEP + 1, TOGETHER):
            lags = range(first, min(first + TOGETHER, STEP + 1))
            for lag in range(first + TOGETHER, min(first + 2 * TOGETHER, STEP + 1)):
                shift(lag)
            for pair in range(pairs - 1 if first == STEP else 0, pairs):
                both = jnp.dot(
                    shifted[:, pl.ds(first * nsub, len(lags) * nsub)],
                    jnp.concatenate([tile(lag, pair) for lag in lags], axis=0),
                    preferred_element_type=jnp.float32,
                )
                if first:
                    totals[pair][...] += both
                else:
                    totals[pair][...] = both
        for pair in range(pairs):
            add_pair(sums_ref, pair, totals[pair][...])

    if here is None:
        add_block()
    else:
        pl.when(here(tm_ref[0]))(add_block)
    for ref in early_ref:
        ref[...] = sums_ref[pl.ds(0, ref.shape[0]), :]


def bands_kernel(widths_ref, bands_ref):
    shape = (bands_ref.shape[0], LANES)
    lag = lax.broadcasted_iota(jnp.int32, shape, 0) - lax.broadcasted_iota(jnp.int32, shape, 1)
    for at in range(widths_ref.shape[0]):
        band = jnp.where((lag >= 0) & (lag < widths_ref[at]), 1.0, 0.0)
        bands_ref[:, pl.ds(at * LANES, LANES)] = band.astype(jnp.bfloat16)


def boxcars_kernel(scale, widths_ref, bands_ref, sums_ref, later_ref, out_ref, values, mixed, sems):
    trials = sums_ref.shape[1]
    length = sums_ref.shape[0] - REACH
    filters = widths_ref.shape[0]
    whole = length - REACH
    total = jnp.concatenate(
        [
            sums_ref[pl.ds(REACH, whole), :],
            sums_ref[pl.ds(length, REACH), :] + later_ref[pl.ds(0, REACH), :],
            later_ref[pl.ds(REACH, WMAX), :],
        ],
        axis=0,
    )
    for first in range(0, length + WMAX, LANES):
        tile = (total[first : first + LANES] * scale).T
        values[:, pl.ds(first, LANES)] = tile.astype(jnp.bfloat16)
    parts, pieces = sems.shape
    share = trials // pieces
    widths = [jnp.full((1, LANES), widths_ref[at], jnp.int32).astype(jnp.float32) for at in range(filters)]
    shares = [1.0 / jnp.sqrt(width) for width in widths]
    tiles = mixed.reshape(parts, trials, filters, LANES)
    copies = []
    for piece in range(pieces):
        some = pl.ds(piece * share, share)
        windows = [values[some, pl.ds(part * LANES, LANES + WMAX)] for part in range(parts)]
        sums = jnp.dot(jnp.concatenate(windows, axis=0), bands_ref[...], preferred_element_type=jnp.float32)
        for part in range(parts):
            for at in range(filters):
                mixed[part, pl.ds(piece * share * filters + at, share, stride=filters), :] = (
                    sums[part * share : (part + 1) * share, at * LANES : (at + 1) * LANES] * shares[at]
                )
            target = out_ref.at[some, :, pl.ds(part * LANES, LANES)]
            copies.append(pltpu.make_async_copy(tiles.at[part, some], target, sems.at[part, piece]))
            copies[-1].start()
    for copy in copies:
        copy.wait()


def call(kernel, out_shape, in_specs, args, scratch=(), flops=0, **options):
    several = isinstance(out_shape, list)
    options.setdefault("out_specs", [VMEM] * len(out_shape) if several else VMEM)
    return pl.pallas_call(
        kernel,
        out_shape=out_shape,
        in_specs=in_specs,
        scratch_shapes=list(scratch),
        compiler_params=pltpu.CompilerParams(vmem_limit_bytes=16 << 20),
        cost_estimate=pl.CostEstimate(flops=flops, bytes_accessed=1 << 20, transcendentals=0),
        **options,
    )(*args)


def one_beam(own, delays, offsets, me, widths, groups, outer, per_sub, scale):
    chans, length = own.shape
    padded, all_subs = offsets.shape
    sub_dev = chans // per_sub
    inner = groups // outer
    filters = widths.shape[0]
    span = length + DCH
    packed = 2 * sub_dev == LANES
    series_shape = (-(-span // 32) * 16, LANES) if packed else (sub_dev, length + LANES)
    steps = 4
    series, fetched = call(
        functools.partial(series_kernel, per_sub, packed),
        [
            jax.ShapeDtypeStruct(series_shape, jnp.bfloat16),
            jax.ShapeDtypeStruct((padded, all_subs), jnp.int32),
        ],
        [HBM, HBM, HBM],
        tuple(pltpu.with_memory_space_constraint(x, pltpu.HBM) for x in (delays[None, :], own, offsets)),
        [
            pltpu.VMEM((1, chans), jnp.int32),
            pltpu.VMEM((chans, length), jnp.bfloat16),
            pltpu.SemaphoreType.DMA,
            pltpu.SemaphoreType.DMA((2 * steps,)),
        ],
    )
    line = [series] + [exchanged(series, "sub", flip * inner) for flip in range(1, outer)]
    nsub = outer * sub_dev
    table = call(offsets_kernel, jax.ShapeDtypeStruct((all_subs, padded), jnp.float32), [VMEM], (fetched,))
    bands = call(
        bands_kernel,
        jax.ShapeDtypeStruct((LANES + WMAX, filters * LANES), jnp.bfloat16),
        [SMEM],
        (widths,),
    )
    joined = call(
        functools.partial(join_packed_kernel if packed else join_kernel, outer),
        jax.ShapeDtypeStruct((span, nsub), jnp.bfloat16),
        [VMEM] * outer + [ANY] * 2,
        (*line, table, bands),
    )
    blocks = [joined] + [exchanged(joined, "sub", flip) for flip in range(1, inner)]
    scratch = [
        pltpu.VMEM((span + 2 * STEP, nsub), jnp.float32),
        pltpu.VMEM((span + STEP, (STEP + 1) * nsub), jnp.bfloat16),
        pltpu.VMEM((nsub, padded), jnp.float32),
        *[pltpu.VMEM((span + STEP, 2 * padded), jnp.float32)] * (GROUPS // 2),
    ]
    flops = 2 * (span + STEP) * nsub * padded * (OMAX + 2)
    sums_shape = jax.ShapeDtypeStruct((length + REACH, padded), jnp.float32)
    early_shape = jax.ShapeDtypeStruct((REACH + WMAX, padded), jnp.float32)
    steps = [(flip, None) for flip in range(inner - 1)]
    steps += [(inner - 1, lambda tm: tm > 0), (inner - 1, lambda tm: tm == 0)]
    given = ()
    for at, (flip, here) in enumerate(steps):
        sums, *rest = call(
            functools.partial(sums_kernel, at > 0, here, outer, inner, flip),
            [sums_shape, early_shape] if at == inner - 1 else [sums_shape],
            [SMEM] * 2 + [VMEM] * (2 + len(given)),
            (*me, blocks[flip], table, *given),
            scratch,
            flops,
        )
        given = (sums,)
        if rest:
            later = passed_back(rest[0], "tm")
    parts = length // LANES
    pieces = 2
    return call(
        functools.partial(boxcars_kernel, scale),
        jax.ShapeDtypeStruct((padded, filters, length), jnp.float32),
        [SMEM, VMEM, VMEM, VMEM],
        (widths, bands, sums, later),
        [
            pltpu.VMEM((padded, length + WMAX), jnp.bfloat16),
            pltpu.VMEM((parts, padded * filters, LANES), jnp.float32),
            pltpu.SemaphoreType.DMA((parts, pieces)),
        ],
        out_specs=HBM,
    )


def per_device(data, delays, offsets, widths):
    beams, chans, length = data.shape
    trials, nsub = offsets.shape
    groups = lax.axis_size("sub")
    outer = 1 << (groups.bit_length() // 2)
    outer = outer if groups % (outer * outer) == 0 else outer // 2
    per_sub = chans // (nsub // groups)
    scale = 1.0 / math.sqrt(chans * groups)
    padded = max(trials, LANES)
    table = jnp.pad(offsets, ((0, padded - trials), (0, 0))) if padded > trials else offsets
    me = [lax.axis_index(axis).astype(jnp.int32).reshape(1) for axis in ("sub", "tm")]
    outs = [
        one_beam(data[beam], delays, table, me, widths, groups, outer, per_sub, scale)[:trials, None]
        for beam in range(beams)
    ]
    return outs[0] if beams == 1 else jnp.concatenate(outs, axis=1)


def solution(mesh):
    placed = (P(None, "sub", "tm"), P("sub"), P("sub", None), P())
    return jax.shard_map(
        per_device,
        mesh=mesh,
        in_specs=placed,
        out_specs=P("sub", None, None, "tm"),
        check_vma=False,
    )
```

```python
import functools
import math

import jax
import jax.numpy as jnp
from jax import lax
from jax.experimental import pallas as pl
from jax.experimental.pallas import tpu as pltpu
from jax.sharding import PartitionSpec as P

WMAX = 128
DCH = 16
OMAX = 96
LANES = 128
STEP = 16
GROUPS = OMAX // STEP
TOGETHER = 1
REACH = OMAX + DCH
VMEM = pl.BlockSpec(memory_space=pltpu.VMEM)
SMEM = pl.BlockSpec(memory_space=pltpu.SMEM)
HBM = pl.BlockSpec(memory_space=pltpu.HBM)
ANY = pl.BlockSpec(memory_space=pl.ANY)


def passed_back(value, axis):
    count = lax.axis_size(axis)
    return lax.ppermute(value, axis, [(source, source - 1) for source in range(1, count)])


def exchanged(value, axis, flip):
    count = lax.axis_size(axis)
    return lax.ppermute(value, axis, [(source, source ^ flip) for source in range(count)])


def series_kernel(
    per_sub, packed, delays_ref, data_ref, offsets_ref, series_ref, fetched_ref, delays, held, delays_sem, sems
):
    chans, length = data_ref.shape
    block = min(chans, 256)
    subs = block // per_sub
    wide = length + LANES
    first_copy = pltpu.make_async_copy(delays_ref, delays, delays_sem)
    first_copy.start()
    copies = []
    steps = sems.shape[0] // 2
    for source, target, base in ((data_ref, held, 0), (offsets_ref, fetched_ref, steps)):
        share = source.shape[0] // steps
        for at in range(steps):
            here = pl.ds(at * share, share)
            copies.append(
                pltpu.make_async_copy(source.at[here, :], target.at[here, :], sems.at[base + at])
            )
            copies[-1].start()
    rows = lax.broadcasted_iota(jnp.int32, (DCH * subs, block), 0)
    owner = lax.broadcasted_iota(jnp.int32, (1, block), 1) // per_sub
    blank = jnp.zeros((subs, LANES), jnp.float32)
    first_copy.wait()
    members = [
        jnp.where(rows == delays[:, at * block : (at + 1) * block] * subs + owner, 1.0, 0.0).astype(jnp.bfloat16)
        for at in range(chans // block)
    ]
    for copy in copies[:steps]:
        copy.wait()
    parts = []
    for at, member in enumerate(members):
        picked = jnp.dot(member, held[pl.ds(at * block, block), :], preferred_element_type=jnp.float32)
        total = None
        for delay in range(DCH):
            late = jnp.concatenate([picked[delay * subs : (delay + 1) * subs, :], blank], axis=1)
            late = pltpu.roll(late, DCH - delay, 1)
            total = late if total is None else total + late
        parts.append(total)
    total = jnp.concatenate(parts, axis=0)
    if packed:
        half = series_ref.shape[0]
        both = jnp.concatenate([total, pltpu.roll(total, wide - half, 1)], axis=0)
        for first in range(0, half, LANES):
            count = min(LANES, half - first)
            tile = both[:, first : first + LANES].T
            series_ref[pl.ds(first, count), :] = tile[:count].astype(jnp.bfloat16)
    else:
        series_ref[...] = total.astype(jnp.bfloat16)
    for copy in copies[steps:]:
        copy.wait()


def join_packed_kernel(outer, *refs):
    blocks, joined_ref = refs[:outer], refs[-1]
    half = blocks[0].shape[0]
    rest = joined_ref.shape[0] - half
    lane = lax.broadcasted_iota(jnp.int32, (half, LANES), 1)
    for at in range(outer // 2):
        left = blocks[2 * at][...].astype(jnp.float32)
        right = blocks[2 * at + 1][...].astype(jnp.float32)
        lanes = pl.ds(at * LANES, LANES)
        early = jnp.where(lane < LANES // 2, left, pltpu.roll(right, LANES // 2, 1))
        late = jnp.where(lane < LANES // 2, pltpu.roll(left, LANES // 2, 1), right)
        joined_ref[pl.ds(0, half), lanes] = early.astype(jnp.bfloat16)
        joined_ref[pl.ds(half, rest), lanes] = late[:rest].astype(jnp.bfloat16)


def join_kernel(outer, *refs):
    blocks, joined_ref = refs[:outer], refs[-1]
    subs = blocks[0].shape[0]
    rows = joined_ref.shape[0]
    several = LANES // subs
    for at in range(outer // several):
        for first in range(0, rows, LANES):
            count = min(LANES, rows - first)
            tile = jnp.concatenate(
                [
                    blocks[at * several + slot][:, pl.ds(first, LANES)].astype(jnp.float32)
                    for slot in range(several)
                ],
                axis=0,
            ).T
            joined_ref[pl.ds(first, count), pl.ds(at * LANES, LANES)] = tile[:count].astype(jnp.bfloat16)


def offsets_kernel(offsets_ref, table_ref):
    for at in range(offsets_ref.shape[1] // LANES):
        here = pl.ds(at * LANES, LANES)
        table_ref[here, :] = offsets_ref[:, here].astype(jnp.float32).T


def slot_start(slot, flip, outer, inner, subs, me):
    return pl.multiple_of((((me // inner) ^ slot) * inner + ((me % inner) ^ flip)) * subs, subs)


def add_pair(total, pair, both):
    rows, trials = both.shape[0], both.shape[1] // 2
    for odd in range(2):
        first = STEP * (GROUPS - 1 - 2 * pair - odd)
        total[pl.ds(first, rows), :] += both[:, odd * trials : (odd + 1) * trials]


def sums_kernel(given, here, outer, inner, flip, me_ref, tm_ref, joined_ref, table_ref, *refs):
    pairs = GROUPS // 2
    before_ref, sums_ref, *early_ref = refs[: -3 - pairs] if given else (None, *refs[: -3 - pairs])
    moving, shifted, table = refs[-3 - pairs : -pairs]
    totals = refs[-pairs:]
    if before_ref is None:
        sums_ref[...] = jnp.zeros_like(sums_ref)
    else:
        sums_ref[...] = before_ref[...]

    def add_block():
        span, nsub = joined_ref.shape
        subs = nsub // outer
        for slot in range(outer):
            start = slot_start(slot, flip, outer, inner, subs, me_ref[0])
            table[pl.ds(slot * subs, subs), :] = table_ref[pl.ds(start, subs), :]
        blank = jnp.zeros((STEP, nsub), jnp.float32)
        moving[pl.ds(0, STEP), :] = blank
        moving[pl.ds(STEP, span), :] = joined_ref[...].astype(jnp.float32)
        moving[pl.ds(STEP + span, STEP), :] = blank

        def shift(lag):
            shifted[:, pl.ds(lag * nsub, nsub)] = moving[pl.ds(lag, span + STEP), :].astype(jnp.bfloat16)

        def tile(lag, pair):
            halves = [
                jnp.where(table[...] == float(STEP * (2 * pair + odd) + lag), 1.0, 0.0).astype(jnp.bfloat16)
                if lag < STEP or odd
                else jnp.zeros(table.shape, jnp.bfloat16)
                for odd in range(2)
            ]
            return jnp.concatenate(halves, axis=1)

        for lag in range(TOGETHER):
            shift(lag)
        for first in range(0, STEP + 1, TOGETHER):
            lags = range(first, min(first + TOGETHER, STEP + 1))
            for lag in range(first + TOGETHER, min(first + 2 * TOGETHER, STEP + 1)):
                shift(lag)
            for pair in range(pairs - 1 if first == STEP else 0, pairs):
                both = jnp.dot(
                    shifted[:, pl.ds(first * nsub, len(lags) * nsub)],
                    jnp.concatenate([tile(lag, pair) for lag in lags], axis=0),
                    preferred_element_type=jnp.float32,
                )
                if first:
                    totals[pair][...] += both
                else:
                    totals[pair][...] = both
        for pair in range(pairs):
            add_pair(sums_ref, pair, totals[pair][...])

    if here is None:
        add_block()
    else:
        pl.when(here(tm_ref[0]))(add_block)
    for ref in early_ref:
        ref[...] = sums_ref[pl.ds(0, ref.shape[0]), :]


def bands_kernel(widths_ref, bands_ref, shares_ref):
    shape = (bands_ref.shape[0], LANES)
    lag = lax.broadcasted_iota(jnp.int32, shape, 0) - lax.broadcasted_iota(jnp.int32, shape, 1)
    for at in range(widths_ref.shape[0]):
        band = jnp.where((lag >= 0) & (lag < widths_ref[at]), 1.0, 0.0)
        bands_ref[:, pl.ds(at * LANES, LANES)] = band.astype(jnp.bfloat16)
        width = jnp.full((1, LANES), widths_ref[at], jnp.int32).astype(jnp.float32)
        shares_ref[pl.ds(at, 1), :] = 1.0 / jnp.sqrt(width)


def boxcars_kernel(scale, shares_ref, bands_ref, sums_ref, later_ref, out_ref, values, mixed, sems):
    trials = sums_ref.shape[1]
    length = sums_ref.shape[0] - REACH
    filters = shares_ref.shape[0]
    whole = length - REACH
    total = jnp.concatenate(
        [
            sums_ref[pl.ds(REACH, whole), :],
            sums_ref[pl.ds(length, REACH), :] + later_ref[pl.ds(0, REACH), :],
            later_ref[pl.ds(REACH, WMAX), :],
        ],
        axis=0,
    )
    for first in range(0, length + WMAX, LANES):
        tile = (total[first : first + LANES] * scale).T
        values[:, pl.ds(first, LANES)] = tile.astype(jnp.bfloat16)
    parts, pieces = sems.shape
    share = trials // pieces
    shares = [shares_ref[pl.ds(at, 1), :] for at in range(filters)]
    tiles = mixed.reshape(parts, trials, filters, LANES)
    copies = []
    for piece in range(pieces):
        some = pl.ds(piece * share, share)
        windows = [values[some, pl.ds(part * LANES, LANES + WMAX)] for part in range(parts)]
        sums = jnp.dot(jnp.concatenate(windows, axis=0), bands_ref[...], preferred_element_type=jnp.float32)
        for part in range(parts):
            for at in range(filters):
                mixed[part, pl.ds(piece * share * filters + at, share, stride=filters), :] = (
                    sums[part * share : (part + 1) * share, at * LANES : (at + 1) * LANES] * shares[at]
                )
            target = out_ref.at[some, :, pl.ds(part * LANES, LANES)]
            copies.append(pltpu.make_async_copy(tiles.at[part, some], target, sems.at[part, piece]))
            copies[-1].start()
    for copy in copies:
        copy.wait()


def call(kernel, out_shape, in_specs, args, scratch=(), flops=0, **options):
    several = isinstance(out_shape, list)
    options.setdefault("out_specs", [VMEM] * len(out_shape) if several else VMEM)
    return pl.pallas_call(
        kernel,
        out_shape=out_shape,
        in_specs=in_specs,
        scratch_shapes=list(scratch),
        compiler_params=pltpu.CompilerParams(vmem_limit_bytes=16 << 20),
        cost_estimate=pl.CostEstimate(flops=flops, bytes_accessed=1 << 20, transcendentals=0),
        **options,
    )(*args)


def one_beam(own, delays, offsets, me, widths, groups, outer, per_sub, scale):
    chans, length = own.shape
    padded, all_subs = offsets.shape
    sub_dev = chans // per_sub
    inner = groups // outer
    filters = widths.shape[0]
    span = length + DCH
    packed = 2 * sub_dev == LANES
    series_shape = (-(-span // 32) * 16, LANES) if packed else (sub_dev, length + LANES)
    steps = 4
    series, fetched = call(
        functools.partial(series_kernel, per_sub, packed),
        [
            jax.ShapeDtypeStruct(series_shape, jnp.bfloat16),
            jax.ShapeDtypeStruct((padded, all_subs), jnp.int32),
        ],
        [HBM, HBM, HBM],
        tuple(pltpu.with_memory_space_constraint(x, pltpu.HBM) for x in (delays[None, :], own, offsets)),
        [
            pltpu.VMEM((1, chans), jnp.int32),
            pltpu.VMEM((chans, length), jnp.bfloat16),
            pltpu.SemaphoreType.DMA,
            pltpu.SemaphoreType.DMA((2 * steps,)),
        ],
    )
    line = [series] + [exchanged(series, "sub", flip * inner) for flip in range(1, outer)]
    nsub = outer * sub_dev
    table = call(offsets_kernel, jax.ShapeDtypeStruct((all_subs, padded), jnp.float32), [VMEM], (fetched,))
    bands, shares = call(
        bands_kernel,
        [
            jax.ShapeDtypeStruct((LANES + WMAX, filters * LANES), jnp.bfloat16),
            jax.ShapeDtypeStruct((filters, LANES), jnp.float32),
        ],
        [SMEM],
        (widths,),
    )
    joined = call(
        functools.partial(join_packed_kernel if packed else join_kernel, outer),
        jax.ShapeDtypeStruct((span, nsub), jnp.bfloat16),
        [VMEM] * outer + [ANY] * 2,
        (*line, table, bands),
    )
    blocks = [joined] + [exchanged(joined, "sub", flip) for flip in range(1, inner)]
    scratch = [
        pltpu.VMEM((span + 2 * STEP, nsub), jnp.float32),
        pltpu.VMEM((span + STEP, (STEP + 1) * nsub), jnp.bfloat16),
        pltpu.VMEM((nsub, padded), jnp.float32),
        *[pltpu.VMEM((span + STEP, 2 * padded), jnp.float32)] * (GROUPS // 2),
    ]
    flops = 2 * (span + STEP) * nsub * padded * (OMAX + 2)
    sums_shape = jax.ShapeDtypeStruct((length + REACH, padded), jnp.float32)
    early_shape = jax.ShapeDtypeStruct((REACH + WMAX, padded), jnp.float32)
    steps = [(flip, None) for flip in range(inner - 1)]
    steps += [(inner - 1, lambda tm: tm > 0), (inner - 1, lambda tm: tm == 0)]
    given = ()
    for at, (flip, here) in enumerate(steps):
        sums, *rest = call(
            functools.partial(sums_kernel, at > 0, here, outer, inner, flip),
            [sums_shape, early_shape] if at == inner - 1 else [sums_shape],
            [SMEM] * 2 + [VMEM] * (2 + len(given)),
            (*me, blocks[flip], table, *given),
            scratch,
            flops,
        )
        given = (sums,)
        if rest:
            later = passed_back(rest[0], "tm")
    parts = length // LANES
    pieces = 2
    return call(
        functools.partial(boxcars_kernel, scale),
        jax.ShapeDtypeStruct((padded, filters, length), jnp.float32),
        [VMEM] * 4,
        (shares, bands, sums, later),
        [
            pltpu.VMEM((padded, length + WMAX), jnp.bfloat16),
            pltpu.VMEM((parts, padded * filters, LANES), jnp.float32),
            pltpu.SemaphoreType.DMA((parts, pieces)),
        ],
        out_specs=HBM,
    )


def per_device(data, delays, offsets, widths):
    beams, chans, length = data.shape
    trials, nsub = offsets.shape
    groups = lax.axis_size("sub")
    outer = 1 << (groups.bit_length() // 2)
    outer = outer if groups % (outer * outer) == 0 else outer // 2
    per_sub = chans // (nsub // groups)
    scale = 1.0 / math.sqrt(chans * groups)
    padded = max(trials, LANES)
    table = jnp.pad(offsets, ((0, padded - trials), (0, 0))) if padded > trials else offsets
    me = [lax.axis_index(axis).astype(jnp.int32).reshape(1) for axis in ("sub", "tm")]
    outs = [
        one_beam(data[beam], delays, table, me, widths, groups, outer, per_sub, scale)[:trials, None]
        for beam in range(beams)
    ]
    return outs[0] if beams == 1 else jnp.concatenate(outs, axis=1)


def solution(mesh):
    placed = (P(None, "sub", "tm"), P("sub"), P("sub", None), P())
    return jax.shard_map(
        per_device,
        mesh=mesh,
        in_specs=placed,
        out_specs=P("sub", None, None, "tm"),
        check_vma=False,
    )
```

```python
import functools
import math

import jax
import jax.numpy as jnp
from jax import lax
from jax.experimental import pallas as pl
from jax.experimental.pallas import tpu as pltpu
from jax.sharding import PartitionSpec as P

WMAX = 128
DCH = 16
OMAX = 96
LANES = 128
STEP = 16
GROUPS = OMAX // STEP
TOGETHER = 2
REACH = OMAX + DCH
VMEM = pl.BlockSpec(memory_space=pltpu.VMEM)
SMEM = pl.BlockSpec(memory_space=pltpu.SMEM)
HBM = pl.BlockSpec(memory_space=pltpu.HBM)
ANY = pl.BlockSpec(memory_space=pl.ANY)


def passed_back(value, axis):
    count = lax.axis_size(axis)
    return lax.ppermute(value, axis, [(source, source - 1) for source in range(1, count)])


def exchanged(value, axis, flip):
    count = lax.axis_size(axis)
    return lax.ppermute(value, axis, [(source, source ^ flip) for source in range(count)])


def series_kernel(
    per_sub, packed, delays_ref, data_ref, offsets_ref, series_ref, fetched_ref, delays, held, delays_sem, sems
):
    chans, length = data_ref.shape
    block = min(chans, 256)
    subs = block // per_sub
    wide = length + LANES
    first_copy = pltpu.make_async_copy(delays_ref, delays, delays_sem)
    first_copy.start()
    copies = []
    steps = sems.shape[0] // 2
    for source, target, base in ((data_ref, held, 0), (offsets_ref, fetched_ref, steps)):
        share = source.shape[0] // steps
        for at in range(steps):
            here = pl.ds(at * share, share)
            copies.append(
                pltpu.make_async_copy(source.at[here, :], target.at[here, :], sems.at[base + at])
            )
            copies[-1].start()
    rows = lax.broadcasted_iota(jnp.int32, (DCH * subs, block), 0)
    owner = lax.broadcasted_iota(jnp.int32, (1, block), 1) // per_sub
    blank = jnp.zeros((subs, LANES), jnp.float32)
    first_copy.wait()
    members = [
        jnp.where(rows == delays[:, at * block : (at + 1) * block] * subs + owner, 1.0, 0.0).astype(jnp.bfloat16)
        for at in range(chans // block)
    ]
    for copy in copies[:steps]:
        copy.wait()
    parts = []
    for at, member in enumerate(members):
        picked = jnp.dot(member, held[pl.ds(at * block, block), :], preferred_element_type=jnp.float32)
        total = None
        for delay in range(DCH):
            late = jnp.concatenate([picked[delay * subs : (delay + 1) * subs, :], blank], axis=1)
            late = pltpu.roll(late, DCH - delay, 1)
            total = late if total is None else total + late
        parts.append(total)
    total = jnp.concatenate(parts, axis=0)
    if packed:
        half = series_ref.shape[0]
        both = jnp.concatenate([total, pltpu.roll(total, wide - half, 1)], axis=0)
        for first in range(0, half, LANES):
            count = min(LANES, half - first)
            tile = both[:, first : first + LANES].T
            series_ref[pl.ds(first, count), :] = tile[:count].astype(jnp.bfloat16)
    else:
        series_ref[...] = total.astype(jnp.bfloat16)
    for copy in copies[steps:]:
        copy.wait()


def join_packed_kernel(outer, *refs):
    blocks, joined_ref = refs[:outer], refs[-1]
    half = blocks[0].shape[0]
    rest = joined_ref.shape[0] - half
    lane = lax.broadcasted_iota(jnp.int32, (half, LANES), 1)
    for at in range(outer // 2):
        left = blocks[2 * at][...].astype(jnp.float32)
        right = blocks[2 * at + 1][...].astype(jnp.float32)
        lanes = pl.ds(at * LANES, LANES)
        early = jnp.where(lane < LANES // 2, left, pltpu.roll(right, LANES // 2, 1))
        late = jnp.where(lane < LANES // 2, pltpu.roll(left, LANES // 2, 1), right)
        joined_ref[pl.ds(0, half), lanes] = early.astype(jnp.bfloat16)
        joined_ref[pl.ds(half, rest), lanes] = late[:rest].astype(jnp.bfloat16)


def join_kernel(outer, *refs):
    blocks, joined_ref = refs[:outer], refs[-1]
    subs = blocks[0].shape[0]
    rows = joined_ref.shape[0]
    several = LANES // subs
    for at in range(outer // several):
        for first in range(0, rows, LANES):
            count = min(LANES, rows - first)
            tile = jnp.concatenate(
                [
                    blocks[at * several + slot][:, pl.ds(first, LANES)].astype(jnp.float32)
                    for slot in range(several)
                ],
                axis=0,
            ).T
            joined_ref[pl.ds(first, count), pl.ds(at * LANES, LANES)] = tile[:count].astype(jnp.bfloat16)


def offsets_kernel(offsets_ref, table_ref):
    for at in range(offsets_ref.shape[1] // LANES):
        here = pl.ds(at * LANES, LANES)
        table_ref[here, :] = offsets_ref[:, here].astype(jnp.float32).T


def slot_start(slot, flip, outer, inner, subs, me):
    return pl.multiple_of((((me // inner) ^ slot) * inner + ((me % inner) ^ flip)) * subs, subs)


def add_pair(total, pair, both):
    rows, trials = both.shape[0], both.shape[1] // 2
    for odd in range(2):
        first = STEP * (GROUPS - 1 - 2 * pair - odd)
        total[pl.ds(first, rows), :] += both[:, odd * trials : (odd + 1) * trials]


def sums_kernel(given, here, outer, inner, flip, me_ref, tm_ref, joined_ref, table_ref, *refs):
    pairs = GROUPS // 2
    before_ref, sums_ref, *early_ref = refs[:-3] if given else (None, *refs[:-3])
    moving, shifted, table = refs[-3:]
    if before_ref is None:
        sums_ref[...] = jnp.zeros_like(sums_ref)
    else:
        sums_ref[...] = before_ref[...]

    def add_block():
        span, nsub = joined_ref.shape
        subs = nsub // outer
        for slot in range(outer):
            start = slot_start(slot, flip, outer, inner, subs, me_ref[0])
            table[pl.ds(slot * subs, subs), :] = table_ref[pl.ds(start, subs), :]
        blank = jnp.zeros((STEP, nsub), jnp.float32)
        moving[pl.ds(0, STEP), :] = blank
        moving[pl.ds(STEP, span), :] = joined_ref[...].astype(jnp.float32)
        moving[pl.ds(STEP + span, STEP), :] = blank

        def shift(lag):
            shifted[:, pl.ds(lag * nsub, nsub)] = moving[pl.ds(lag, span + STEP), :].astype(jnp.bfloat16)

        def tile(lag, pair):
            halves = [
                jnp.where(table[...] == float(STEP * (2 * pair + odd) + lag), 1.0, 0.0).astype(jnp.bfloat16)
                if lag < STEP or odd
                else jnp.zeros(table.shape, jnp.bfloat16)
                for odd in range(2)
            ]
            return jnp.concatenate(halves, axis=1)

        for lag in range(TOGETHER):
            shift(lag)
        for first in range(0, STEP + 1, TOGETHER):
            lags = range(first, min(first + TOGETHER, STEP + 1))
            for lag in range(first + TOGETHER, min(first + 2 * TOGETHER, STEP + 1)):
                shift(lag)
            for pair in range(pairs - 1 if first == STEP else 0, pairs):
                both = jnp.dot(
                    shifted[:, pl.ds(first * nsub, len(lags) * nsub)],
                    jnp.concatenate([tile(lag, pair) for lag in lags], axis=0),
                    preferred_element_type=jnp.float32,
                )
                add_pair(sums_ref, pair, both)

    if here is None:
        add_block()
    else:
        pl.when(here(tm_ref[0]))(add_block)
    for ref in early_ref:
        ref[...] = sums_ref[pl.ds(0, ref.shape[0]), :]


def bands_kernel(widths_ref, bands_ref, shares_ref):
    shape = (bands_ref.shape[0], LANES)
    lag = lax.broadcasted_iota(jnp.int32, shape, 0) - lax.broadcasted_iota(jnp.int32, shape, 1)
    for at in range(widths_ref.shape[0]):
        band = jnp.where((lag >= 0) & (lag < widths_ref[at]), 1.0, 0.0)
        bands_ref[:, pl.ds(at * LANES, LANES)] = band.astype(jnp.bfloat16)
        width = jnp.full((1, LANES), widths_ref[at], jnp.int32).astype(jnp.float32)
        shares_ref[pl.ds(at, 1), :] = 1.0 / jnp.sqrt(width)


def boxcars_kernel(scale, shares_ref, bands_ref, sums_ref, later_ref, out_ref, values, mixed, sems):
    trials = sums_ref.shape[1]
    length = sums_ref.shape[0] - REACH
    filters = shares_ref.shape[0]
    whole = length - REACH
    total = jnp.concatenate(
        [
            sums_ref[pl.ds(REACH, whole), :],
            sums_ref[pl.ds(length, REACH), :] + later_ref[pl.ds(0, REACH), :],
            later_ref[pl.ds(REACH, WMAX), :],
        ],
        axis=0,
    )
    for first in range(0, length + WMAX, LANES):
        tile = (total[first : first + LANES] * scale).T
        values[:, pl.ds(first, LANES)] = tile.astype(jnp.bfloat16)
    parts, pieces = sems.shape
    share = trials // pieces
    shares = [shares_ref[pl.ds(at, 1), :] for at in range(filters)]
    tiles = mixed.reshape(parts, trials, filters, LANES)
    copies = []
    for piece in range(pieces):
        some = pl.ds(piece * share, share)
        windows = [values[some, pl.ds(part * LANES, LANES + WMAX)] for part in range(parts)]
        sums = jnp.dot(jnp.concatenate(windows, axis=0), bands_ref[...], preferred_element_type=jnp.float32)
        for part in range(parts):
            for at in range(filters):
                mixed[part, pl.ds(piece * share * filters + at, share, stride=filters), :] = (
                    sums[part * share : (part + 1) * share, at * LANES : (at + 1) * LANES] * shares[at]
                )
            target = out_ref.at[some, :, pl.ds(part * LANES, LANES)]
            copies.append(pltpu.make_async_copy(tiles.at[part, some], target, sems.at[part, piece]))
            copies[-1].start()
    for copy in copies:
        copy.wait()


def call(kernel, out_shape, in_specs, args, scratch=(), flops=0, **options):
    several = isinstance(out_shape, list)
    options.setdefault("out_specs", [VMEM] * len(out_shape) if several else VMEM)
    return pl.pallas_call(
        kernel,
        out_shape=out_shape,
        in_specs=in_specs,
        scratch_shapes=list(scratch),
        compiler_params=pltpu.CompilerParams(vmem_limit_bytes=16 << 20),
        cost_estimate=pl.CostEstimate(flops=flops, bytes_accessed=1 << 20, transcendentals=0),
        **options,
    )(*args)


def one_beam(own, delays, offsets, me, widths, groups, outer, per_sub, scale):
    chans, length = own.shape
    padded, all_subs = offsets.shape
    sub_dev = chans // per_sub
    inner = groups // outer
    filters = widths.shape[0]
    span = length + DCH
    packed = 2 * sub_dev == LANES
    series_shape = (-(-span // 32) * 16, LANES) if packed else (sub_dev, length + LANES)
    steps = 4
    series, fetched = call(
        functools.partial(series_kernel, per_sub, packed),
        [
            jax.ShapeDtypeStruct(series_shape, jnp.bfloat16),
            jax.ShapeDtypeStruct((padded, all_subs), jnp.int32),
        ],
        [HBM, HBM, HBM],
        tuple(pltpu.with_memory_space_constraint(x, pltpu.HBM) for x in (delays[None, :], own, offsets)),
        [
            pltpu.VMEM((1, chans), jnp.int32),
            pltpu.VMEM((chans, length), jnp.bfloat16),
            pltpu.SemaphoreType.DMA,
            pltpu.SemaphoreType.DMA((2 * steps,)),
        ],
    )
    line = [series] + [exchanged(series, "sub", flip * inner) for flip in range(1, outer)]
    nsub = outer * sub_dev
    table = call(offsets_kernel, jax.ShapeDtypeStruct((all_subs, padded), jnp.float32), [VMEM], (fetched,))
    bands, shares = call(
        bands_kernel,
        [
            jax.ShapeDtypeStruct((LANES + WMAX, filters * LANES), jnp.bfloat16),
            jax.ShapeDtypeStruct((filters, LANES), jnp.float32),
        ],
        [SMEM],
        (widths,),
    )
    joined = call(
        functools.partial(join_packed_kernel if packed else join_kernel, outer),
        jax.ShapeDtypeStruct((span, nsub), jnp.bfloat16),
        [VMEM] * outer + [ANY] * 2,
        (*line, table, bands),
    )
    blocks = [joined] + [exchanged(joined, "sub", flip) for flip in range(1, inner)]
    scratch = [
        pltpu.VMEM((span + 2 * STEP, nsub), jnp.float32),
        pltpu.VMEM((span + STEP, (STEP + 1) * nsub), jnp.bfloat16),
        pltpu.VMEM((nsub, padded), jnp.float32),
    ]
    flops = 2 * (span + STEP) * nsub * padded * (OMAX + 2)
    sums_shape = jax.ShapeDtypeStruct((length + REACH, padded), jnp.float32)
    early_shape = jax.ShapeDtypeStruct((REACH + WMAX, padded), jnp.float32)
    steps = [(flip, None) for flip in range(inner - 1)]
    steps += [(inner - 1, lambda tm: tm > 0), (inner - 1, lambda tm: tm == 0)]
    given = ()
    for at, (flip, here) in enumerate(steps):
        sums, *rest = call(
            functools.partial(sums_kernel, at > 0, here, outer, inner, flip),
            [sums_shape, early_shape] if at == inner - 1 else [sums_shape],
            [SMEM] * 2 + [VMEM] * (2 + len(given)),
            (*me, blocks[flip], table, *given),
            scratch,
            flops,
        )
        given = (sums,)
        if rest:
            later = passed_back(rest[0], "tm")
    parts = length // LANES
    pieces = 2
    return call(
        functools.partial(boxcars_kernel, scale),
        jax.ShapeDtypeStruct((padded, filters, length), jnp.float32),
        [VMEM] * 4,
        (shares, bands, sums, later),
        [
            pltpu.VMEM((padded, length + WMAX), jnp.bfloat16),
            pltpu.VMEM((parts, padded * filters, LANES), jnp.float32),
            pltpu.SemaphoreType.DMA((parts, pieces)),
        ],
        out_specs=HBM,
    )


def per_device(data, delays, offsets, widths):
    beams, chans, length = data.shape
    trials, nsub = offsets.shape
    groups = lax.axis_size("sub")
    outer = 1 << (groups.bit_length() // 2)
    outer = outer if groups % (outer * outer) == 0 else outer // 2
    per_sub = chans // (nsub // groups)
    scale = 1.0 / math.sqrt(chans * groups)
    padded = max(trials, LANES)
    table = jnp.pad(offsets, ((0, padded - trials), (0, 0))) if padded > trials else offsets
    me = [lax.axis_index(axis).astype(jnp.int32).reshape(1) for axis in ("sub", "tm")]
    outs = [
        one_beam(data[beam], delays, table, me, widths, groups, outer, per_sub, scale)[:trials, None]
        for beam in range(beams)
    ]
    return outs[0] if beams == 1 else jnp.concatenate(outs, axis=1)


def solution(mesh):
    placed = (P(None, "sub", "tm"), P("sub"), P("sub", None), P())
    return jax.shard_map(
        per_device,
        mesh=mesh,
        in_specs=placed,
        out_specs=P("sub", None, None, "tm"),
        check_vma=False,
    )
```

```python
import functools
import math

import jax
import jax.numpy as jnp
from jax import lax
from jax.experimental import pallas as pl
from jax.experimental.pallas import tpu as pltpu
from jax.sharding import PartitionSpec as P

WMAX = 128
DCH = 16
OMAX = 96
LANES = 128
STEP = 16
GROUPS = OMAX // STEP
TOGETHER = 1
REACH = OMAX + DCH
VMEM = pl.BlockSpec(memory_space=pltpu.VMEM)
SMEM = pl.BlockSpec(memory_space=pltpu.SMEM)
HBM = pl.BlockSpec(memory_space=pltpu.HBM)
ANY = pl.BlockSpec(memory_space=pl.ANY)


def passed_back(value, axis):
    count = lax.axis_size(axis)
    return lax.ppermute(value, axis, [(source, source - 1) for source in range(1, count)])


def exchanged(value, axis, flip):
    count = lax.axis_size(axis)
    return lax.ppermute(value, axis, [(source, source ^ flip) for source in range(count)])


def series_kernel(
    per_sub, packed, delays_ref, data_ref, series_ref, delays, held, delays_sem, sems
):
    chans, length = data_ref.shape
    block = min(chans, 256)
    subs = block // per_sub
    wide = length + LANES
    first_copy = pltpu.make_async_copy(delays_ref, delays, delays_sem)
    first_copy.start()
    copies = []
    share = chans // sems.shape[0]
    for at in range(sems.shape[0]):
        here = pl.ds(at * share, share)
        copies.append(pltpu.make_async_copy(data_ref.at[here, :], held.at[here, :], sems.at[at]))
        copies[-1].start()
    rows = lax.broadcasted_iota(jnp.int32, (DCH * subs, block), 0)
    owner = lax.broadcasted_iota(jnp.int32, (1, block), 1) // per_sub
    blank = jnp.zeros((subs, LANES), jnp.float32)
    first_copy.wait()
    members = [
        jnp.where(rows == delays[:, at * block : (at + 1) * block] * subs + owner, 1.0, 0.0).astype(jnp.bfloat16)
        for at in range(chans // block)
    ]
    for copy in copies:
        copy.wait()
    parts = []
    for at, member in enumerate(members):
        picked = jnp.dot(member, held[pl.ds(at * block, block), :], preferred_element_type=jnp.float32)
        total = None
        for delay in range(DCH):
            late = jnp.concatenate([picked[delay * subs : (delay + 1) * subs, :], blank], axis=1)
            late = pltpu.roll(late, DCH - delay, 1)
            total = late if total is None else total + late
        parts.append(total)
    total = jnp.concatenate(parts, axis=0)
    if packed:
        half = series_ref.shape[0]
        both = jnp.concatenate([total, pltpu.roll(total, wide - half, 1)], axis=0)
        for first in range(0, half, LANES):
            count = min(LANES, half - first)
            tile = both[:, first : first + LANES].T
            series_ref[pl.ds(first, count), :] = tile[:count].astype(jnp.bfloat16)
    else:
        series_ref[...] = total.astype(jnp.bfloat16)


def join_packed_kernel(outer, *refs):
    blocks, joined_ref = refs[:outer], refs[-1]
    half = blocks[0].shape[0]
    rest = joined_ref.shape[0] - half
    lane = lax.broadcasted_iota(jnp.int32, (half, LANES), 1)
    for at in range(outer // 2):
        left = blocks[2 * at][...].astype(jnp.float32)
        right = blocks[2 * at + 1][...].astype(jnp.float32)
        lanes = pl.ds(at * LANES, LANES)
        early = jnp.where(lane < LANES // 2, left, pltpu.roll(right, LANES // 2, 1))
        late = jnp.where(lane < LANES // 2, pltpu.roll(left, LANES // 2, 1), right)
        joined_ref[pl.ds(0, half), lanes] = early.astype(jnp.bfloat16)
        joined_ref[pl.ds(half, rest), lanes] = late[:rest].astype(jnp.bfloat16)


def join_kernel(outer, *refs):
    blocks, joined_ref = refs[:outer], refs[-1]
    subs = blocks[0].shape[0]
    rows = joined_ref.shape[0]
    several = LANES // subs
    for at in range(outer // several):
        for first in range(0, rows, LANES):
            count = min(LANES, rows - first)
            tile = jnp.concatenate(
                [
                    blocks[at * several + slot][:, pl.ds(first, LANES)].astype(jnp.float32)
                    for slot in range(several)
                ],
                axis=0,
            ).T
            joined_ref[pl.ds(first, count), pl.ds(at * LANES, LANES)] = tile[:count].astype(jnp.bfloat16)


def slot_start(slot, flip, outer, inner, subs, me):
    return pl.multiple_of((((me // inner) ^ slot) * inner + ((me % inner) ^ flip)) * subs, subs)


def add_pair(total, pair, both):
    rows, trials = both.shape[0], both.shape[1] // 2
    for odd in range(2):
        first = STEP * (GROUPS - 1 - 2 * pair - odd)
        total[pl.ds(first, rows), :] += both[:, odd * trials : (odd + 1) * trials]


def sums_kernel(given, here, outer, inner, flip, me_ref, tm_ref, joined_ref, table_ref, *refs):
    pairs = GROUPS // 2
    before_ref, sums_ref, *early_ref = refs[: -3 - pairs] if given else (None, *refs[: -3 - pairs])
    moving, shifted, table = refs[-3 - pairs : -pairs]
    totals = refs[-pairs:]
    if before_ref is None:
        sums_ref[...] = jnp.zeros_like(sums_ref)
    else:
        sums_ref[...] = before_ref[...]

    def add_block():
        span, nsub = joined_ref.shape
        subs = nsub // outer
        for slot in range(outer):
            start = slot_start(slot, flip, outer, inner, subs, me_ref[0])
            table[pl.ds(slot * subs, subs), :] = table_ref[pl.ds(start, subs), :]
        blank = jnp.zeros((STEP, nsub), jnp.float32)
        moving[pl.ds(0, STEP), :] = blank
        moving[pl.ds(STEP, span), :] = joined_ref[...].astype(jnp.float32)
        moving[pl.ds(STEP + span, STEP), :] = blank

        def shift(lag):
            shifted[:, pl.ds(lag * nsub, nsub)] = moving[pl.ds(lag, span + STEP), :].astype(jnp.bfloat16)

        def tile(lag, pair):
            halves = [
                jnp.where(table[...] == float(STEP * (2 * pair + odd) + lag), 1.0, 0.0).astype(jnp.bfloat16)
                if lag < STEP or odd
                else jnp.zeros(table.shape, jnp.bfloat16)
                for odd in range(2)
            ]
            return jnp.concatenate(halves, axis=1)

        for lag in range(TOGETHER):
            shift(lag)
        for first in range(0, STEP + 1, TOGETHER):
            lags = range(first, min(first + TOGETHER, STEP + 1))
            for lag in range(first + TOGETHER, min(first + 2 * TOGETHER, STEP + 1)):
                shift(lag)
            for pair in range(pairs - 1 if first == STEP else 0, pairs):
                both = jnp.dot(
                    shifted[:, pl.ds(first * nsub, len(lags) * nsub)],
                    jnp.concatenate([tile(lag, pair) for lag in lags], axis=0),
                    preferred_element_type=jnp.float32,
                )
                if first:
                    totals[pair][...] += both
                else:
                    totals[pair][...] = both
        for pair in range(pairs):
            add_pair(sums_ref, pair, totals[pair][...])

    if here is None:
        add_block()
    else:
        pl.when(here(tm_ref[0]))(add_block)
    for ref in early_ref:
        ref[...] = sums_ref[pl.ds(0, ref.shape[0]), :]


def tables_kernel(widths_ref, offsets_ref, bands_ref, shares_ref, table_ref, widths, offsets, widths_sem, sems):
    first_copy = pltpu.make_async_copy(widths_ref, widths, widths_sem)
    first_copy.start()
    share = offsets_ref.shape[0] // sems.shape[0]
    copies = []
    for at in range(sems.shape[0]):
        here = pl.ds(at * share, share)
        copies.append(pltpu.make_async_copy(offsets_ref.at[here, :], offsets.at[here, :], sems.at[at]))
        copies[-1].start()
    shape = (bands_ref.shape[0], LANES)
    lag = lax.broadcasted_iota(jnp.int32, shape, 0) - lax.broadcasted_iota(jnp.int32, shape, 1)
    first_copy.wait()
    for at in range(widths_ref.shape[0]):
        band = jnp.where((lag >= 0) & (lag < widths[at]), 1.0, 0.0)
        bands_ref[:, pl.ds(at * LANES, LANES)] = band.astype(jnp.bfloat16)
        width = jnp.full((1, LANES), widths[at], jnp.int32).astype(jnp.float32)
        shares_ref[pl.ds(at, 1), :] = 1.0 / jnp.sqrt(width)
    for copy in copies:
        copy.wait()
    for at in range(offsets.shape[1] // LANES):
        here = pl.ds(at * LANES, LANES)
        table_ref[here, :] = offsets[:, here].astype(jnp.float32).T


def boxcars_kernel(scale, shares_ref, bands_ref, sums_ref, later_ref, out_ref, values, mixed, sems):
    trials = sums_ref.shape[1]
    length = sums_ref.shape[0] - REACH
    filters = shares_ref.shape[0]
    whole = length - REACH
    total = jnp.concatenate(
        [
            sums_ref[pl.ds(REACH, whole), :],
            sums_ref[pl.ds(length, REACH), :] + later_ref[pl.ds(0, REACH), :],
            later_ref[pl.ds(REACH, WMAX), :],
        ],
        axis=0,
    )
    for first in range(0, length + WMAX, LANES):
        tile = (total[first : first + LANES] * scale).T
        values[:, pl.ds(first, LANES)] = tile.astype(jnp.bfloat16)
    parts, pieces = sems.shape
    share = trials // pieces
    shares = [shares_ref[pl.ds(at, 1), :] for at in range(filters)]
    tiles = mixed.reshape(parts, trials, filters, LANES)
    copies = []
    for piece in range(pieces):
        some = pl.ds(piece * share, share)
        windows = [values[some, pl.ds(part * LANES, LANES + WMAX)] for part in range(parts)]
        sums = jnp.dot(jnp.concatenate(windows, axis=0), bands_ref[...], preferred_element_type=jnp.float32)
        for part in range(parts):
            for at in range(filters):
                mixed[part, pl.ds(piece * share * filters + at, share, stride=filters), :] = (
                    sums[part * share : (part + 1) * share, at * LANES : (at + 1) * LANES] * shares[at]
                )
            target = out_ref.at[some, :, pl.ds(part * LANES, LANES)]
            copies.append(pltpu.make_async_copy(tiles.at[part, some], target, sems.at[part, piece]))
            copies[-1].start()
    for copy in copies:
        copy.wait()


def call(kernel, out_shape, in_specs, args, scratch=(), flops=0, **options):
    several = isinstance(out_shape, list)
    options.setdefault("out_specs", [VMEM] * len(out_shape) if several else VMEM)
    return pl.pallas_call(
        kernel,
        out_shape=out_shape,
        in_specs=in_specs,
        scratch_shapes=list(scratch),
        compiler_params=pltpu.CompilerParams(vmem_limit_bytes=16 << 20),
        cost_estimate=pl.CostEstimate(flops=flops, bytes_accessed=1 << 20, transcendentals=0),
        **options,
    )(*args)


def one_beam(own, delays, offsets, me, widths, groups, outer, per_sub, scale):
    chans, length = own.shape
    padded, all_subs = offsets.shape
    sub_dev = chans // per_sub
    inner = groups // outer
    filters = widths.shape[0]
    span = length + DCH
    packed = 2 * sub_dev == LANES
    series_shape = (-(-span // 32) * 16, LANES) if packed else (sub_dev, length + LANES)
    steps = 4
    series = call(
        functools.partial(series_kernel, per_sub, packed),
        jax.ShapeDtypeStruct(series_shape, jnp.bfloat16),
        [HBM, HBM],
        tuple(pltpu.with_memory_space_constraint(x, pltpu.HBM) for x in (delays[None, :], own)),
        [
            pltpu.VMEM((1, chans), jnp.int32),
            pltpu.VMEM((chans, length), jnp.bfloat16),
            pltpu.SemaphoreType.DMA,
            pltpu.SemaphoreType.DMA((steps,)),
        ],
    )
    line = [series] + [exchanged(series, "sub", flip * inner) for flip in range(1, outer)]
    nsub = outer * sub_dev
    bands, shares, table = call(
        tables_kernel,
        [
            jax.ShapeDtypeStruct((LANES + WMAX, filters * LANES), jnp.bfloat16),
            jax.ShapeDtypeStruct((filters, LANES), jnp.float32),
            jax.ShapeDtypeStruct((all_subs, padded), jnp.float32),
        ],
        [HBM, HBM],
        tuple(pltpu.with_memory_space_constraint(x, pltpu.HBM) for x in (widths, offsets)),
        [
            pltpu.SMEM((filters,), jnp.int32),
            pltpu.VMEM((padded, all_subs), jnp.int32),
            pltpu.SemaphoreType.DMA,
            pltpu.SemaphoreType.DMA((steps,)),
        ],
    )
    joined = call(
        functools.partial(join_packed_kernel if packed else join_kernel, outer),
        jax.ShapeDtypeStruct((span, nsub), jnp.bfloat16),
        [VMEM] * outer + [ANY] * 2,
        (*line, table, bands),
    )
    blocks = [joined] + [exchanged(joined, "sub", flip) for flip in range(1, inner)]
    scratch = [
        pltpu.VMEM((span + 2 * STEP, nsub), jnp.float32),
        pltpu.VMEM((span + STEP, (STEP + 1) * nsub), jnp.bfloat16),
        pltpu.VMEM((nsub, padded), jnp.float32),
        *[pltpu.VMEM((span + STEP, 2 * padded), jnp.float32)] * (GROUPS // 2),
    ]
    flops = 2 * (span + STEP) * nsub * padded * (OMAX + 2)
    sums_shape = jax.ShapeDtypeStruct((length + REACH, padded), jnp.float32)
    early_shape = jax.ShapeDtypeStruct((REACH + WMAX, padded), jnp.float32)
    steps = [(flip, None) for flip in range(inner - 1)]
    steps += [(inner - 1, lambda tm: tm > 0), (inner - 1, lambda tm: tm == 0)]
    given = ()
    for at, (flip, here) in enumerate(steps):
        sums, *rest = call(
            functools.partial(sums_kernel, at > 0, here, outer, inner, flip),
            [sums_shape, early_shape] if at == inner - 1 else [sums_shape],
            [SMEM] * 2 + [VMEM] * (2 + len(given)),
            (*me, blocks[flip], table, *given),
            scratch,
            flops,
        )
        given = (sums,)
        if rest:
            later = passed_back(rest[0], "tm")
    parts = length // LANES
    pieces = 2
    return call(
        functools.partial(boxcars_kernel, scale),
        jax.ShapeDtypeStruct((padded, filters, length), jnp.float32),
        [VMEM] * 4,
        (shares, bands, sums, later),
        [
            pltpu.VMEM((padded, length + WMAX), jnp.bfloat16),
            pltpu.VMEM((parts, padded * filters, LANES), jnp.float32),
            pltpu.SemaphoreType.DMA((parts, pieces)),
        ],
        out_specs=HBM,
    )


def per_device(data, delays, offsets, widths):
    beams, chans, length = data.shape
    trials, nsub = offsets.shape
    groups = lax.axis_size("sub")
    outer = 1 << (groups.bit_length() // 2)
    outer = outer if groups % (outer * outer) == 0 else outer // 2
    per_sub = chans // (nsub // groups)
    scale = 1.0 / math.sqrt(chans * groups)
    padded = max(trials, LANES)
    table = jnp.pad(offsets, ((0, padded - trials), (0, 0))) if padded > trials else offsets
    me = [lax.axis_index(axis).astype(jnp.int32).reshape(1) for axis in ("sub", "tm")]
    outs = [
        one_beam(data[beam], delays, table, me, widths, groups, outer, per_sub, scale)[:trials, None]
        for beam in range(beams)
    ]
    return outs[0] if beams == 1 else jnp.concatenate(outs, axis=1)


def solution(mesh):
    placed = (P(None, "sub", "tm"), P("sub"), P("sub", None), P())
    return jax.shard_map(
        per_device,
        mesh=mesh,
        in_specs=placed,
        out_specs=P("sub", None, None, "tm"),
        check_vma=False,
    )
```

```python
import functools
import math

import jax
import jax.numpy as jnp
from jax import lax
from jax.experimental import pallas as pl
from jax.experimental.pallas import tpu as pltpu
from jax.sharding import PartitionSpec as P

WMAX = 128
DCH = 16
OMAX = 96
LANES = 128
STEP = 16
GROUPS = OMAX // STEP
TOGETHER = 1
REACH = OMAX + DCH
VMEM = pl.BlockSpec(memory_space=pltpu.VMEM)
SMEM = pl.BlockSpec(memory_space=pltpu.SMEM)
HBM = pl.BlockSpec(memory_space=pltpu.HBM)
ANY = pl.BlockSpec(memory_space=pl.ANY)


def passed_back(value, axis):
    count = lax.axis_size(axis)
    return lax.ppermute(value, axis, [(source, source - 1) for source in range(1, count)])


def exchanged(value, axis, flip):
    count = lax.axis_size(axis)
    return lax.ppermute(value, axis, [(source, source ^ flip) for source in range(count)])


def series_kernel(
    per_sub, packed, delays_ref, data_ref, series_ref, delays, held, delays_sem, sems
):
    chans, length = data_ref.shape
    block = min(chans, 256)
    subs = block // per_sub
    wide = length + LANES
    first_copy = pltpu.make_async_copy(delays_ref, delays, delays_sem)
    first_copy.start()
    copies = []
    share = chans // sems.shape[0]
    for at in range(sems.shape[0]):
        here = pl.ds(at * share, share)
        copies.append(pltpu.make_async_copy(data_ref.at[here, :], held.at[here, :], sems.at[at]))
        copies[-1].start()
    rows = lax.broadcasted_iota(jnp.int32, (DCH * subs, block), 0)
    owner = lax.broadcasted_iota(jnp.int32, (1, block), 1) // per_sub
    blank = jnp.zeros((subs, LANES), jnp.float32)
    first_copy.wait()
    members = [
        jnp.where(rows == delays[:, at * block : (at + 1) * block] * subs + owner, 1.0, 0.0).astype(jnp.bfloat16)
        for at in range(chans // block)
    ]
    for copy in copies:
        copy.wait()
    parts = []
    for at, member in enumerate(members):
        picked = jnp.dot(member, held[pl.ds(at * block, block), :], preferred_element_type=jnp.float32)
        total = None
        for delay in range(DCH):
            late = jnp.concatenate([picked[delay * subs : (delay + 1) * subs, :], blank], axis=1)
            late = pltpu.roll(late, DCH - delay, 1)
            total = late if total is None else total + late
        parts.append(total)
    total = jnp.concatenate(parts, axis=0)
    if packed:
        half = series_ref.shape[0]
        both = jnp.concatenate([total, pltpu.roll(total, wide - half, 1)], axis=0)
        for first in range(0, half, LANES):
            count = min(LANES, half - first)
            tile = both[:, first : first + LANES].T
            series_ref[pl.ds(first, count), :] = tile[:count].astype(jnp.bfloat16)
    else:
        series_ref[...] = total.astype(jnp.bfloat16)


def join_packed_kernel(outer, *refs):
    blocks, joined_ref = refs[:outer], refs[-1]
    half = blocks[0].shape[0]
    rest = joined_ref.shape[0] - half
    lane = lax.broadcasted_iota(jnp.int32, (half, LANES), 1)
    for at in range(outer // 2):
        left = blocks[2 * at][...].astype(jnp.float32)
        right = blocks[2 * at + 1][...].astype(jnp.float32)
        lanes = pl.ds(at * LANES, LANES)
        early = jnp.where(lane < LANES // 2, left, pltpu.roll(right, LANES // 2, 1))
        late = jnp.where(lane < LANES // 2, pltpu.roll(left, LANES // 2, 1), right)
        joined_ref[pl.ds(0, half), lanes] = early.astype(jnp.bfloat16)
        joined_ref[pl.ds(half, rest), lanes] = late[:rest].astype(jnp.bfloat16)


def join_kernel(outer, *refs):
    blocks, joined_ref = refs[:outer], refs[-1]
    subs = blocks[0].shape[0]
    rows = joined_ref.shape[0]
    several = LANES // subs
    for at in range(outer // several):
        for first in range(0, rows, LANES):
            count = min(LANES, rows - first)
            tile = jnp.concatenate(
                [
                    blocks[at * several + slot][:, pl.ds(first, LANES)].astype(jnp.float32)
                    for slot in range(several)
                ],
                axis=0,
            ).T
            joined_ref[pl.ds(first, count), pl.ds(at * LANES, LANES)] = tile[:count].astype(jnp.bfloat16)


def slot_start(slot, flip, outer, inner, subs, me):
    return pl.multiple_of((((me // inner) ^ slot) * inner + ((me % inner) ^ flip)) * subs, subs)


def add_pair(total, pair, both):
    rows, trials = both.shape[0], both.shape[1] // 2
    for odd in range(2):
        first = STEP * (GROUPS - 1 - 2 * pair - odd)
        total[pl.ds(first, rows), :] += both[:, odd * trials : (odd + 1) * trials]


def sums_kernel(given, here, outer, inner, flip, me_ref, tm_ref, joined_ref, table_ref, *refs):
    pairs = GROUPS // 2
    before_ref, sums_ref, *early_ref = refs[: -3 - pairs] if given else (None, *refs[: -3 - pairs])
    moving, shifted, table = refs[-3 - pairs : -pairs]
    totals = refs[-pairs:]
    if before_ref is None:
        sums_ref[...] = jnp.zeros_like(sums_ref)
    else:
        sums_ref[...] = before_ref[...]

    def add_block():
        span, nsub = joined_ref.shape
        subs = nsub // outer
        for slot in range(outer):
            start = slot_start(slot, flip, outer, inner, subs, me_ref[0])
            table[pl.ds(slot * subs, subs), :] = table_ref[pl.ds(start, subs), :]
        blank = jnp.zeros((STEP, nsub), jnp.float32)
        moving[pl.ds(0, STEP), :] = blank
        moving[pl.ds(STEP, span), :] = joined_ref[...].astype(jnp.float32)
        moving[pl.ds(STEP + span, STEP), :] = blank

        def shift(lag):
            shifted[:, pl.ds(lag * nsub, nsub)] = moving[pl.ds(lag, span + STEP), :].astype(jnp.bfloat16)

        def tile(lag, pair):
            halves = [
                jnp.where(table[...] == float(STEP * (2 * pair + odd) + lag), 1.0, 0.0).astype(jnp.bfloat16)
                if lag < STEP or odd
                else jnp.zeros(table.shape, jnp.bfloat16)
                for odd in range(2)
            ]
            return jnp.concatenate(halves, axis=1)

        for lag in range(TOGETHER):
            shift(lag)
        for first in range(0, STEP + 1, TOGETHER):
            lags = range(first, min(first + TOGETHER, STEP + 1))
            for lag in range(first + TOGETHER, min(first + 2 * TOGETHER, STEP + 1)):
                shift(lag)
            for pair in range(pairs - 1 if first == STEP else 0, pairs):
                both = jnp.dot(
                    shifted[:, pl.ds(first * nsub, len(lags) * nsub)],
                    jnp.concatenate([tile(lag, pair) for lag in lags], axis=0),
                    preferred_element_type=jnp.float32,
                )
                if first:
                    totals[pair][...] += both
                else:
                    totals[pair][...] = both
        for pair in range(pairs):
            add_pair(sums_ref, pair, totals[pair][...])

    if here is None:
        add_block()
    else:
        pl.when(here(tm_ref[0]))(add_block)
    for ref in early_ref:
        ref[...] = sums_ref[pl.ds(0, ref.shape[0]), :]


def tables_kernel(widths_ref, offsets_ref, bands_ref, shares_ref, table_ref, widths, offsets, widths_sem, sems):
    first_copy = pltpu.make_async_copy(widths_ref, widths, widths_sem)
    first_copy.start()
    share = offsets_ref.shape[0] // sems.shape[0]
    copies = []
    for at in range(sems.shape[0]):
        here = pl.ds(at * share, share)
        copies.append(pltpu.make_async_copy(offsets_ref.at[here, :], offsets.at[here, :], sems.at[at]))
        copies[-1].start()
    shape = (bands_ref.shape[0], LANES)
    lag = lax.broadcasted_iota(jnp.int32, shape, 0) - lax.broadcasted_iota(jnp.int32, shape, 1)
    first_copy.wait()
    for at in range(widths_ref.shape[0]):
        band = jnp.where((lag >= 0) & (lag < widths[at]), 1.0, 0.0)
        bands_ref[:, pl.ds(at * LANES, LANES)] = band.astype(jnp.bfloat16)
        width = jnp.full((1, LANES), widths[at], jnp.int32).astype(jnp.float32)
        shares_ref[pl.ds(at, 1), :] = 1.0 / jnp.sqrt(width)
    for copy in copies:
        copy.wait()
    for at in range(offsets.shape[1] // LANES):
        here = pl.ds(at * LANES, LANES)
        table_ref[here, :] = offsets[:, here].astype(jnp.float32).T


def boxcars_kernel(scale, shares_ref, bands_ref, sums_ref, later_ref, out_ref, values, mixed, sems):
    trials = sums_ref.shape[1]
    length = sums_ref.shape[0] - REACH
    filters = shares_ref.shape[0]
    whole = length - REACH
    total = jnp.concatenate(
        [
            sums_ref[pl.ds(REACH, whole), :],
            sums_ref[pl.ds(length, REACH), :] + later_ref[pl.ds(0, REACH), :],
            later_ref[pl.ds(REACH, WMAX), :],
        ],
        axis=0,
    )
    for first in range(0, length + WMAX, LANES):
        tile = (total[first : first + LANES] * scale).T
        values[:, pl.ds(first, LANES)] = tile.astype(jnp.bfloat16)
    parts, pieces = sems.shape
    share = trials // pieces
    shares = [shares_ref[pl.ds(at, 1), :] for at in range(filters)]
    tiles = mixed.reshape(parts, trials, filters, LANES)
    copies = []
    for piece in range(pieces):
        some = pl.ds(piece * share, share)
        windows = [values[some, pl.ds(part * LANES, LANES + WMAX)] for part in range(parts)]
        sums = jnp.dot(jnp.concatenate(windows, axis=0), bands_ref[...], preferred_element_type=jnp.float32)
        for part in range(parts):
            for at in range(filters):
                mixed[part, pl.ds(piece * share * filters + at, share, stride=filters), :] = (
                    sums[part * share : (part + 1) * share, at * LANES : (at + 1) * LANES] * shares[at]
                )
            target = out_ref.at[some, :, pl.ds(part * LANES, LANES)]
            copies.append(pltpu.make_async_copy(tiles.at[part, some], target, sems.at[part, piece]))
            copies[-1].start()
    for copy in copies:
        copy.wait()


def call(kernel, out_shape, in_specs, args, scratch=(), flops=0, **options):
    several = isinstance(out_shape, list)
    options.setdefault("out_specs", [VMEM] * len(out_shape) if several else VMEM)
    return pl.pallas_call(
        kernel,
        out_shape=out_shape,
        in_specs=in_specs,
        scratch_shapes=list(scratch),
        compiler_params=pltpu.CompilerParams(vmem_limit_bytes=16 << 20),
        cost_estimate=pl.CostEstimate(flops=flops, bytes_accessed=1 << 20, transcendentals=0),
        **options,
    )(*args)


def one_beam(own, delays, offsets, me, widths, groups, outer, per_sub, scale):
    chans, length = own.shape
    padded, all_subs = offsets.shape
    sub_dev = chans // per_sub
    inner = groups // outer
    filters = widths.shape[0]
    span = length + DCH
    packed = 2 * sub_dev == LANES
    series_shape = (-(-span // 32) * 16, LANES) if packed else (sub_dev, length + LANES)
    steps = 8
    series = call(
        functools.partial(series_kernel, per_sub, packed),
        jax.ShapeDtypeStruct(series_shape, jnp.bfloat16),
        [HBM, HBM],
        tuple(pltpu.with_memory_space_constraint(x, pltpu.HBM) for x in (delays[None, :], own)),
        [
            pltpu.VMEM((1, chans), jnp.int32),
            pltpu.VMEM((chans, length), jnp.bfloat16),
            pltpu.SemaphoreType.DMA,
            pltpu.SemaphoreType.DMA((steps,)),
        ],
    )
    line = [series] + [exchanged(series, "sub", flip * inner) for flip in range(1, outer)]
    nsub = outer * sub_dev
    bands, shares, table = call(
        tables_kernel,
        [
            jax.ShapeDtypeStruct((LANES + WMAX, filters * LANES), jnp.bfloat16),
            jax.ShapeDtypeStruct((filters, LANES), jnp.float32),
            jax.ShapeDtypeStruct((all_subs, padded), jnp.float32),
        ],
        [HBM, HBM],
        tuple(pltpu.with_memory_space_constraint(x, pltpu.HBM) for x in (widths, offsets)),
        [
            pltpu.SMEM((filters,), jnp.int32),
            pltpu.VMEM((padded, all_subs), jnp.int32),
            pltpu.SemaphoreType.DMA,
            pltpu.SemaphoreType.DMA((steps,)),
        ],
    )
    joined = call(
        functools.partial(join_packed_kernel if packed else join_kernel, outer),
        jax.ShapeDtypeStruct((span, nsub), jnp.bfloat16),
        [VMEM] * outer + [ANY] * 2,
        (*line, table, bands),
    )
    blocks = [joined] + [exchanged(joined, "sub", flip) for flip in range(1, inner)]
    scratch = [
        pltpu.VMEM((span + 2 * STEP, nsub), jnp.float32),
        pltpu.VMEM((span + STEP, (STEP + 1) * nsub), jnp.bfloat16),
        pltpu.VMEM((nsub, padded), jnp.float32),
        *[pltpu.VMEM((span + STEP, 2 * padded), jnp.float32)] * (GROUPS // 2),
    ]
    flops = 2 * (span + STEP) * nsub * padded * (OMAX + 2)
    sums_shape = jax.ShapeDtypeStruct((length + REACH, padded), jnp.float32)
    early_shape = jax.ShapeDtypeStruct((REACH + WMAX, padded), jnp.float32)
    steps = [(flip, None) for flip in range(inner - 1)]
    steps += [(inner - 1, lambda tm: tm > 0), (inner - 1, lambda tm: tm == 0)]
    given = ()
    for at, (flip, here) in enumerate(steps):
        sums, *rest = call(
            functools.partial(sums_kernel, at > 0, here, outer, inner, flip),
            [sums_shape, early_shape] if at == inner - 1 else [sums_shape],
            [SMEM] * 2 + [VMEM] * (2 + len(given)),
            (*me, blocks[flip], table, *given),
            scratch,
            flops,
        )
        given = (sums,)
        if rest:
            later = passed_back(rest[0], "tm")
    parts = length // LANES
    pieces = 4
    return call(
        functools.partial(boxcars_kernel, scale),
        jax.ShapeDtypeStruct((padded, filters, length), jnp.float32),
        [VMEM] * 4,
        (shares, bands, sums, later),
        [
            pltpu.VMEM((padded, length + WMAX), jnp.bfloat16),
            pltpu.VMEM((parts, padded * filters, LANES), jnp.float32),
            pltpu.SemaphoreType.DMA((parts, pieces)),
        ],
        out_specs=HBM,
    )


def per_device(data, delays, offsets, widths):
    beams, chans, length = data.shape
    trials, nsub = offsets.shape
    groups = lax.axis_size("sub")
    outer = 1 << (groups.bit_length() // 2)
    outer = outer if groups % (outer * outer) == 0 else outer // 2
    per_sub = chans // (nsub // groups)
    scale = 1.0 / math.sqrt(chans * groups)
    padded = max(trials, LANES)
    table = jnp.pad(offsets, ((0, padded - trials), (0, 0))) if padded > trials else offsets
    me = [lax.axis_index(axis).astype(jnp.int32).reshape(1) for axis in ("sub", "tm")]
    outs = [
        one_beam(data[beam], delays, table, me, widths, groups, outer, per_sub, scale)[:trials, None]
        for beam in range(beams)
    ]
    return outs[0] if beams == 1 else jnp.concatenate(outs, axis=1)


def solution(mesh):
    placed = (P(None, "sub", "tm"), P("sub"), P("sub", None), P())
    return jax.shard_map(
        per_device,
        mesh=mesh,
        in_specs=placed,
        out_specs=P("sub", None, None, "tm"),
        check_vma=False,
    )
```

```python
import functools
import math

import jax
import jax.numpy as jnp
from jax import lax
from jax.experimental import pallas as pl
from jax.experimental.pallas import tpu as pltpu
from jax.sharding import PartitionSpec as P

WMAX = 128
DCH = 16
OMAX = 96
LANES = 128
STEP = 16
GROUPS = OMAX // STEP
TOGETHER = 1
REACH = OMAX + DCH
VMEM = pl.BlockSpec(memory_space=pltpu.VMEM)
SMEM = pl.BlockSpec(memory_space=pltpu.SMEM)
HBM = pl.BlockSpec(memory_space=pltpu.HBM)
ANY = pl.BlockSpec(memory_space=pl.ANY)


def passed_back(value, axis):
    count = lax.axis_size(axis)
    return lax.ppermute(value, axis, [(source, source - 1) for source in range(1, count)])


def exchanged(value, axis, flip):
    count = lax.axis_size(axis)
    return lax.ppermute(value, axis, [(source, source ^ flip) for source in range(count)])


def series_kernel(
    per_sub, packed, delays_ref, data_ref, series_ref, delays, held, delays_sem, sems
):
    chans, length = data_ref.shape
    block = min(chans, 256)
    subs = block // per_sub
    wide = length + LANES
    first_copy = pltpu.make_async_copy(delays_ref, delays, delays_sem)
    first_copy.start()
    copies = []
    share = chans // sems.shape[0]
    for at in range(sems.shape[0]):
        here = pl.ds(at * share, share)
        copies.append(pltpu.make_async_copy(data_ref.at[here, :], held.at[here, :], sems.at[at]))
        copies[-1].start()
    rows = lax.broadcasted_iota(jnp.int32, (DCH * subs, block), 0)
    owner = lax.broadcasted_iota(jnp.int32, (1, block), 1) // per_sub
    blank = jnp.zeros((subs, LANES), jnp.float32)
    first_copy.wait()
    members = [
        jnp.where(rows == delays[:, at * block : (at + 1) * block] * subs + owner, 1.0, 0.0).astype(jnp.bfloat16)
        for at in range(chans // block)
    ]
    for copy in copies:
        copy.wait()
    parts = []
    for at, member in enumerate(members):
        picked = jnp.dot(member, held[pl.ds(at * block, block), :], preferred_element_type=jnp.float32)
        total = None
        for delay in range(DCH):
            late = jnp.concatenate([picked[delay * subs : (delay + 1) * subs, :], blank], axis=1)
            late = pltpu.roll(late, DCH - delay, 1)
            total = late if total is None else total + late
        parts.append(total)
    total = jnp.concatenate(parts, axis=0)
    if packed:
        half = series_ref.shape[0]
        both = jnp.concatenate([total, pltpu.roll(total, wide - half, 1)], axis=0)
        for first in range(0, half, LANES):
            count = min(LANES, half - first)
            tile = both[:, first : first + LANES].T
            series_ref[pl.ds(first, count), :] = tile[:count].astype(jnp.bfloat16)
    else:
        series_ref[...] = total.astype(jnp.bfloat16)


def join_packed_kernel(outer, *refs):
    blocks, joined_ref = refs[:outer], refs[-1]
    half = blocks[0].shape[0]
    rest = joined_ref.shape[0] - half
    lane = lax.broadcasted_iota(jnp.int32, (half, LANES), 1)
    for at in range(outer // 2):
        left = blocks[2 * at][...].astype(jnp.float32)
        right = blocks[2 * at + 1][...].astype(jnp.float32)
        lanes = pl.ds(at * LANES, LANES)
        early = jnp.where(lane < LANES // 2, left, pltpu.roll(right, LANES // 2, 1))
        late = jnp.where(lane < LANES // 2, pltpu.roll(left, LANES // 2, 1), right)
        joined_ref[pl.ds(0, half), lanes] = early.astype(jnp.bfloat16)
        joined_ref[pl.ds(half, rest), lanes] = late[:rest].astype(jnp.bfloat16)


def join_kernel(outer, *refs):
    blocks, joined_ref = refs[:outer], refs[-1]
    subs = blocks[0].shape[0]
    rows = joined_ref.shape[0]
    several = LANES // subs
    for at in range(outer // several):
        for first in range(0, rows, LANES):
            count = min(LANES, rows - first)
            tile = jnp.concatenate(
                [
                    blocks[at * several + slot][:, pl.ds(first, LANES)].astype(jnp.float32)
                    for slot in range(several)
                ],
                axis=0,
            ).T
            joined_ref[pl.ds(first, count), pl.ds(at * LANES, LANES)] = tile[:count].astype(jnp.bfloat16)


def slot_start(slot, flip, outer, inner, subs, me):
    return pl.multiple_of((((me // inner) ^ slot) * inner + ((me % inner) ^ flip)) * subs, subs)


def add_pair(total, pair, both):
    rows, trials = both.shape[0], both.shape[1] // 2
    for odd in range(2):
        first = STEP * (GROUPS - 1 - 2 * pair - odd)
        total[pl.ds(first, rows), :] += both[:, odd * trials : (odd + 1) * trials]


def sums_kernel(given, here, outer, inner, flip, me_ref, tm_ref, joined_ref, table_ref, *refs):
    pairs = GROUPS // 2
    before_ref, sums_ref, *early_ref = refs[: -3 - pairs] if given else (None, *refs[: -3 - pairs])
    moving, shifted, table = refs[-3 - pairs : -pairs]
    totals = refs[-pairs:]
    if before_ref is None:
        sums_ref[...] = jnp.zeros_like(sums_ref)
    else:
        sums_ref[...] = before_ref[...]

    def add_block():
        span, nsub = joined_ref.shape
        subs = nsub // outer
        for slot in range(outer):
            start = slot_start(slot, flip, outer, inner, subs, me_ref[0])
            table[pl.ds(slot * subs, subs), :] = table_ref[pl.ds(start, subs), :]
        blank = jnp.zeros((STEP, nsub), jnp.float32)
        moving[pl.ds(0, STEP), :] = blank
        moving[pl.ds(STEP, span), :] = joined_ref[...].astype(jnp.float32)
        moving[pl.ds(STEP + span, STEP), :] = blank

        def shift(lag):
            shifted[:, pl.ds(lag * nsub, nsub)] = moving[pl.ds(lag, span + STEP), :].astype(jnp.bfloat16)

        def tile(lag, pair):
            halves = [
                jnp.where(table[...] == float(STEP * (2 * pair + odd) + lag), 1.0, 0.0).astype(jnp.bfloat16)
                if lag < STEP or odd
                else jnp.zeros(table.shape, jnp.bfloat16)
                for odd in range(2)
            ]
            return jnp.concatenate(halves, axis=1)

        for lag in range(TOGETHER):
            shift(lag)
        for first in range(0, STEP + 1, TOGETHER):
            lags = range(first, min(first + TOGETHER, STEP + 1))
            for pair in range(pairs - 1 if first == STEP else 0, pairs):
                both = jnp.dot(
                    shifted[:, pl.ds(first * nsub, len(lags) * nsub)],
                    jnp.concatenate([tile(lag, pair) for lag in lags], axis=0),
                    preferred_element_type=jnp.float32,
                )
                if first:
                    totals[pair][...] += both
                else:
                    totals[pair][...] = both
                if pair == 0:
                    for lag in range(first + TOGETHER, min(first + 2 * TOGETHER, STEP + 1)):
                        shift(lag)
        for pair in range(pairs):
            add_pair(sums_ref, pair, totals[pair][...])

    if here is None:
        add_block()
    else:
        pl.when(here(tm_ref[0]))(add_block)
    for ref in early_ref:
        ref[...] = sums_ref[pl.ds(0, ref.shape[0]), :]


def tables_kernel(widths_ref, offsets_ref, bands_ref, shares_ref, table_ref, widths, offsets, widths_sem, sems):
    first_copy = pltpu.make_async_copy(widths_ref, widths, widths_sem)
    first_copy.start()
    share = offsets_ref.shape[0] // sems.shape[0]
    copies = []
    for at in range(sems.shape[0]):
        here = pl.ds(at * share, share)
        copies.append(pltpu.make_async_copy(offsets_ref.at[here, :], offsets.at[here, :], sems.at[at]))
        copies[-1].start()
    shape = (bands_ref.shape[0], LANES)
    lag = lax.broadcasted_iota(jnp.int32, shape, 0) - lax.broadcasted_iota(jnp.int32, shape, 1)
    first_copy.wait()
    for at in range(widths_ref.shape[0]):
        band = jnp.where((lag >= 0) & (lag < widths[at]), 1.0, 0.0)
        bands_ref[:, pl.ds(at * LANES, LANES)] = band.astype(jnp.bfloat16)
        width = jnp.full((1, LANES), widths[at], jnp.int32).astype(jnp.float32)
        shares_ref[pl.ds(at, 1), :] = 1.0 / jnp.sqrt(width)
    for copy in copies:
        copy.wait()
    for at in range(offsets.shape[1] // LANES):
        here = pl.ds(at * LANES, LANES)
        table_ref[here, :] = offsets[:, here].astype(jnp.float32).T


def boxcars_kernel(scale, shares_ref, bands_ref, sums_ref, later_ref, out_ref, values, mixed, sems):
    trials = sums_ref.shape[1]
    length = sums_ref.shape[0] - REACH
    filters = shares_ref.shape[0]
    whole = length - REACH
    total = jnp.concatenate(
        [
            sums_ref[pl.ds(REACH, whole), :],
            sums_ref[pl.ds(length, REACH), :] + later_ref[pl.ds(0, REACH), :],
            later_ref[pl.ds(REACH, WMAX), :],
        ],
        axis=0,
    )
    for first in range(0, length + WMAX, LANES):
        tile = (total[first : first + LANES] * scale).T
        values[:, pl.ds(first, LANES)] = tile.astype(jnp.bfloat16)
    parts, pieces = sems.shape
    share = trials // pieces
    shares = [shares_ref[pl.ds(at, 1), :] for at in range(filters)]
    tiles = mixed.reshape(parts, trials, filters, LANES)
    copies = []
    for piece in range(pieces):
        some = pl.ds(piece * share, share)
        windows = [values[some, pl.ds(part * LANES, LANES + WMAX)] for part in range(parts)]
        sums = jnp.dot(jnp.concatenate(windows, axis=0), bands_ref[...], preferred_element_type=jnp.float32)
        for part in range(parts):
            for at in range(filters):
                mixed[part, pl.ds(piece * share * filters + at, share, stride=filters), :] = (
                    sums[part * share : (part + 1) * share, at * LANES : (at + 1) * LANES] * shares[at]
                )
            target = out_ref.at[some, :, pl.ds(part * LANES, LANES)]
            copies.append(pltpu.make_async_copy(tiles.at[part, some], target, sems.at[part, piece]))
            copies[-1].start()
    for copy in copies:
        copy.wait()


def call(kernel, out_shape, in_specs, args, scratch=(), flops=0, **options):
    several = isinstance(out_shape, list)
    options.setdefault("out_specs", [VMEM] * len(out_shape) if several else VMEM)
    return pl.pallas_call(
        kernel,
        out_shape=out_shape,
        in_specs=in_specs,
        scratch_shapes=list(scratch),
        compiler_params=pltpu.CompilerParams(vmem_limit_bytes=16 << 20),
        cost_estimate=pl.CostEstimate(flops=flops, bytes_accessed=1 << 20, transcendentals=0),
        **options,
    )(*args)


def one_beam(own, delays, offsets, me, widths, groups, outer, per_sub, scale):
    chans, length = own.shape
    padded, all_subs = offsets.shape
    sub_dev = chans // per_sub
    inner = groups // outer
    filters = widths.shape[0]
    span = length + DCH
    packed = 2 * sub_dev == LANES
    series_shape = (-(-span // 32) * 16, LANES) if packed else (sub_dev, length + LANES)
    steps = 4
    series = call(
        functools.partial(series_kernel, per_sub, packed),
        jax.ShapeDtypeStruct(series_shape, jnp.bfloat16),
        [HBM, HBM],
        tuple(pltpu.with_memory_space_constraint(x, pltpu.HBM) for x in (delays[None, :], own)),
        [
            pltpu.VMEM((1, chans), jnp.int32),
            pltpu.VMEM((chans, length), jnp.bfloat16),
            pltpu.SemaphoreType.DMA,
            pltpu.SemaphoreType.DMA((steps,)),
        ],
    )
    line = [series] + [exchanged(series, "sub", flip * inner) for flip in range(1, outer)]
    nsub = outer * sub_dev
    bands, shares, table = call(
        tables_kernel,
        [
            jax.ShapeDtypeStruct((LANES + WMAX, filters * LANES), jnp.bfloat16),
            jax.ShapeDtypeStruct((filters, LANES), jnp.float32),
            jax.ShapeDtypeStruct((all_subs, padded), jnp.float32),
        ],
        [HBM, HBM],
        tuple(pltpu.with_memory_space_constraint(x, pltpu.HBM) for x in (widths, offsets)),
        [
            pltpu.SMEM((filters,), jnp.int32),
            pltpu.VMEM((padded, all_subs), jnp.int32),
            pltpu.SemaphoreType.DMA,
            pltpu.SemaphoreType.DMA((steps,)),
        ],
    )
    joined = call(
        functools.partial(join_packed_kernel if packed else join_kernel, outer),
        jax.ShapeDtypeStruct((span, nsub), jnp.bfloat16),
        [VMEM] * outer + [ANY] * 2,
        (*line, table, bands),
    )
    blocks = [joined] + [exchanged(joined, "sub", flip) for flip in range(1, inner)]
    scratch = [
        pltpu.VMEM((span + 2 * STEP, nsub), jnp.float32),
        pltpu.VMEM((span + STEP, (STEP + 1) * nsub), jnp.bfloat16),
        pltpu.VMEM((nsub, padded), jnp.float32),
        *[pltpu.VMEM((span + STEP, 2 * padded), jnp.float32)] * (GROUPS // 2),
    ]
    flops = 2 * (span + STEP) * nsub * padded * (OMAX + 2)
    sums_shape = jax.ShapeDtypeStruct((length + REACH, padded), jnp.float32)
    early_shape = jax.ShapeDtypeStruct((REACH + WMAX, padded), jnp.float32)
    steps = [(flip, None) for flip in range(inner - 1)]
    steps += [(inner - 1, lambda tm: tm > 0), (inner - 1, lambda tm: tm == 0)]
    given = ()
    for at, (flip, here) in enumerate(steps):
        sums, *rest = call(
            functools.partial(sums_kernel, at > 0, here, outer, inner, flip),
            [sums_shape, early_shape] if at == inner - 1 else [sums_shape],
            [SMEM] * 2 + [VMEM] * (2 + len(given)),
            (*me, blocks[flip], table, *given),
            scratch,
            flops,
        )
        given = (sums,)
        if rest:
            later = passed_back(rest[0], "tm")
    parts = length // LANES
    pieces = 2
    return call(
        functools.partial(boxcars_kernel, scale),
        jax.ShapeDtypeStruct((padded, filters, length), jnp.float32),
        [VMEM] * 4,
        (shares, bands, sums, later),
        [
            pltpu.VMEM((padded, length + WMAX), jnp.bfloat16),
            pltpu.VMEM((parts, padded * filters, LANES), jnp.float32),
            pltpu.SemaphoreType.DMA((parts, pieces)),
        ],
        out_specs=HBM,
    )


def per_device(data, delays, offsets, widths):
    beams, chans, length = data.shape
    trials, nsub = offsets.shape
    groups = lax.axis_size("sub")
    outer = 1 << (groups.bit_length() // 2)
    outer = outer if groups % (outer * outer) == 0 else outer // 2
    per_sub = chans // (nsub // groups)
    scale = 1.0 / math.sqrt(chans * groups)
    padded = max(trials, LANES)
    table = jnp.pad(offsets, ((0, padded - trials), (0, 0))) if padded > trials else offsets
    me = [lax.axis_index(axis).astype(jnp.int32).reshape(1) for axis in ("sub", "tm")]
    outs = [
        one_beam(data[beam], delays, table, me, widths, groups, outer, per_sub, scale)[:trials, None]
        for beam in range(beams)
    ]
    return outs[0] if beams == 1 else jnp.concatenate(outs, axis=1)


def solution(mesh):
    placed = (P(None, "sub", "tm"), P("sub"), P("sub", None), P())
    return jax.shard_map(
        per_device,
        mesh=mesh,
        in_specs=placed,
        out_specs=P("sub", None, None, "tm"),
        check_vma=False,
    )
```

```python
import functools
import math

import jax
import jax.numpy as jnp
from jax import lax
from jax.experimental import pallas as pl
from jax.experimental.pallas import tpu as pltpu
from jax.sharding import PartitionSpec as P

WMAX = 128
DCH = 16
OMAX = 96
LANES = 128
STEP = 16
GROUPS = OMAX // STEP
TOGETHER = 1
REACH = OMAX + DCH
VMEM = pl.BlockSpec(memory_space=pltpu.VMEM)
SMEM = pl.BlockSpec(memory_space=pltpu.SMEM)
HBM = pl.BlockSpec(memory_space=pltpu.HBM)
ANY = pl.BlockSpec(memory_space=pl.ANY)


def passed_back(value, axis):
    count = lax.axis_size(axis)
    return lax.ppermute(value, axis, [(source, source - 1) for source in range(1, count)])


def exchanged(value, axis, flip):
    count = lax.axis_size(axis)
    return lax.ppermute(value, axis, [(source, source ^ flip) for source in range(count)])


def series_kernel(
    per_sub, packed, delays_ref, data_ref, series_ref, delays, held, delays_sem, sems
):
    chans, length = data_ref.shape
    block = min(chans, 256)
    subs = block // per_sub
    wide = length + LANES
    first_copy = pltpu.make_async_copy(delays_ref, delays, delays_sem)
    first_copy.start()
    copies = []
    share = chans // sems.shape[0]
    for at in range(sems.shape[0]):
        here = pl.ds(at * share, share)
        copies.append(pltpu.make_async_copy(data_ref.at[here, :], held.at[here, :], sems.at[at]))
        copies[-1].start()
    rows = lax.broadcasted_iota(jnp.int32, (DCH * subs, block), 0)
    owner = lax.broadcasted_iota(jnp.int32, (1, block), 1) // per_sub
    lane = lax.broadcasted_iota(jnp.int32, (subs, length), 1)
    first_copy.wait()
    members = [
        jnp.where(rows == delays[:, at * block : (at + 1) * block] * subs + owner, 1.0, 0.0).astype(jnp.bfloat16)
        for at in range(chans // block)
    ]
    for copy in copies:
        copy.wait()
    parts = []
    for at, member in enumerate(members):
        picked = jnp.dot(member, held[pl.ds(at * block, block), :], preferred_element_type=jnp.float32)
        early, late = None, None
        for delay in range(DCH):
            turned = pltpu.roll(picked[delay * subs : (delay + 1) * subs, :], DCH - delay, 1)
            inside = jnp.where(lane >= DCH - delay, turned, 0.0)
            beyond = jnp.where(lane[:, :LANES] < DCH - delay, turned[:, :LANES], 0.0)
            early = inside if early is None else early + inside
            late = beyond if late is None else late + beyond
        total = jnp.concatenate([early, late], axis=1)
        parts.append(total)
    total = jnp.concatenate(parts, axis=0)
    if packed:
        half = series_ref.shape[0]
        both = jnp.concatenate([total, pltpu.roll(total, wide - half, 1)], axis=0)
        for first in range(0, half, LANES):
            count = min(LANES, half - first)
            tile = both[:, first : first + LANES].T
            series_ref[pl.ds(first, count), :] = tile[:count].astype(jnp.bfloat16)
    else:
        series_ref[...] = total.astype(jnp.bfloat16)


def join_packed_kernel(outer, *refs):
    blocks, joined_ref = refs[:outer], refs[-1]
    half = blocks[0].shape[0]
    rest = joined_ref.shape[0] - half
    lane = lax.broadcasted_iota(jnp.int32, (half, LANES), 1)
    for at in range(outer // 2):
        left = blocks[2 * at][...].astype(jnp.float32)
        right = blocks[2 * at + 1][...].astype(jnp.float32)
        lanes = pl.ds(at * LANES, LANES)
        early = jnp.where(lane < LANES // 2, left, pltpu.roll(right, LANES // 2, 1))
        late = jnp.where(lane < LANES // 2, pltpu.roll(left, LANES // 2, 1), right)
        joined_ref[pl.ds(0, half), lanes] = early.astype(jnp.bfloat16)
        joined_ref[pl.ds(half, rest), lanes] = late[:rest].astype(jnp.bfloat16)


def join_kernel(outer, *refs):
    blocks, joined_ref = refs[:outer], refs[-1]
    subs = blocks[0].shape[0]
    rows = joined_ref.shape[0]
    several = LANES // subs
    for at in range(outer // several):
        for first in range(0, rows, LANES):
            count = min(LANES, rows - first)
            tile = jnp.concatenate(
                [
                    blocks[at * several + slot][:, pl.ds(first, LANES)].astype(jnp.float32)
                    for slot in range(several)
                ],
                axis=0,
            ).T
            joined_ref[pl.ds(first, count), pl.ds(at * LANES, LANES)] = tile[:count].astype(jnp.bfloat16)


def slot_start(slot, flip, outer, inner, subs, me):
    return pl.multiple_of((((me // inner) ^ slot) * inner + ((me % inner) ^ flip)) * subs, subs)


def add_pair(total, pair, both):
    rows, trials = both.shape[0], both.shape[1] // 2
    for odd in range(2):
        first = STEP * (GROUPS - 1 - 2 * pair - odd)
        total[pl.ds(first, rows), :] += both[:, odd * trials : (odd + 1) * trials]


def sums_kernel(given, here, outer, inner, flip, me_ref, tm_ref, joined_ref, table_ref, *refs):
    pairs = GROUPS // 2
    before_ref, sums_ref, *early_ref = refs[: -3 - pairs] if given else (None, *refs[: -3 - pairs])
    moving, shifted, table = refs[-3 - pairs : -pairs]
    totals = refs[-pairs:]
    if before_ref is None:
        sums_ref[...] = jnp.zeros_like(sums_ref)
    else:
        sums_ref[...] = before_ref[...]

    def add_block():
        span, nsub = joined_ref.shape
        subs = nsub // outer
        for slot in range(outer):
            start = slot_start(slot, flip, outer, inner, subs, me_ref[0])
            table[pl.ds(slot * subs, subs), :] = table_ref[pl.ds(start, subs), :]
        blank = jnp.zeros((STEP, nsub), jnp.float32)
        moving[pl.ds(0, STEP), :] = blank
        moving[pl.ds(STEP, span), :] = joined_ref[...].astype(jnp.float32)
        moving[pl.ds(STEP + span, STEP), :] = blank

        def shift(lag):
            shifted[:, pl.ds(lag * nsub, nsub)] = moving[pl.ds(lag, span + STEP), :].astype(jnp.bfloat16)

        def tile(lag, pair):
            halves = [
                jnp.where(table[...] == float(STEP * (2 * pair + odd) + lag), 1.0, 0.0).astype(jnp.bfloat16)
                if lag < STEP or odd
                else jnp.zeros(table.shape, jnp.bfloat16)
                for odd in range(2)
            ]
            return jnp.concatenate(halves, axis=1)

        for lag in range(TOGETHER):
            shift(lag)
        for first in range(0, STEP + 1, TOGETHER):
            lags = range(first, min(first + TOGETHER, STEP + 1))
            for lag in range(first + TOGETHER, min(first + 2 * TOGETHER, STEP + 1)):
                shift(lag)
            for pair in range(pairs - 1 if first == STEP else 0, pairs):
                both = jnp.dot(
                    shifted[:, pl.ds(first * nsub, len(lags) * nsub)],
                    jnp.concatenate([tile(lag, pair) for lag in lags], axis=0),
                    preferred_element_type=jnp.float32,
                )
                if first:
                    totals[pair][...] += both
                else:
                    totals[pair][...] = both
        for pair in range(pairs):
            add_pair(sums_ref, pair, totals[pair][...])

    if here is None:
        add_block()
    else:
        pl.when(here(tm_ref[0]))(add_block)
    for ref in early_ref:
        ref[...] = sums_ref[pl.ds(0, ref.shape[0]), :]


def tables_kernel(widths_ref, offsets_ref, bands_ref, shares_ref, table_ref, widths, offsets, widths_sem, sems):
    first_copy = pltpu.make_async_copy(widths_ref, widths, widths_sem)
    first_copy.start()
    share = offsets_ref.shape[0] // sems.shape[0]
    copies = []
    for at in range(sems.shape[0]):
        here = pl.ds(at * share, share)
        copies.append(pltpu.make_async_copy(offsets_ref.at[here, :], offsets.at[here, :], sems.at[at]))
        copies[-1].start()
    shape = (bands_ref.shape[0], LANES)
    lag = lax.broadcasted_iota(jnp.int32, shape, 0) - lax.broadcasted_iota(jnp.int32, shape, 1)
    first_copy.wait()
    for at in range(widths_ref.shape[0]):
        band = jnp.where((lag >= 0) & (lag < widths[at]), 1.0, 0.0)
        bands_ref[:, pl.ds(at * LANES, LANES)] = band.astype(jnp.bfloat16)
        width = jnp.full((1, LANES), widths[at], jnp.int32).astype(jnp.float32)
        shares_ref[pl.ds(at, 1), :] = 1.0 / jnp.sqrt(width)
    for copy in copies:
        copy.wait()
    for at in range(offsets.shape[1] // LANES):
        here = pl.ds(at * LANES, LANES)
        table_ref[here, :] = offsets[:, here].astype(jnp.float32).T


def boxcars_kernel(scale, shares_ref, bands_ref, sums_ref, later_ref, out_ref, values, mixed, sems):
    trials = sums_ref.shape[1]
    length = sums_ref.shape[0] - REACH
    filters = shares_ref.shape[0]
    whole = length - REACH
    total = jnp.concatenate(
        [
            sums_ref[pl.ds(REACH, whole), :],
            sums_ref[pl.ds(length, REACH), :] + later_ref[pl.ds(0, REACH), :],
            later_ref[pl.ds(REACH, WMAX), :],
        ],
        axis=0,
    )
    for first in range(0, length + WMAX, LANES):
        tile = (total[first : first + LANES] * scale).T
        values[:, pl.ds(first, LANES)] = tile.astype(jnp.bfloat16)
    parts, pieces = sems.shape
    share = trials // pieces
    shares = [shares_ref[pl.ds(at, 1), :] for at in range(filters)]
    tiles = mixed.reshape(parts, trials, filters, LANES)
    copies = []
    for piece in range(pieces):
        some = pl.ds(piece * share, share)
        windows = [values[some, pl.ds(part * LANES, LANES + WMAX)] for part in range(parts)]
        sums = jnp.dot(jnp.concatenate(windows, axis=0), bands_ref[...], preferred_element_type=jnp.float32)
        for part in range(parts):
            for at in range(filters):
                mixed[part, pl.ds(piece * share * filters + at, share, stride=filters), :] = (
                    sums[part * share : (part + 1) * share, at * LANES : (at + 1) * LANES] * shares[at]
                )
            target = out_ref.at[some, :, pl.ds(part * LANES, LANES)]
            copies.append(pltpu.make_async_copy(tiles.at[part, some], target, sems.at[part, piece]))
            copies[-1].start()
    for copy in copies:
        copy.wait()


def call(kernel, out_shape, in_specs, args, scratch=(), flops=0, **options):
    several = isinstance(out_shape, list)
    options.setdefault("out_specs", [VMEM] * len(out_shape) if several else VMEM)
    return pl.pallas_call(
        kernel,
        out_shape=out_shape,
        in_specs=in_specs,
        scratch_shapes=list(scratch),
        compiler_params=pltpu.CompilerParams(vmem_limit_bytes=16 << 20),
        cost_estimate=pl.CostEstimate(flops=flops, bytes_accessed=1 << 20, transcendentals=0),
        **options,
    )(*args)


def one_beam(own, delays, offsets, me, widths, groups, outer, per_sub, scale):
    chans, length = own.shape
    padded, all_subs = offsets.shape
    sub_dev = chans // per_sub
    inner = groups // outer
    filters = widths.shape[0]
    span = length + DCH
    packed = 2 * sub_dev == LANES
    series_shape = (-(-span // 32) * 16, LANES) if packed else (sub_dev, length + LANES)
    steps = 4
    series = call(
        functools.partial(series_kernel, per_sub, packed),
        jax.ShapeDtypeStruct(series_shape, jnp.bfloat16),
        [HBM, HBM],
        tuple(pltpu.with_memory_space_constraint(x, pltpu.HBM) for x in (delays[None, :], own)),
        [
            pltpu.VMEM((1, chans), jnp.int32),
            pltpu.VMEM((chans, length), jnp.bfloat16),
            pltpu.SemaphoreType.DMA,
            pltpu.SemaphoreType.DMA((steps,)),
        ],
    )
    line = [series] + [exchanged(series, "sub", flip * inner) for flip in range(1, outer)]
    nsub = outer * sub_dev
    bands, shares, table = call(
        tables_kernel,
        [
            jax.ShapeDtypeStruct((LANES + WMAX, filters * LANES), jnp.bfloat16),
            jax.ShapeDtypeStruct((filters, LANES), jnp.float32),
            jax.ShapeDtypeStruct((all_subs, padded), jnp.float32),
        ],
        [HBM, HBM],
        tuple(pltpu.with_memory_space_constraint(x, pltpu.HBM) for x in (widths, offsets)),
        [
            pltpu.SMEM((filters,), jnp.int32),
            pltpu.VMEM((padded, all_subs), jnp.int32),
            pltpu.SemaphoreType.DMA,
            pltpu.SemaphoreType.DMA((steps,)),
        ],
    )
    joined = call(
        functools.partial(join_packed_kernel if packed else join_kernel, outer),
        jax.ShapeDtypeStruct((span, nsub), jnp.bfloat16),
        [VMEM] * outer + [ANY] * 2,
        (*line, table, bands),
    )
    blocks = [joined] + [exchanged(joined, "sub", flip) for flip in range(1, inner)]
    scratch = [
        pltpu.VMEM((span + 2 * STEP, nsub), jnp.float32),
        pltpu.VMEM((span + STEP, (STEP + 1) * nsub), jnp.bfloat16),
        pltpu.VMEM((nsub, padded), jnp.float32),
        *[pltpu.VMEM((span + STEP, 2 * padded), jnp.float32)] * (GROUPS // 2),
    ]
    flops = 2 * (span + STEP) * nsub * padded * (OMAX + 2)
    sums_shape = jax.ShapeDtypeStruct((length + REACH, padded), jnp.float32)
    early_shape = jax.ShapeDtypeStruct((REACH + WMAX, padded), jnp.float32)
    steps = [(flip, None) for flip in range(inner - 1)]
    steps += [(inner - 1, lambda tm: tm > 0), (inner - 1, lambda tm: tm == 0)]
    given = ()
    for at, (flip, here) in enumerate(steps):
        sums, *rest = call(
            functools.partial(sums_kernel, at > 0, here, outer, inner, flip),
            [sums_shape, early_shape] if at == inner - 1 else [sums_shape],
            [SMEM] * 2 + [VMEM] * (2 + len(given)),
            (*me, blocks[flip], table, *given),
            scratch,
            flops,
        )
        given = (sums,)
        if rest:
            later = passed_back(rest[0], "tm")
    parts = length // LANES
    pieces = 2
    return call(
        functools.partial(boxcars_kernel, scale),
        jax.ShapeDtypeStruct((padded, filters, length), jnp.float32),
        [VMEM] * 4,
        (shares, bands, sums, later),
        [
            pltpu.VMEM((padded, length + WMAX), jnp.bfloat16),
            pltpu.VMEM((parts, padded * filters, LANES), jnp.float32),
            pltpu.SemaphoreType.DMA((parts, pieces)),
        ],
        out_specs=HBM,
    )


def per_device(data, delays, offsets, widths):
    beams, chans, length = data.shape
    trials, nsub = offsets.shape
    groups = lax.axis_size("sub")
    outer = 1 << (groups.bit_length() // 2)
    outer = outer if groups % (outer * outer) == 0 else outer // 2
    per_sub = chans // (nsub // groups)
    scale = 1.0 / math.sqrt(chans * groups)
    padded = max(trials, LANES)
    table = jnp.pad(offsets, ((0, padded - trials), (0, 0))) if padded > trials else offsets
    me = [lax.axis_index(axis).astype(jnp.int32).reshape(1) for axis in ("sub", "tm")]
    outs = [
        one_beam(data[beam], delays, table, me, widths, groups, outer, per_sub, scale)[:trials, None]
        for beam in range(beams)
    ]
    return outs[0] if beams == 1 else jnp.concatenate(outs, axis=1)


def solution(mesh):
    placed = (P(None, "sub", "tm"), P("sub"), P("sub", None), P())
    return jax.shard_map(
        per_device,
        mesh=mesh,
        in_specs=placed,
        out_specs=P("sub", None, None, "tm"),
        check_vma=False,
    )
```
